32 devices in a mesh: dp: 8 (over y, x, core), fsdp: 4 (over z).
Axes of the slice: x: 2, y: 2, z: 4, core: 2. Of those that a mesh axis runs over, the one named last changes fastest.
Arguments:
- fields: bfloat16 [8, 6, 48, 48, 48, 128], P('dp', None, 'fsdp'), may hold values from -6 to 6
- targets: bfloat16 [8, 6, 48, 2304], P('dp', None, 'fsdp'), may hold values from -6 to 6
- lists: int32 [8, 6], P('dp'), may hold values from 0 to 5, each once within a row
- counts: int32 [8], replicated, may hold values from 1 to 6, as said below
- spectral_w: bfloat16 [32, 2, 128, 128], P('fsdp'), may hold values from -0.375 to 0.375
- local_w: bfloat16 [128, 128], replicated, may hold values from -0.5 to 0.5
- proj: float32 [128], replicated, may hold values from -0.5 to 0.5
Outputs:
- grad_spectral: float32 [32, 2, 128, 128], P('fsdp')
- grad_local: float32 [128, 128], replicated
The draws below stay inside these ranges and needn't reach their ends.
Inputs may be any that keep to these rules, and one draw needn't show every extreme that they name: Each row of lists names every slot of its lane once; the first counts[l] entries of row l are lane l's live grids. `counts`: exactly one lane has 6 live grids; every other lane has 1 or 2.
All inputs are finite; a program needn't handle non-finite values.
Results may differ from the reference program's by a relative error of at most 0.0036.
The reference program's roundings to bfloat16 on the way count: a program that leaves them out, or rounds other values in their place, can miss the bound.
Values may be sent and summed in bfloat16 or wider, within the bound.
No kernel may reach another device: no remote copies, remote signals or barrier semaphores. Data moves between devices by JAX's collectives and lax.ppermute only.
A program may use at most 128 MiB of HBM per device.

```python
import math
import jax
import jax.numpy as jnp
from jax import lax

C = 128
G = 48
MX = 4
MY = 4
MZ = 2
MODES = 32
SLOTS = 6
N_DP = 8


def draw_counts(key, part):
    base_counts = jax.random.randint(jax.random.fold_in(key, 11), (N_DP,), 1, 3, dtype=jnp.int32)
    busiest = jax.random.randint(jax.random.fold_in(key, 12), (), 0, N_DP, dtype=jnp.int32)
    return jnp.where(jnp.arange(N_DP, dtype=jnp.int32) == busiest, SLOTS, base_counts).astype(jnp.int32)


def steps_of(stream_key, shape, pieces, smallest, high):
    loudness = 1.0
    for dim, parts in pieces:
        steps = jax.random.uniform(jax.random.fold_in(jax.random.fold_in(stream_key, 6), dim), (parts,), jnp.float32, smallest / len(pieces), high / len(pieces))
        loudness = loudness * jnp.repeat(jnp.exp(steps), shape[dim] // parts).reshape((-1,) + (1,) * (len(shape) - 1 - dim))
    return loudness


def scatter_about(rng, shape, scale, reach, cuts=(), kind=jnp.bfloat16):
    values = scale * jax.random.normal(rng, shape, jnp.float32)
    if cuts:
        values = values * steps_of(rng, shape, cuts, -0.22, 0.18)
    return jnp.clip(values, -reach, reach).astype(kind)


def setup_inputs(seed: int = 0) -> dict:
    seeds = jax.random.split(jax.random.key(seed), 8)
    fields = scatter_about(seeds[0], (N_DP, SLOTS, G, G, G, C), 1.0, 6.0, ((0, 8), (2, 4)))
    targets = scatter_about(seeds[1], (N_DP, SLOTS, G, G * G), 1.0, 6.0, ((0, 8), (2, 4)))
    lists = jax.vmap(lambda own: jax.random.permutation(own, SLOTS))(jax.random.split(seeds[2], N_DP)).reshape((N_DP, SLOTS)).astype(jnp.int32)
    counts = draw_counts(jax.random.fold_in(seeds[7], 71), 0)
    spectral_w = scatter_about(seeds[4], (MODES, 2, C, C), (2 * C) ** -0.5, 0.375, ((0, 4),))
    local_w = scatter_about(seeds[5], (C, C), C ** -0.5, 0.5)
    proj = scatter_about(seeds[6], (C,), C ** -0.5, 0.5, (), jnp.float32)
    return dict(fields=fields, targets=targets, lists=lists, counts=counts, spectral_w=spectral_w, local_w=local_w, proj=proj)


highest = lax.Precision.HIGHEST
root_half = 0.7071067811865476
inv_root_two_pi = 0.3989422804014327

def phase_table(mode_ids, cell_ids, length, direction):
    product = mode_ids[:, None] * cell_ids[None, :] % length
    angle = product.astype(jnp.float32) * (2.0 * math.pi / length)
    return (jnp.cos(angle), direction * jnp.sin(angle))

def mode_lists():
    kx_ids = jnp.arange(MX, dtype=jnp.int32) - MX // 2
    ky_ids = jnp.arange(MY, dtype=jnp.int32) - MY // 2
    kz_ids = jnp.arange(MZ, dtype=jnp.int32)
    return (kx_ids, ky_ids, kz_ids)

def complex_contract(real_part, imag_part, cos_t, sin_t, form):

    def product(left, right):
        return jnp.einsum(form, left, right, precision=highest)
    return (product(real_part, cos_t) - product(imag_part, sin_t), product(real_part, sin_t) + product(imag_part, cos_t))

def forward_modes(grid_field, x_cells, scale):
    grid_len = grid_field.shape[1]
    kx_ids, ky_ids, kz_ids = mode_lists()
    cells = jnp.arange(grid_len, dtype=jnp.int32)
    cos_z, sin_z = phase_table(kz_ids, cells, grid_len, -1.0)
    cos_zb = lax.optimization_barrier(cos_z.astype(jnp.bfloat16)).astype(jnp.float32)
    sin_zb = lax.optimization_barrier(sin_z.astype(jnp.bfloat16)).astype(jnp.float32)
    field_wide = grid_field.astype(jnp.float32)
    part_re = jnp.einsum('abzc,kz->abkc', field_wide, cos_zb, precision=highest)
    part_im = jnp.einsum('abzc,kz->abkc', field_wide, sin_zb, precision=highest)
    cos_y, sin_y = phase_table(ky_ids, cells, grid_len, -1.0)
    next_re, next_im = complex_contract(part_re, part_im, cos_y, sin_y, 'abkc,jb->ajkc')
    cos_x, sin_x = phase_table(kx_ids, x_cells, grid_len, -1.0)
    last_re, last_im = complex_contract(next_re, next_im, cos_x, sin_x, 'ajkc,ia->ijkc')
    stacked = jnp.stack([last_re, last_im], axis=3) * scale
    return stacked.reshape(MX * MY * MZ, 2, stacked.shape[-1])

def inverse_modes(spectrum, x_cells, grid_len):
    kx_ids, ky_ids, kz_ids = mode_lists()
    cells = jnp.arange(grid_len, dtype=jnp.int32)
    values = spectrum.astype(jnp.float32).reshape(MX, MY, MZ, 2, spectrum.shape[-1])
    cos_x, sin_x = phase_table(kx_ids, x_cells, grid_len, 1.0)
    first_re, first_im = complex_contract(values[:, :, :, 0], values[:, :, :, 1], cos_x, sin_x, 'ijkc,ia->ajkc')
    cos_y, sin_y = phase_table(ky_ids, cells, grid_len, 1.0)
    second_re, second_im = complex_contract(first_re, first_im, cos_y, sin_y, 'ajkc,jb->abkc')
    cos_z, sin_z = phase_table(kz_ids, cells, grid_len, 1.0)
    real_out = jnp.einsum('abkc,kz->abzc', second_re, cos_z, precision=highest)
    real_out = real_out - jnp.einsum('abkc,kz->abzc', second_im, sin_z, precision=highest)
    return real_out * float(MX * MY * MZ) ** (-0.5)

def mix_modes(coeff_b, weights):
    coeff_f = coeff_b.astype(jnp.float32)
    weight_f = weights.astype(jnp.float32)
    signs = jnp.array([1.0, -1.0], jnp.float32).reshape(1, 2, 1, 1)
    spec_re = jnp.einsum('gmri,mrio->gmo', coeff_f, weight_f * signs, precision=highest)
    spec_im = jnp.einsum('gmri,mrio->gmo', coeff_f[:, :, ::-1], weight_f, precision=highest)
    return jnp.stack([spec_re, spec_im], axis=2)

def weight_grad(coeff_b, back_stack):
    coeff_f = coeff_b.astype(jnp.float32)
    rotated = jnp.stack([-coeff_f[:, :, 1], coeff_f[:, :, 0]], axis=2)
    grad_re = jnp.einsum('gmri,gmro->mio', coeff_f, back_stack, precision=highest)
    grad_im = jnp.einsum('gmri,gmro->mio', rotated, back_stack, precision=highest)
    return jnp.stack([grad_re, grad_im], axis=1)

def point_part(grid_field, branch, local_w, proj, grid_target, scale):
    width = grid_field.shape[-1]
    flat_field = grid_field.reshape(-1, width)
    pre = branch.reshape(-1, width) + jnp.dot(flat_field, local_w, preferred_element_type=jnp.float32)
    erf_part = lax.erf(pre * root_half)
    active = 0.5 * pre * (1.0 + erf_part)
    pred = jnp.dot(active, proj, precision=highest)
    resid = (pred - grid_target.reshape(-1).astype(jnp.float32)) * scale
    slope = 0.5 * (1.0 + erf_part) + pre * jnp.exp(-0.5 * pre * pre) * inv_root_two_pi
    d_pre = (resid[:, None] * proj[None, :] * slope).astype(jnp.bfloat16)
    local_grad = jnp.dot(flat_field.T, d_pre, preferred_element_type=jnp.float32)
    return (d_pre.reshape(grid_field.shape), local_grad)

def reference(fields, targets, lists, counts, spectral_w, local_w, proj):
    slot_ids = jnp.arange(SLOTS, dtype=jnp.int32)
    lane_ids = jnp.arange(N_DP, dtype=jnp.int32)
    keyed = jnp.where(slot_ids[None, :] < counts[:, None], lane_ids[:, None] * SLOTS + lists, N_DP * SLOTS)
    ordered = jnp.sort(keyed.reshape(-1)).astype(jnp.int32)
    grid_total = jnp.sum(counts).astype(jnp.int32)
    scale = 1.0 / grid_total.astype(jnp.float32)
    all_fields = fields.reshape(N_DP * SLOTS, G, G, G, C)
    all_targets = targets.reshape(N_DP * SLOTS, G, G * G)
    x_cells = jnp.arange(G, dtype=jnp.int32)
    mode_scale = float(MODES) ** (-0.5)

    def visit(position, carry):
        grad_spectral, grad_local = carry
        which = ordered[position].astype(jnp.int32)
        grid_field = lax.dynamic_index_in_dim(all_fields, which, 0, keepdims=False)
        grid_target = lax.dynamic_index_in_dim(all_targets, which, 0, keepdims=False)
        coeff_b = forward_modes(grid_field, x_cells, float(G) ** (-1.5)).astype(jnp.bfloat16)
        spectrum = mix_modes(coeff_b[None], spectral_w)[0].astype(jnp.bfloat16)
        branch = inverse_modes(spectrum, x_cells, G)
        d_pre, local_grad = point_part(grid_field, branch, local_w, proj, grid_target, scale)
        grid_back = forward_modes(d_pre, x_cells, mode_scale)
        return (grad_spectral + weight_grad(coeff_b[None], grid_back[None]), grad_local + local_grad)
    start = (jnp.zeros((MODES, 2, C, C), jnp.float32), jnp.zeros((C, C), jnp.float32))
    grad_spectral, grad_local = lax.fori_loop(0, grid_total, visit, start)
    return (grad_spectral, grad_local)
```

```python
import functools
import math

import jax
import jax.numpy as jnp
import ml_dtypes
import numpy as np
from jax import lax
from jax.experimental import pallas as pl
from jax.experimental.pallas import tpu as pltpu
from jax.sharding import PartitionSpec as P

MX = 4
MY = 4
MZ = 2
MODES = MX * MY * MZ
VMEM_BYTES = 40 * 1024 * 1024
f32 = jnp.float32
bf16 = jnp.bfloat16
inv_root_two_pi = 0.3989422804014327
half_log2e = 0.7213475204444817
erf_p = 0.3275911 * 0.7071067811865476
erf_a = tuple(0.5 * a for a in (0.254829592, -0.284496736, 1.421413741, -1.453152027, 1.061405429))


def split_bf16(values):
    high = values.astype(ml_dtypes.bfloat16)
    low = (values - high.astype(np.float64)).astype(ml_dtypes.bfloat16)
    return high, low


def angles(mode_ids, length):
    product = np.outer(mode_ids, np.arange(length)) % length
    return product * (2.0 * math.pi / length)


def phase_constants(length):
    y_angle = angles(np.arange(MY) - MY // 2, length)
    z_angle = angles(np.arange(MZ), length)
    rounded = lambda v: v.astype(np.float32).astype(ml_dtypes.bfloat16).astype(np.float64)
    cz, sz = rounded(np.cos(z_angle)), rounded(-np.sin(z_angle))
    cy, sy = np.cos(y_angle), -np.sin(y_angle)
    both = lambda a, b: (a[:, None, :, None] * b[None, :, None, :]).reshape(MY * MZ, length * length)
    fwd = np.concatenate([both(cy, cz) - both(sy, sz), both(sy, cz) + both(cy, sz)], axis=0)
    fwd = np.concatenate(split_bf16(fwd), axis=0)
    cz, sz = np.cos(z_angle), np.sin(z_angle)
    cy, sy = np.cos(y_angle), np.sin(y_angle)
    inv = np.concatenate([both(cy, cz) - both(sy, sz), -(both(sy, cz) + both(cy, sz))], axis=0).T
    high, low = split_bf16(inv)
    pad = np.zeros((length * length, 128 - 4 * high.shape[1]), ml_dtypes.bfloat16)
    inv = np.concatenate([high, low, high, low, pad], axis=1)
    x_angle = angles(np.arange(MX) - MX // 2, length).T
    xtab = np.stack([np.cos(x_angle), np.sin(x_angle)], axis=2).astype(np.float32)
    return fwd, inv, xtab.reshape(-1)


def scalar_places(slots):
    return dict(count=slots, total=slots + 1, shard=slots + 2, first=slots + 3)


def combine_planes(q_ref, xtab_ref, cell0, shard, planes, scale, store):
    for d in range(MX):
        i = lax.rem(shard + d, MX)
        re = jnp.zeros((8, 128), f32)
        im = jnp.zeros((8, 128), f32)
        for a in range(planes):
            at = ((cell0 + a) * MX + i) * 2
            c = xtab_ref[at]
            s = xtab_ref[at + 1]
            q_re = q_ref[a, 0:8, :]
            q_im = q_ref[a, 8:16, :]
            re = re + (q_re * c + q_im * s)
            im = im + (q_im * c - q_re * s)
        store(d, re * scale, im * scale)


def forward_kernel(
    slots, planes, step_planes, scale, meta_ref, xtab_ref, f_ref, basis_ref, *rest
):
    outs, q_ref = rest[:MX], rest[MX]
    place = scalar_places(slots)
    g, blk = pl.program_id(0), pl.program_id(1)
    live = g < meta_ref[place["count"]]
    row = pl.multiple_of(g * 16, 16)

    @pl.when(live)
    def _():
        cells = f_ref.shape[3] * f_ref.shape[4]
        for p in range(step_planes):
            field = f_ref[0, 0, p].reshape(cells, 128)
            part = jnp.dot(basis_ref[...], field, preferred_element_type=f32)
            q_ref[blk * step_planes + p] = part[0:16] + part[16:32]

        @pl.when(blk == planes // step_planes - 1)
        def _():
            def store(d, re, im):
                outs[d][pl.ds(row, 8), :] = re
                outs[d][pl.ds(row + 8, 8), :] = im

            combine_planes(
                q_ref, xtab_ref, meta_ref[place["first"]], meta_ref[place["shard"]], planes, scale, store
            )

    @pl.when(jnp.logical_not(live) & (blk == 0))
    def _():
        for out in outs:
            out[pl.ds(row, 16), :] = jnp.zeros((16, 128), f32)


def gelu_parts(pre):
    bell = jnp.exp2(pre * pre * (-half_log2e))
    t = pl.reciprocal(1.0 + erf_p * jnp.abs(pre), approx=True)
    poly = erf_a[4]
    for a in (erf_a[3], erf_a[2], erf_a[1], erf_a[0]):
        poly = poly * t + a
    tail = poly * t * bell
    cdf = jnp.where(pre >= 0.0, 1.0 - tail, tail)
    return cdf, bell


def backward_kernel(
    slots, planes, step_planes, rows_step, scale, meta_ref, xtab_ref, f_ref, t_ref, *rest
):
    specs = rest[:MX]
    w_ref, proj_ref, inv_ref, basis_ref, eye_ref, ones_ref = rest[MX : MX + 6]
    outs = rest[MX + 6 : 2 * MX + 6]
    rhs_ref, d_ref, total_ref, q_ref, t16_ref, spec_ref = rest[2 * MX + 6 :]
    place = scalar_places(slots)
    g, blk = pl.program_id(0), pl.program_id(1)
    blocks = planes // step_planes
    live = g < meta_ref[place["count"]]
    row = pl.multiple_of(g * 16, 16)
    shard = meta_ref[place["shard"]]
    cell0 = meta_ref[place["first"]]
    cells = f_ref.shape[3] * f_ref.shape[4]
    third = cells // 3
    steps = third // rows_step
    subs = rows_step // 128

    @pl.when((g == 0) & (blk == 0))
    def _():
        total_ref[...] = jnp.zeros_like(total_ref)
        rhs_ref[0:128, :] = w_ref[...]
        rhs_ref[128:256, :] = jnp.zeros((128, 128), bf16)

    @pl.when(live)
    def _():
        @pl.when(blk == 0)
        def _():
            lines = t_ref[0, 0].astype(f32)
            for a in range(planes):
                line = jnp.broadcast_to(lines[a : a + 1, :], (16, cells))
                t16_ref[a] = line.astype(bf16)
            for d in range(MX):
                spec_ref[d] = specs[d][pl.ds(row, 16), :].astype(f32)

        count = meta_ref[place["total"]].astype(f32)
        proj = proj_ref[...]
        proj_scaled = proj / jnp.full((1, 128), count, f32)

        def plane(p, carry):
            a = blk * step_planes + p
            re = jnp.zeros((8, 128), f32)
            im = jnp.zeros((8, 128), f32)
            for d in range(MX):
                i = lax.rem(shard - d + MX, MX)
                at = ((cell0 + a) * MX + i) * 2
                c = xtab_ref[at]
                s = xtab_ref[at + 1]
                s_re = spec_ref[d, 0:8, :]
                s_im = spec_ref[d, 8:16, :]
                re = re + (s_re * c - s_im * s)
                im = im + (s_re * s + s_im * c)
            first = jnp.concatenate([re, im], axis=0) * scale
            high = first.astype(bf16)
            low = (first - high.astype(f32)).astype(bf16)
            rhs_ref[128:144, :] = high
            rhs_ref[144:160, :] = high
            rhs_ref[160:176, :] = low
            rhs_ref[176:192, :] = low
            field = f_ref[0, 0, p].reshape(cells, 128)

            def stage_one(r0):
                part = slice(r0, r0 + rows_step)
                lhs = jnp.concatenate([field[part], inv_ref[part, :]], axis=1)
                pre = jnp.dot(lhs, rhs_ref[...], preferred_element_type=f32)
                cdf, bell = gelu_parts(pre)
                slope = (cdf + pre * bell * inv_root_two_pi) * proj_scaled
                active = (pre * cdf * proj).astype(bf16)
                wanted = []
                for j in range(subs):
                    at = r0 + j * 128
                    line = t16_ref[a, :, at : at + 128]
                    wanted.extend(line * eye_ref[n : n + 16, :] for n in range(0, 128, 16))
                wanted = jnp.concatenate(wanted, axis=0)
                return jnp.concatenate([active, wanted], axis=1), slope

            def stage_two(r0, both, slope):
                resid = jnp.dot(both, ones_ref[...], preferred_element_type=f32)
                d_ref[r0 : r0 + rows_step, :] = (resid * slope).astype(bf16)

            q = jnp.zeros((32, 128), f32)
            for k in range(3):
                waiting = None
                for s in range(steps):
                    r0 = k * third + s * rows_step
                    made = stage_one(r0)
                    if waiting is not None:
                        stage_two(*waiting)
                    waiting = (r0,) + made
                stage_two(*waiting)
                part = slice(k * third, (k + 1) * third)
                lhs = jnp.concatenate([field[part].T, basis_ref[:, part]], axis=0)
                sums = jnp.dot(lhs, d_ref[part, :], preferred_element_type=f32)
                total_ref[...] += sums[0:128]
                q = q + sums[128:160]
            q_ref[a] = q[0:16] + q[16:32]
            return carry

        lax.fori_loop(0, step_planes, plane, 0)

        @pl.when(blk == blocks - 1)
        def _():
            def store(d, re, im):
                outs[d][pl.ds(row, 8), :] = re
                outs[d][pl.ds(row + 8, 8), :] = im

            combine_planes(q_ref, xtab_ref, cell0, shard, planes, scale, store)

    @pl.when(jnp.logical_not(live) & (blk == 0))
    def _():
        for out in outs:
            out[pl.ds(row, 16), :] = jnp.zeros((16, 128), f32)

    @pl.when((g == slots - 1) & (blk == blocks - 1))
    def _():
        part = 128 // MX
        for d in range(MX):
            i = lax.rem(shard + d, MX)
            at = pl.multiple_of(i * part, part)
            outs[d][slots * 16 : slots * 16 + part, :] = total_ref[pl.ds(at, part), :]


def mix_kernel(slots, per, shards, *refs):
    parts = refs[:shards]
    w_ref, coeff_out, spec_out, c_ref, s_ref = refs[shards:]
    total = parts[0][...]
    for part in parts[1:]:
        total = total + part[...]
    coeff = total.astype(bf16)
    coeff_out[...] = coeff
    c_ref[...] = coeff.astype(f32)
    for m in range(per):
        re_rows = pl.ds(m, slots, stride=2 * per)
        im_rows = pl.ds(per + m, slots, stride=2 * per)
        re = c_ref[re_rows, :].astype(bf16)
        im = c_ref[im_rows, :].astype(bf16)
        weight = w_ref[m].reshape(256, 128)
        s_ref[re_rows, :] = jnp.dot(
            jnp.concatenate([re, -im], axis=1), weight, preferred_element_type=f32
        )
        s_ref[im_rows, :] = jnp.dot(
            jnp.concatenate([im, re], axis=1), weight, preferred_element_type=f32
        )
    spec_out[...] = s_ref[...].astype(bf16)


def sum_kernel(count, *refs):
    total = refs[0][...]
    for part in refs[1:count]:
        total = total + part[...]
    refs[count][...] = total


def local_sum_kernel(count, rows, *refs):
    size = refs[count].shape[0]
    total = refs[0][rows : rows + size, :]
    for part in refs[1:count]:
        total = total + part[rows : rows + size, :]
    refs[count][...] = total


def weight_kernel(lanes, slots, per, *refs):
    coeffs, backs = refs[:lanes], refs[lanes : 2 * lanes]
    out_ref, c_ref, b_ref = refs[2 * lanes :]
    rows = slots * 2 * per
    for n in range(lanes):
        c_ref[n * rows : (n + 1) * rows, :] = coeffs[n][...].astype(f32)
        b_ref[n * rows : (n + 1) * rows, :] = backs[n][0:rows, :]
    for m in range(per):
        re_rows = pl.ds(m, lanes * slots, stride=2 * per)
        im_rows = pl.ds(per + m, lanes * slots, stride=2 * per)
        c_re = c_ref[re_rows, :].astype(bf16)
        c_im = c_ref[im_rows, :].astype(bf16)
        b_re = b_ref[re_rows, :]
        b_im = b_ref[im_rows, :]
        left = jnp.concatenate([c_re, c_im], axis=0)
        right = jnp.concatenate(
            [jnp.concatenate([b_re, b_im], axis=1), jnp.concatenate([b_im, -b_re], axis=1)], axis=0
        )
        high = right.astype(bf16)
        low = (right - high.astype(f32)).astype(bf16)
        left = jnp.concatenate([left, left], axis=0)
        right = jnp.concatenate([high, low], axis=0)
        grad = lax.dot_general(
            left, right, (((0,), (0,)), ((), ())), preferred_element_type=f32
        )
        out_ref[m, 0] = grad[:, 0:128]
        out_ref[m, 1] = grad[:, 128:256]


def place_kernel(shards, meta_ref, *refs):
    out_ref = refs[shards]
    size = refs[0].shape[0]
    for d in range(shards):
        i = lax.rem(meta_ref[0] - d + shards, shards)
        out_ref[pl.ds(pl.multiple_of(i * size, size), size), :] = refs[d][...]


def whole_vmem(count):
    return [pl.BlockSpec(memory_space=pltpu.VMEM)] * count


def params():
    return pltpu.CompilerParams(vmem_limit_bytes=VMEM_BYTES)


def rotations(value_of, axis, size):
    got = [value_of(0)]
    for d in range(1, size):
        perm = [(s, (s + d) % size) for s in range(size)]
        got.append(lax.ppermute(value_of(d), axis, perm))
    return got


def body(lanes, shards, fields, targets, lists, counts, spectral_w, local_w, proj):
    _, slots, planes, grid_len, _, width = fields.shape
    per = MODES // shards
    split = shards // MX
    cells = grid_len * grid_len
    step_planes = max(n for n in (1, 2, 3, 4) if planes % n == 0)
    blocks = planes // step_planes
    basis, inverse, xtab = phase_constants(grid_len)
    lane = lax.axis_index("dp")
    shard = lax.axis_index("fsdp").astype(jnp.int32)
    turn = shard if split == 1 else jnp.int32(0)
    meta = jnp.concatenate(
        [
            lists[0],
            counts[lane][None],
            jnp.sum(counts)[None],
            turn[None],
            (shard * planes)[None],
        ]
    ).astype(jnp.int32)
    place = scalar_places(slots)

    def field_block(g, blk, meta_ref, xtab_ref):
        count = meta_ref[place["count"]]
        slot = meta_ref[jnp.minimum(g, count - 1)]
        return (0, slot, jnp.where(g < count, blk, blocks - 1), 0, 0, 0)

    def target_block(g, blk, meta_ref, xtab_ref):
        count = meta_ref[place["count"]]
        return (0, meta_ref[jnp.minimum(g, count - 1)], 0, 0)

    def fixed(*shape):
        return pl.BlockSpec(shape, lambda g, blk, meta_ref, xtab_ref: (0,) * len(shape))

    field_spec = pl.BlockSpec((1, 1, step_planes, grid_len, grid_len, width), field_block)
    part_rows = slots * 16
    parts = pl.pallas_call(
        functools.partial(forward_kernel, slots, planes, step_planes, float(grid_len) ** (-1.5)),
        grid_spec=pltpu.PrefetchScalarGridSpec(
            num_scalar_prefetch=2,
            grid=(slots, blocks),
            in_specs=[field_spec, fixed(*basis.shape)],
            out_specs=[fixed(part_rows, width)] * MX,
            scratch_shapes=[pltpu.VMEM((planes, 16, width), f32)],
        ),
        out_shape=[jax.ShapeDtypeStruct((part_rows, width), f32)] * MX,
        compiler_params=params(),
        name="forward_modes",
    )(meta, xtab, fields, basis)

    def shard_parts(pieces, count):
        if split == 1:
            return lambda d: pieces[d]
        stacked = jnp.stack(pieces).reshape(MX, count, 2, split, per, width)
        stacked = jnp.moveaxis(stacked, 3, 1).reshape(shards, count * 2 * per, width)
        return lambda d: lax.dynamic_index_in_dim(stacked, (shard + d) % shards, 0, keepdims=False)

    def mode_parts(pieces, count):
        if split == 1:
            return pieces
        stacked = jnp.stack(pieces)[(shard - jnp.arange(shards)) % shards]
        stacked = stacked.reshape(MX, split, count, 2, per, width)
        stacked = jnp.moveaxis(stacked, 1, 3).reshape(MX, count * 16, width)
        return [stacked[(-d) % MX] for d in range(MX)]

    came = rotations(shard_parts(parts, slots), "fsdp", shards)
    own_rows = slots * 2 * per
    coeff, own_spectrum = pl.pallas_call(
        functools.partial(mix_kernel, slots, per, shards),
        in_specs=whole_vmem(shards + 1),
        out_specs=whole_vmem(2),
        out_shape=[jax.ShapeDtypeStruct((own_rows, width), bf16)] * 2,
        scratch_shapes=[pltpu.VMEM((own_rows, width), f32)] * 2,
        compiler_params=params(),
        name="mix_modes",
    )(*came, spectral_w)
    spectrum = mode_parts(rotations(lambda d: own_spectrum, "fsdp", shards), slots)
    coeffs = rotations(lambda d: coeff, "dp", lanes)

    local_rows = width // MX
    eye = np.eye(128, dtype=ml_dtypes.bfloat16)
    ones = np.ones((128, 128), ml_dtypes.bfloat16)
    ones = np.concatenate([ones, -ones], axis=0)
    results = pl.pallas_call(
        functools.partial(backward_kernel, slots, planes, step_planes, 256, float(MODES) ** (-0.5)),
        grid_spec=pltpu.PrefetchScalarGridSpec(
            num_scalar_prefetch=2,
            grid=(slots, blocks),
            in_specs=[field_spec, pl.BlockSpec((1, 1, planes, cells), target_block)]
            + [fixed(part_rows, width)] * MX
            + [
                fixed(width, width),
                fixed(1, width),
                fixed(*inverse.shape),
                fixed(*basis.shape),
                fixed(*eye.shape),
                fixed(*ones.shape),
            ],
            out_specs=[fixed(part_rows + local_rows, width)] * MX,
            scratch_shapes=[
                pltpu.VMEM((256, width), bf16),
                pltpu.VMEM((cells, width), bf16),
                pltpu.VMEM((width, width), f32),
                pltpu.VMEM((planes, 16, width), f32),
                pltpu.VMEM((planes, 16, cells), bf16),
                pltpu.VMEM((MX, 16, width), f32),
            ],
        ),
        out_shape=[jax.ShapeDtypeStruct((part_rows + local_rows, width), f32)] * MX,
        compiler_params=params(),
        cost_estimate=pl.CostEstimate(
            flops=4 * slots * planes * cells * 256 * 256,
            bytes_accessed=slots * planes * cells * width * 2,
            transcendentals=0,
        ),
        name="backward_modes",
    )(
        meta, xtab, fields, targets, *spectrum, local_w, proj.reshape(1, width), inverse, basis, eye, ones
    )

    if split == 1:
        chunk = lambda d: results[d]
    else:
        backs = shard_parts([r[:part_rows] for r in results], slots)
        local = jnp.concatenate([r[part_rows:] for r in results], axis=0)
        rows = width // shards
        chunk = lambda d: jnp.concatenate(
            [backs(d), lax.dynamic_slice_in_dim(local, (shard + d) % shards * rows, rows, 0)], axis=0
        )
    came = rotations(chunk, "fsdp", shards)
    own_sum = pl.pallas_call(
        functools.partial(sum_kernel, shards),
        in_specs=whole_vmem(shards),
        out_specs=pl.BlockSpec(memory_space=pltpu.VMEM),
        out_shape=jax.ShapeDtypeStruct(came[0].shape, f32),
        compiler_params=params(),
        name="sum_shards",
    )(*came)
    sums = rotations(lambda d: own_sum, "dp", lanes)
    own_local = pl.pallas_call(
        functools.partial(local_sum_kernel, lanes, own_rows),
        in_specs=whole_vmem(lanes),
        out_specs=pl.BlockSpec(memory_space=pltpu.VMEM),
        out_shape=jax.ShapeDtypeStruct((width // shards, width), f32),
        compiler_params=params(),
        name="sum_local",
    )(*sums)
    locals_ = rotations(lambda d: own_local, "fsdp", shards)
    grad_spectral = pl.pallas_call(
        functools.partial(weight_kernel, lanes, slots, per),
        in_specs=whole_vmem(2 * lanes),
        out_specs=pl.BlockSpec(memory_space=pltpu.VMEM),
        out_shape=jax.ShapeDtypeStruct((per, 2, width, width), f32),
        scratch_shapes=[pltpu.VMEM((lanes * own_rows, width), f32)] * 2,
        compiler_params=params(),
        cost_estimate=pl.CostEstimate(
            flops=2 * per * 192 * 128 * 256, bytes_accessed=2 * per * 2 * width * width * 4, transcendentals=0
        ),
        name="weight_grad",
    )(*coeffs, *sums)
    grad_local = pl.pallas_call(
        functools.partial(place_kernel, shards),
        in_specs=[pl.BlockSpec(memory_space=pltpu.SMEM)] + whole_vmem(shards),
        out_specs=pl.BlockSpec(memory_space=pltpu.VMEM),
        out_shape=jax.ShapeDtypeStruct((width, width), f32),
        compiler_params=params(),
        name="place_local",
    )(shard[None], *locals_)
    return (grad_spectral, grad_local)


def solution(mesh):
    return jax.shard_map(
        functools.partial(body, mesh.shape["dp"], mesh.shape["fsdp"]),
        mesh=mesh,
        in_specs=(
            P("dp", None, "fsdp", None, None, None),
            P("dp", None, "fsdp", None),
            P("dp", None),
            P(),
            P("fsdp", None, None, None),
            P(),
            P(),
        ),
        out_specs=(P("fsdp", None, None, None), P()),
        check_vma=False,
    )
```

```python
import functools
import math

import jax
import jax.numpy as jnp
import ml_dtypes
import numpy as np
from jax import lax
from jax.experimental import pallas as pl
from jax.experimental.pallas import tpu as pltpu
from jax.sharding import PartitionSpec as P

MX = 4
MY = 4
MZ = 2
MODES = MX * MY * MZ
VMEM_BYTES = 40 * 1024 * 1024
f32 = jnp.float32
bf16 = jnp.bfloat16
inv_root_two_pi = 0.3989422804014327
half_log2e = 0.7213475204444817
erf_p = 0.3275911 * 0.7071067811865476
erf_a = tuple(0.5 * a for a in (0.254829592, -0.284496736, 1.421413741, -1.453152027, 1.061405429))


def split_bf16(values):
    high = values.astype(ml_dtypes.bfloat16)
    low = (values - high.astype(np.float64)).astype(ml_dtypes.bfloat16)
    return high, low


def angles(mode_ids, length):
    product = np.outer(mode_ids, np.arange(length)) % length
    return product * (2.0 * math.pi / length)


def phase_constants(length):
    y_angle = angles(np.arange(MY) - MY // 2, length)
    z_angle = angles(np.arange(MZ), length)
    rounded = lambda v: v.astype(np.float32).astype(ml_dtypes.bfloat16).astype(np.float64)
    cz, sz = rounded(np.cos(z_angle)), rounded(-np.sin(z_angle))
    cy, sy = np.cos(y_angle), -np.sin(y_angle)
    both = lambda a, b: (a[:, None, :, None] * b[None, :, None, :]).reshape(MY * MZ, length * length)
    fwd = np.concatenate([both(cy, cz) - both(sy, sz), both(sy, cz) + both(cy, sz)], axis=0)
    fwd = np.concatenate(split_bf16(fwd), axis=0)
    cz, sz = np.cos(z_angle), np.sin(z_angle)
    cy, sy = np.cos(y_angle), np.sin(y_angle)
    inv = np.concatenate([both(cy, cz) - both(sy, sz), -(both(sy, cz) + both(cy, sz))], axis=0).T
    high, low = split_bf16(inv)
    pad = np.zeros((length * length, 128 - 4 * high.shape[1]), ml_dtypes.bfloat16)
    inv = np.concatenate([high, low, high, low, pad], axis=1)
    x_angle = angles(np.arange(MX) - MX // 2, length).T
    xtab = np.stack([np.cos(x_angle), np.sin(x_angle)], axis=2).astype(np.float32)
    return fwd, inv, xtab.reshape(-1)


def scalar_places(slots):
    return dict(count=slots, total=slots + 1, shard=slots + 2, first=slots + 3)


def combine_planes(q_ref, xtab_ref, cell0, shard, planes, scale, store):
    for d in range(MX):
        i = lax.rem(shard + d, MX)
        re = jnp.zeros((8, 128), f32)
        im = jnp.zeros((8, 128), f32)
        for a in range(planes):
            at = ((cell0 + a) * MX + i) * 2
            c = xtab_ref[at]
            s = xtab_ref[at + 1]
            q_re = q_ref[a, 0:8, :]
            q_im = q_ref[a, 8:16, :]
            re = re + (q_re * c + q_im * s)
            im = im + (q_im * c - q_re * s)
        store(d, re * scale, im * scale)


def forward_kernel(
    slots, planes, step_planes, scale, meta_ref, xtab_ref, f_ref, basis_ref, *rest
):
    outs, q_ref = rest[:MX], rest[MX]
    place = scalar_places(slots)
    g, blk = pl.program_id(0), pl.program_id(1)
    live = g < meta_ref[place["count"]]
    row = pl.multiple_of(g * 16, 16)

    @pl.when(live)
    def _():
        cells = f_ref.shape[3] * f_ref.shape[4]
        for p in range(step_planes):
            field = f_ref[0, 0, p].reshape(cells, 128)
            part = jnp.dot(basis_ref[...], field, preferred_element_type=f32)
            q_ref[blk * step_planes + p] = part[0:16] + part[16:32]

        @pl.when(blk == planes // step_planes - 1)
        def _():
            def store(d, re, im):
                outs[d][pl.ds(row, 8), :] = re
                outs[d][pl.ds(row + 8, 8), :] = im

            combine_planes(
                q_ref, xtab_ref, meta_ref[place["first"]], meta_ref[place["shard"]], planes, scale, store
            )

    @pl.when(jnp.logical_not(live) & (blk == 0))
    def _():
        for out in outs:
            out[pl.ds(row, 16), :] = jnp.zeros((16, 128), f32)


def gelu_parts(pre):
    bell = jnp.exp2(pre * pre * (-half_log2e))
    t = pl.reciprocal(1.0 + erf_p * jnp.abs(pre), approx=True)
    poly = erf_a[4]
    for a in (erf_a[3], erf_a[2], erf_a[1], erf_a[0]):
        poly = poly * t + a
    tail = poly * t * bell
    cdf = jnp.where(pre >= 0.0, 1.0 - tail, tail)
    return cdf, bell


def backward_kernel(
    slots, planes, step_planes, rows_step, scale, meta_ref, xtab_ref, f_ref, t_ref, *rest
):
    specs = rest[:MX]
    w_ref, proj_ref, inv_ref, basis_ref, eye_ref, ones_ref = rest[MX : MX + 6]
    outs = rest[MX + 6 : 2 * MX + 6]
    rhs_ref, pre_ref, slope_ref, both_ref, d_ref, total_ref, q_ref, t16_ref, spec_ref = rest[2 * MX + 6 :]
    place = scalar_places(slots)
    g, blk = pl.program_id(0), pl.program_id(1)
    blocks = planes // step_planes
    live = g < meta_ref[place["count"]]
    row = pl.multiple_of(g * 16, 16)
    shard = meta_ref[place["shard"]]
    cell0 = meta_ref[place["first"]]
    cells = f_ref.shape[3] * f_ref.shape[4]
    third = cells // 3
    unroll = 2 if step_planes % 2 == 0 else 1

    @pl.when((g == 0) & (blk == 0))
    def _():
        total_ref[...] = jnp.zeros_like(total_ref)
        for n in range(2):
            rhs_ref[n, 0:128, :] = w_ref[...]
            rhs_ref[n, 128:256, :] = jnp.zeros((128, 128), bf16)

    @pl.when(live)
    def _():
        @pl.when(blk == 0)
        def _():
            lines = t_ref[0, 0].astype(f32)
            for a in range(planes):
                line = jnp.broadcast_to(lines[a : a + 1, :], (16, cells))
                t16_ref[a] = line.astype(bf16)
            for d in range(MX):
                spec_ref[d] = specs[d][pl.ds(row, 16), :].astype(f32)

        count = meta_ref[place["total"]].astype(f32)
        proj = proj_ref[...]
        proj_scaled = proj / jnp.full((1, 128), count, f32)

        def first_rows(a, rhs):
            re = jnp.zeros((8, 128), f32)
            im = jnp.zeros((8, 128), f32)
            for d in range(MX):
                i = lax.rem(shard - d + MX, MX)
                at = ((cell0 + a) * MX + i) * 2
                c = xtab_ref[at]
                s = xtab_ref[at + 1]
                s_re = spec_ref[d, 0:8, :]
                s_im = spec_ref[d, 8:16, :]
                re = re + (s_re * c - s_im * s)
                im = im + (s_re * s + s_im * c)
            first = jnp.concatenate([re, im], axis=0) * scale
            high = first.astype(bf16)
            low = (first - high.astype(f32)).astype(bf16)
            rhs[128:144, :] = high
            rhs[144:160, :] = high
            rhs[160:176, :] = low
            rhs[176:192, :] = low

        def planes_together(n, carry):
            units = [(u, k) for u in range(unroll) for k in range(3)]
            q = [jnp.zeros((32, 128), f32) for _ in range(unroll)]

            def before(s):
                u, k = units[s]
                rhs = rhs_ref.at[u % 2]
                if k == 0:
                    first_rows(blk * step_planes + n * unroll + u, rhs)
                field = f_ref[0, 0, n * unroll + u].reshape(cells, 128)
                part = slice(k * third, (k + 1) * third)
                lhs = jnp.concatenate([field[part], inv_ref[part, :]], axis=1)
                pre_ref[s % 2] = jnp.dot(lhs, rhs[...], preferred_element_type=f32)

            def elementwise(s):
                u, k = units[s]
                a = blk * step_planes + n * unroll + u
                for r0 in range(0, third, rows_step):
                    rows = slice(r0, r0 + rows_step)
                    pre = pre_ref[s % 2, rows, :]
                    cdf, bell = gelu_parts(pre)
                    slope_ref[s % 2, rows, :] = (cdf + pre * bell * inv_root_two_pi) * proj_scaled
                    both_ref[s % 2, rows, 0:128] = (pre * cdf * proj).astype(bf16)
                    for r1 in range(r0, r0 + rows_step, 16):
                        n1 = r1 % 128
                        at = k * third + r1 - n1
                        line = t16_ref[a, :, at : at + 128]
                        both_ref[s % 2, r1 : r1 + 16, 128:256] = line * eye_ref[n1 : n1 + 16, :]

            def after(s):
                resid = jnp.dot(both_ref[s % 2], ones_ref[...], preferred_element_type=f32)
                for r0 in range(0, third, rows_step):
                    rows = slice(r0, r0 + rows_step)
                    d_ref[s % 2, rows, :] = (resid[rows] * slope_ref[s % 2, rows, :]).astype(bf16)

            def last(s):
                u, k = units[s]
                field = f_ref[0, 0, n * unroll + u].reshape(cells, 128)
                part = slice(k * third, (k + 1) * third)
                lhs = jnp.concatenate([field[part].T, basis_ref[:, part]], axis=0)
                sums = jnp.dot(lhs, d_ref[s % 2], preferred_element_type=f32)
                total_ref[...] += sums[0:128]
                q[u] = q[u] + sums[128:160]
                if k == 2:
                    q_ref[blk * step_planes + n * unroll + u] = q[u][0:16] + q[u][16:32]

            for s in range(len(units) + 3):
                if s >= 3:
                    last(s - 3)
                if 0 <= s - 2 < len(units):
                    after(s - 2)
                if 0 <= s - 1 < len(units):
                    elementwise(s - 1)
                if s < len(units):
                    before(s)
            return carry

        lax.fori_loop(0, step_planes // unroll, planes_together, 0)

        @pl.when(blk == blocks - 1)
        def _():
            def store(d, re, im):
                outs[d][pl.ds(row, 8), :] = re
                outs[d][pl.ds(row + 8, 8), :] = im

            combine_planes(q_ref, xtab_ref, cell0, shard, planes, scale, store)

    @pl.when(jnp.logical_not(live) & (blk == 0))
    def _():
        for out in outs:
            out[pl.ds(row, 16), :] = jnp.zeros((16, 128), f32)

    @pl.when((g == slots - 1) & (blk == blocks - 1))
    def _():
        part = 128 // MX
        for d in range(MX):
            i = lax.rem(shard + d, MX)
            at = pl.multiple_of(i * part, part)
            outs[d][slots * 16 : slots * 16 + part, :] = total_ref[pl.ds(at, part), :]


def mix_kernel(slots, per, shards, *refs):
    parts = refs[:shards]
    w_ref, coeff_out, spec_out, c_ref, s_ref = refs[shards:]
    total = parts[0][...]
    for part in parts[1:]:
        total = total + part[...]
    coeff = total.astype(bf16)
    coeff_out[...] = coeff
    c_ref[...] = coeff.astype(f32)
    for m in range(per):
        re_rows = pl.ds(m, slots, stride=2 * per)
        im_rows = pl.ds(per + m, slots, stride=2 * per)
        re = c_ref[re_rows, :].astype(bf16)
        im = c_ref[im_rows, :].astype(bf16)
        weight = w_ref[m].reshape(256, 128)
        s_ref[re_rows, :] = jnp.dot(
            jnp.concatenate([re, -im], axis=1), weight, preferred_element_type=f32
        )
        s_ref[im_rows, :] = jnp.dot(
            jnp.concatenate([im, re], axis=1), weight, preferred_element_type=f32
        )
    spec_out[...] = s_ref[...].astype(bf16)


def sum_kernel(count, *refs):
    total = refs[0][...]
    for part in refs[1:count]:
        total = total + part[...]
    refs[count][...] = total


def local_sum_kernel(count, rows, *refs):
    size = refs[count].shape[0]
    total = refs[0][rows : rows + size, :]
    for part in refs[1:count]:
        total = total + part[rows : rows + size, :]
    refs[count][...] = total


def weight_kernel(lanes, slots, per, *refs):
    coeffs, backs = refs[:lanes], refs[lanes : 2 * lanes]
    out_ref, c_ref, b_ref = refs[2 * lanes :]
    rows = slots * 2 * per
    for n in range(lanes):
        c_ref[n * rows : (n + 1) * rows, :] = coeffs[n][...].astype(f32)
        b_ref[n * rows : (n + 1) * rows, :] = backs[n][0:rows, :]
    for m in range(per):
        re_rows = pl.ds(m, lanes * slots, stride=2 * per)
        im_rows = pl.ds(per + m, lanes * slots, stride=2 * per)
        c_re = c_ref[re_rows, :].astype(bf16)
        c_im = c_ref[im_rows, :].astype(bf16)
        b_re = b_ref[re_rows, :]
        b_im = b_ref[im_rows, :]
        left = jnp.concatenate([c_re, c_im], axis=0)
        right = jnp.concatenate(
            [jnp.concatenate([b_re, b_im], axis=1), jnp.concatenate([b_im, -b_re], axis=1)], axis=0
        )
        high = right.astype(bf16)
        low = (right - high.astype(f32)).astype(bf16)
        left = jnp.concatenate([left, left], axis=0)
        right = jnp.concatenate([high, low], axis=0)
        grad = lax.dot_general(
            left, right, (((0,), (0,)), ((), ())), preferred_element_type=f32
        )
        out_ref[m, 0] = grad[:, 0:128]
        out_ref[m, 1] = grad[:, 128:256]


def place_kernel(shards, meta_ref, *refs):
    out_ref = refs[shards]
    size = refs[0].shape[0]
    for d in range(shards):
        i = lax.rem(meta_ref[0] - d + shards, shards)
        out_ref[pl.ds(pl.multiple_of(i * size, size), size), :] = refs[d][...]


def whole_vmem(count):
    return [pl.BlockSpec(memory_space=pltpu.VMEM)] * count


def params():
    return pltpu.CompilerParams(vmem_limit_bytes=VMEM_BYTES)


def rotations(value_of, axis, size):
    got = [value_of(0)]
    for d in range(1, size):
        perm = [(s, (s + d) % size) for s in range(size)]
        got.append(lax.ppermute(value_of(d), axis, perm))
    return got


def body(lanes, shards, fields, targets, lists, counts, spectral_w, local_w, proj):
    _, slots, planes, grid_len, _, width = fields.shape
    per = MODES // shards
    split = shards // MX
    cells = grid_len * grid_len
    step_planes = max(n for n in (1, 2, 3, 4) if planes % n == 0)
    blocks = planes // step_planes
    basis, inverse, xtab = phase_constants(grid_len)
    lane = lax.axis_index("dp")
    shard = lax.axis_index("fsdp").astype(jnp.int32)
    turn = shard if split == 1 else jnp.int32(0)
    meta = jnp.concatenate(
        [
            lists[0],
            counts[lane][None],
            jnp.sum(counts)[None],
            turn[None],
            (shard * planes)[None],
        ]
    ).astype(jnp.int32)
    place = scalar_places(slots)

    def field_block(g, blk, meta_ref, xtab_ref):
        count = meta_ref[place["count"]]
        slot = meta_ref[jnp.minimum(g, count - 1)]
        return (0, slot, jnp.where(g < count, blk, blocks - 1), 0, 0, 0)

    def target_block(g, blk, meta_ref, xtab_ref):
        count = meta_ref[place["count"]]
        return (0, meta_ref[jnp.minimum(g, count - 1)], 0, 0)

    def fixed(*shape):
        return pl.BlockSpec(shape, lambda g, blk, meta_ref, xtab_ref: (0,) * len(shape))

    field_spec = pl.BlockSpec((1, 1, step_planes, grid_len, grid_len, width), field_block)
    part_rows = slots * 16
    parts = pl.pallas_call(
        functools.partial(forward_kernel, slots, planes, step_planes, float(grid_len) ** (-1.5)),
        grid_spec=pltpu.PrefetchScalarGridSpec(
            num_scalar_prefetch=2,
            grid=(slots, blocks),
            in_specs=[field_spec, fixed(*basis.shape)],
            out_specs=[fixed(part_rows, width)] * MX,
            scratch_shapes=[pltpu.VMEM((planes, 16, width), f32)],
        ),
        out_shape=[jax.ShapeDtypeStruct((part_rows, width), f32)] * MX,
        compiler_params=params(),
        name="forward_modes",
    )(meta, xtab, fields, basis)

    def shard_parts(pieces, count):
        if split == 1:
            return lambda d: pieces[d]
        stacked = jnp.stack(pieces).reshape(MX, count, 2, split, per, width)
        stacked = jnp.moveaxis(stacked, 3, 1).reshape(shards, count * 2 * per, width)
        return lambda d: lax.dynamic_index_in_dim(stacked, (shard + d) % shards, 0, keepdims=False)

    def mode_parts(pieces, count):
        if split == 1:
            return pieces
        stacked = jnp.stack(pieces)[(shard - jnp.arange(shards)) % shards]
        stacked = stacked.reshape(MX, split, count, 2, per, width)
        stacked = jnp.moveaxis(stacked, 1, 3).reshape(MX, count * 16, width)
        return [stacked[(-d) % MX] for d in range(MX)]

    came = rotations(shard_parts(parts, slots), "fsdp", shards)
    own_rows = slots * 2 * per
    coeff, own_spectrum = pl.pallas_call(
        functools.partial(mix_kernel, slots, per, shards),
        in_specs=whole_vmem(shards + 1),
        out_specs=whole_vmem(2),
        out_shape=[jax.ShapeDtypeStruct((own_rows, width), bf16)] * 2,
        scratch_shapes=[pltpu.VMEM((own_rows, width), f32)] * 2,
        compiler_params=params(),
        name="mix_modes",
    )(*came, spectral_w)
    spectrum = mode_parts(rotations(lambda d: own_spectrum, "fsdp", shards), slots)
    coeffs = rotations(lambda d: coeff, "dp", lanes)

    local_rows = width // MX
    eye = np.eye(128, dtype=ml_dtypes.bfloat16)
    ones = np.ones((128, 128), ml_dtypes.bfloat16)
    ones = np.concatenate([ones, -ones], axis=0)
    results = pl.pallas_call(
        functools.partial(backward_kernel, slots, planes, step_planes, 64, float(MODES) ** (-0.5)),
        grid_spec=pltpu.PrefetchScalarGridSpec(
            num_scalar_prefetch=2,
            grid=(slots, blocks),
            in_specs=[field_spec, pl.BlockSpec((1, 1, planes, cells), target_block)]
            + [fixed(part_rows, width)] * MX
            + [
                fixed(width, width),
                fixed(1, width),
                fixed(*inverse.shape),
                fixed(*basis.shape),
                fixed(*eye.shape),
                fixed(*ones.shape),
            ],
            out_specs=[fixed(part_rows + local_rows, width)] * MX,
            scratch_shapes=[
                pltpu.VMEM((2, 256, width), bf16),
                pltpu.VMEM((2, cells // 3, width), f32),
                pltpu.VMEM((2, cells // 3, width), f32),
                pltpu.VMEM((2, cells // 3, 2 * width), bf16),
                pltpu.VMEM((2, cells // 3, width), bf16),
                pltpu.VMEM((width, width), f32),
                pltpu.VMEM((planes, 16, width), f32),
                pltpu.VMEM((planes, 16, cells), bf16),
                pltpu.VMEM((MX, 16, width), f32),
            ],
        ),
        out_shape=[jax.ShapeDtypeStruct((part_rows + local_rows, width), f32)] * MX,
        compiler_params=params(),
        cost_estimate=pl.CostEstimate(
            flops=4 * slots * planes * cells * 256 * 256,
            bytes_accessed=slots * planes * cells * width * 2,
            transcendentals=0,
        ),
        name="backward_modes",
    )(
        meta, xtab, fields, targets, *spectrum, local_w, proj.reshape(1, width), inverse, basis, eye, ones
    )

    if split == 1:
        chunk = lambda d: results[d]
    else:
        backs = shard_parts([r[:part_rows] for r in results], slots)
        local = jnp.concatenate([r[part_rows:] for r in results], axis=0)
        rows = width // shards
        chunk = lambda d: jnp.concatenate(
            [backs(d), lax.dynamic_slice_in_dim(local, (shard + d) % shards * rows, rows, 0)], axis=0
        )
    came = rotations(chunk, "fsdp", shards)
    own_sum = pl.pallas_call(
        functools.partial(sum_kernel, shards),
        in_specs=whole_vmem(shards),
        out_specs=pl.BlockSpec(memory_space=pltpu.VMEM),
        out_shape=jax.ShapeDtypeStruct(came[0].shape, f32),
        compiler_params=params(),
        name="sum_shards",
    )(*came)
    sums = rotations(lambda d: own_sum, "dp", lanes)
    own_local = pl.pallas_call(
        functools.partial(local_sum_kernel, lanes, own_rows),
        in_specs=whole_vmem(lanes),
        out_specs=pl.BlockSpec(memory_space=pltpu.VMEM),
        out_shape=jax.ShapeDtypeStruct((width // shards, width), f32),
        compiler_params=params(),
        name="sum_local",
    )(*sums)
    locals_ = rotations(lambda d: own_local, "fsdp", shards)
    grad_spectral = pl.pallas_call(
        functools.partial(weight_kernel, lanes, slots, per),
        in_specs=whole_vmem(2 * lanes),
        out_specs=pl.BlockSpec(memory_space=pltpu.VMEM),
        out_shape=jax.ShapeDtypeStruct((per, 2, width, width), f32),
        scratch_shapes=[pltpu.VMEM((lanes * own_rows, width), f32)] * 2,
        compiler_params=params(),
        cost_estimate=pl.CostEstimate(
            flops=2 * per * 192 * 128 * 256, bytes_accessed=2 * per * 2 * width * width * 4, transcendentals=0
        ),
        name="weight_grad",
    )(*coeffs, *sums)
    grad_local = pl.pallas_call(
        functools.partial(place_kernel, shards),
        in_specs=[pl.BlockSpec(memory_space=pltpu.SMEM)] + whole_vmem(shards),
        out_specs=pl.BlockSpec(memory_space=pltpu.VMEM),
        out_shape=jax.ShapeDtypeStruct((width, width), f32),
        compiler_params=params(),
        name="place_local",
    )(shard[None], *locals_)
    return (grad_spectral, grad_local)


def solution(mesh):
    return jax.shard_map(
        functools.partial(body, mesh.shape["dp"], mesh.shape["fsdp"]),
        mesh=mesh,
        in_specs=(
            P("dp", None, "fsdp", None, None, None),
            P("dp", None, "fsdp", None),
            P("dp", None),
            P(),
            P("fsdp", None, None, None),
            P(),
            P(),
        ),
        out_specs=(P("fsdp", None, None, None), P()),
        check_vma=False,
    )
```

```python
import functools
import math

import jax
import jax.numpy as jnp
import ml_dtypes
import numpy as np
from jax import lax
from jax.experimental import pallas as pl
from jax.experimental.pallas import tpu as pltpu
from jax.sharding import PartitionSpec as P

MX = 4
MY = 4
MZ = 2
MODES = MX * MY * MZ
VMEM_BYTES = 40 * 1024 * 1024
f32 = jnp.float32
bf16 = jnp.bfloat16
inv_root_two_pi = 0.3989422804014327
half_log2e = 0.7213475204444817
root_half = 0.7071067811865476


def split_bf16(values):
    high = values.astype(ml_dtypes.bfloat16)
    low = (values - high.astype(np.float64)).astype(ml_dtypes.bfloat16)
    return high, low


def angles(mode_ids, length):
    product = np.outer(mode_ids, np.arange(length)) % length
    return product * (2.0 * math.pi / length)


def phase_constants(length):
    y_angle = angles(np.arange(MY) - MY // 2, length)
    z_angle = angles(np.arange(MZ), length)
    rounded = lambda v: v.astype(np.float32).astype(ml_dtypes.bfloat16).astype(np.float64)
    cz, sz = rounded(np.cos(z_angle)), rounded(-np.sin(z_angle))
    cy, sy = np.cos(y_angle), -np.sin(y_angle)
    both = lambda a, b: (a[:, None, :, None] * b[None, :, None, :]).reshape(MY * MZ, length * length)
    fwd = np.concatenate([both(cy, cz) - both(sy, sz), both(sy, cz) + both(cy, sz)], axis=0)
    fwd = np.concatenate(split_bf16(fwd), axis=0)
    cz, sz = np.cos(z_angle), np.sin(z_angle)
    cy, sy = np.cos(y_angle), np.sin(y_angle)
    inv = np.concatenate([both(cy, cz) - both(sy, sz), -(both(sy, cz) + both(cy, sz))], axis=0).T
    high, low = split_bf16(inv)
    pad = np.zeros((length * length, 128 - 4 * high.shape[1]), ml_dtypes.bfloat16)
    inv = np.concatenate([high, low, high, low, pad], axis=1)
    x_angle = angles(np.arange(MX) - MX // 2, length).T
    xtab = np.stack([np.cos(x_angle), np.sin(x_angle)], axis=2).astype(np.float32)
    return fwd, inv, xtab.reshape(-1)


def scalar_places(slots):
    return dict(count=slots, total=slots + 1, shard=slots + 2, first=slots + 3)


def combine_planes(q_ref, xtab_ref, cell0, shard, planes, scale, store):
    for d in range(MX):
        i = lax.rem(shard + d, MX)
        re = jnp.zeros((8, 128), f32)
        im = jnp.zeros((8, 128), f32)
        for a in range(planes):
            at = ((cell0 + a) * MX + i) * 2
            c = xtab_ref[at]
            s = xtab_ref[at + 1]
            q_re = q_ref[a, 0:8, :]
            q_im = q_ref[a, 8:16, :]
            re = re + (q_re * c + q_im * s)
            im = im + (q_im * c - q_re * s)
        store(d, re * scale, im * scale)


def forward_kernel(
    slots, planes, step_planes, scale, meta_ref, xtab_ref, f_ref, basis_ref, *rest
):
    outs, q_ref = rest[:MX], rest[MX]
    place = scalar_places(slots)
    g, blk = pl.program_id(0), pl.program_id(1)
    live = g < meta_ref[place["count"]]
    row = pl.multiple_of(g * 16, 16)

    @pl.when(live)
    def _():
        cells = f_ref.shape[3] * f_ref.shape[4]
        for p in range(step_planes):
            field = f_ref[0, 0, p].reshape(cells, 128)
            part = jnp.dot(basis_ref[...], field, preferred_element_type=f32)
            q_ref[blk * step_planes + p] = part[0:16] + part[16:32]

        @pl.when(blk == planes // step_planes - 1)
        def _():
            def store(d, re, im):
                outs[d][pl.ds(row, 8), :] = re
                outs[d][pl.ds(row + 8, 8), :] = im

            combine_planes(
                q_ref, xtab_ref, meta_ref[place["first"]], meta_ref[place["shard"]], planes, scale, store
            )

    @pl.when(jnp.logical_not(live) & (blk == 0))
    def _():
        for out in outs:
            out[pl.ds(row, 16), :] = jnp.zeros((16, 128), f32)


def gelu_parts(pre):
    bell = jnp.exp2(pre * pre * (-half_log2e))
    cdf = 0.5 + 0.5 * lax.erf(pre * root_half)
    return cdf, bell


def backward_kernel(
    slots, planes, step_planes, rows_step, scale, meta_ref, xtab_ref, f_ref, t_ref, *rest
):
    specs = rest[:MX]
    w_ref, proj_ref, inv_ref, basis_ref, eye_ref, ones_ref = rest[MX : MX + 6]
    outs = rest[MX + 6 : 2 * MX + 6]
    rhs_ref, pre_ref, slope_ref, both_ref, d_ref, total_ref, q_ref, t16_ref, spec_ref = rest[2 * MX + 6 :]
    place = scalar_places(slots)
    g, blk = pl.program_id(0), pl.program_id(1)
    blocks = planes // step_planes
    live = g < meta_ref[place["count"]]
    row = pl.multiple_of(g * 16, 16)
    shard = meta_ref[place["shard"]]
    cell0 = meta_ref[place["first"]]
    cells = f_ref.shape[3] * f_ref.shape[4]
    third = cells // 3
    unroll = 2 if step_planes % 2 == 0 else 1

    @pl.when((g == 0) & (blk == 0))
    def _():
        total_ref[...] = jnp.zeros_like(total_ref)
        for n in range(2):
            rhs_ref[n, 0:128, :] = w_ref[...]
            rhs_ref[n, 128:256, :] = jnp.zeros((128, 128), bf16)

    @pl.when(live)
    def _():
        @pl.when(blk == 0)
        def _():
            lines = t_ref[0, 0].astype(f32)
            for a in range(planes):
                line = jnp.broadcast_to(lines[a : a + 1, :], (16, cells))
                t16_ref[a] = line.astype(bf16)
            for d in range(MX):
                spec_ref[d] = specs[d][pl.ds(row, 16), :].astype(f32)

        count = meta_ref[place["total"]].astype(f32)
        proj = proj_ref[...]
        proj_scaled = proj / jnp.full((1, 128), count, f32)

        def first_rows(a, rhs):
            re = jnp.zeros((8, 128), f32)
            im = jnp.zeros((8, 128), f32)
            for d in range(MX):
                i = lax.rem(shard - d + MX, MX)
                at = ((cell0 + a) * MX + i) * 2
                c = xtab_ref[at]
                s = xtab_ref[at + 1]
                s_re = spec_ref[d, 0:8, :]
                s_im = spec_ref[d, 8:16, :]
                re = re + (s_re * c - s_im * s)
                im = im + (s_re * s + s_im * c)
            first = jnp.concatenate([re, im], axis=0) * scale
            high = first.astype(bf16)
            low = (first - high.astype(f32)).astype(bf16)
            rhs[128:144, :] = high
            rhs[144:160, :] = high
            rhs[160:176, :] = low
            rhs[176:192, :] = low

        def planes_together(n, carry):
            units = [(u, k) for u in range(unroll) for k in range(3)]
            q = [jnp.zeros((32, 128), f32) for _ in range(unroll)]

            def before(s):
                u, k = units[s]
                rhs = rhs_ref.at[u % 2]
                if k == 0:
                    first_rows(blk * step_planes + n * unroll + u, rhs)
                field = f_ref[0, 0, n * unroll + u].reshape(cells, 128)
                part = slice(k * third, (k + 1) * third)
                lhs = jnp.concatenate([field[part], inv_ref[part, :]], axis=1)
                pre_ref[s % 2] = jnp.dot(lhs, rhs[...], preferred_element_type=f32)

            def elementwise(s):
                u, k = units[s]
                a = blk * step_planes + n * unroll + u
                for r0 in range(0, third, rows_step):
                    rows = slice(r0, r0 + rows_step)
                    pre = pre_ref[s % 2, rows, :]
                    cdf, bell = gelu_parts(pre)
                    slope_ref[s % 2, rows, :] = (cdf + pre * bell * inv_root_two_pi) * proj_scaled
                    both_ref[s % 2, rows, 0:128] = (pre * cdf * proj).astype(bf16)
                    for r1 in range(r0, r0 + rows_step, 16):
                        n1 = r1 % 128
                        at = k * third + r1 - n1
                        line = t16_ref[a, :, at : at + 128]
                        both_ref[s % 2, r1 : r1 + 16, 128:256] = line * eye_ref[n1 : n1 + 16, :]

            def after(s):
                resid = jnp.dot(both_ref[s % 2], ones_ref[...], preferred_element_type=f32)
                for r0 in range(0, third, rows_step):
                    rows = slice(r0, r0 + rows_step)
                    d_ref[s % 2, rows, :] = (resid[rows] * slope_ref[s % 2, rows, :]).astype(bf16)

            def last(s):
                u, k = units[s]
                field = f_ref[0, 0, n * unroll + u].reshape(cells, 128)
                part = slice(k * third, (k + 1) * third)
                lhs = jnp.concatenate([field[part].T, basis_ref[:, part]], axis=0)
                sums = jnp.dot(lhs, d_ref[s % 2], preferred_element_type=f32)
                total_ref[...] += sums[0:128]
                q[u] = q[u] + sums[128:160]
                if k == 2:
                    q_ref[blk * step_planes + n * unroll + u] = q[u][0:16] + q[u][16:32]

            for s in range(len(units) + 3):
                if s >= 3:
                    last(s - 3)
                if 0 <= s - 2 < len(units):
                    after(s - 2)
                if 0 <= s - 1 < len(units):
                    elementwise(s - 1)
                if s < len(units):
                    before(s)
            return carry

        lax.fori_loop(0, step_planes // unroll, planes_together, 0)

        @pl.when(blk == blocks - 1)
        def _():
            def store(d, re, im):
                outs[d][pl.ds(row, 8), :] = re
                outs[d][pl.ds(row + 8, 8), :] = im

            combine_planes(q_ref, xtab_ref, cell0, shard, planes, scale, store)

    @pl.when(jnp.logical_not(live) & (blk == 0))
    def _():
        for out in outs:
            out[pl.ds(row, 16), :] = jnp.zeros((16, 128), f32)

    @pl.when((g == slots - 1) & (blk == blocks - 1))
    def _():
        part = 128 // MX
        for d in range(MX):
            i = lax.rem(shard + d, MX)
            at = pl.multiple_of(i * part, part)
            outs[d][slots * 16 : slots * 16 + part, :] = total_ref[pl.ds(at, part), :]


def mix_kernel(slots, per, shards, *refs):
    parts = refs[:shards]
    w_ref, coeff_out, spec_out, c_ref, s_ref = refs[shards:]
    total = parts[0][...]
    for part in parts[1:]:
        total = total + part[...]
    coeff = total.astype(bf16)
    coeff_out[...] = coeff
    c_ref[...] = coeff.astype(f32)
    for m in range(per):
        re_rows = pl.ds(m, slots, stride=2 * per)
        im_rows = pl.ds(per + m, slots, stride=2 * per)
        re = c_ref[re_rows, :].astype(bf16)
        im = c_ref[im_rows, :].astype(bf16)
        weight = w_ref[m].reshape(256, 128)
        s_ref[re_rows, :] = jnp.dot(
            jnp.concatenate([re, -im], axis=1), weight, preferred_element_type=f32
        )
        s_ref[im_rows, :] = jnp.dot(
            jnp.concatenate([im, re], axis=1), weight, preferred_element_type=f32
        )
    spec_out[...] = s_ref[...].astype(bf16)


def sum_kernel(count, *refs):
    total = refs[0][...]
    for part in refs[1:count]:
        total = total + part[...]
    refs[count][...] = total


def local_sum_kernel(count, rows, *refs):
    size = refs[count].shape[0]
    total = refs[0][rows : rows + size, :]
    for part in refs[1:count]:
        total = total + part[rows : rows + size, :]
    refs[count][...] = total


def weight_kernel(lanes, slots, per, *refs):
    coeffs, backs = refs[:lanes], refs[lanes : 2 * lanes]
    out_ref, c_ref, b_ref = refs[2 * lanes :]
    rows = slots * 2 * per
    for n in range(lanes):
        c_ref[n * rows : (n + 1) * rows, :] = coeffs[n][...].astype(f32)
        b_ref[n * rows : (n + 1) * rows, :] = backs[n][0:rows, :]
    for m in range(per):
        re_rows = pl.ds(m, lanes * slots, stride=2 * per)
        im_rows = pl.ds(per + m, lanes * slots, stride=2 * per)
        c_re = c_ref[re_rows, :].astype(bf16)
        c_im = c_ref[im_rows, :].astype(bf16)
        b_re = b_ref[re_rows, :]
        b_im = b_ref[im_rows, :]
        left = jnp.concatenate([c_re, c_im], axis=0)
        right = jnp.concatenate(
            [jnp.concatenate([b_re, b_im], axis=1), jnp.concatenate([b_im, -b_re], axis=1)], axis=0
        )
        high = right.astype(bf16)
        low = (right - high.astype(f32)).astype(bf16)
        left = jnp.concatenate([left, left], axis=0)
        right = jnp.concatenate([high, low], axis=0)
        grad = lax.dot_general(
            left, right, (((0,), (0,)), ((), ())), preferred_element_type=f32
        )
        out_ref[m, 0] = grad[:, 0:128]
        out_ref[m, 1] = grad[:, 128:256]


def place_kernel(shards, meta_ref, *refs):
    out_ref = refs[shards]
    size = refs[0].shape[0]
    for d in range(shards):
        i = lax.rem(meta_ref[0] - d + shards, shards)
        out_ref[pl.ds(pl.multiple_of(i * size, size), size), :] = refs[d][...]


def whole_vmem(count):
    return [pl.BlockSpec(memory_space=pltpu.VMEM)] * count


def params():
    return pltpu.CompilerParams(vmem_limit_bytes=VMEM_BYTES)


def rotations(value_of, axis, size):
    got = [value_of(0)]
    for d in range(1, size):
        perm = [(s, (s + d) % size) for s in range(size)]
        got.append(lax.ppermute(value_of(d), axis, perm))
    return got


def body(lanes, shards, fields, targets, lists, counts, spectral_w, local_w, proj):
    _, slots, planes, grid_len, _, width = fields.shape
    per = MODES // shards
    split = shards // MX
    cells = grid_len * grid_len
    step_planes = max(n for n in (1, 2, 3, 4) if planes % n == 0)
    blocks = planes // step_planes
    basis, inverse, xtab = phase_constants(grid_len)
    lane = lax.axis_index("dp")
    shard = lax.axis_index("fsdp").astype(jnp.int32)
    turn = shard if split == 1 else jnp.int32(0)
    meta = jnp.concatenate(
        [
            lists[0],
            counts[lane][None],
            jnp.sum(counts)[None],
            turn[None],
            (shard * planes)[None],
        ]
    ).astype(jnp.int32)
    place = scalar_places(slots)

    def field_block(g, blk, meta_ref, xtab_ref):
        count = meta_ref[place["count"]]
        slot = meta_ref[jnp.minimum(g, count - 1)]
        return (0, slot, jnp.where(g < count, blk, blocks - 1), 0, 0, 0)

    def target_block(g, blk, meta_ref, xtab_ref):
        count = meta_ref[place["count"]]
        return (0, meta_ref[jnp.minimum(g, count - 1)], 0, 0)

    def fixed(*shape):
        return pl.BlockSpec(shape, lambda g, blk, meta_ref, xtab_ref: (0,) * len(shape))

    field_spec = pl.BlockSpec((1, 1, step_planes, grid_len, grid_len, width), field_block)
    part_rows = slots * 16
    parts = pl.pallas_call(
        functools.partial(forward_kernel, slots, planes, step_planes, float(grid_len) ** (-1.5)),
        grid_spec=pltpu.PrefetchScalarGridSpec(
            num_scalar_prefetch=2,
            grid=(slots, blocks),
            in_specs=[field_spec, fixed(*basis.shape)],
            out_specs=[fixed(part_rows, width)] * MX,
            scratch_shapes=[pltpu.VMEM((planes, 16, width), f32)],
        ),
        out_shape=[jax.ShapeDtypeStruct((part_rows, width), f32)] * MX,
        compiler_params=params(),
        name="forward_modes",
    )(meta, xtab, fields, basis)

    def shard_parts(pieces, count):
        if split == 1:
            return lambda d: pieces[d]
        stacked = jnp.stack(pieces).reshape(MX, count, 2, split, per, width)
        stacked = jnp.moveaxis(stacked, 3, 1).reshape(shards, count * 2 * per, width)
        return lambda d: lax.dynamic_index_in_dim(stacked, (shard + d) % shards, 0, keepdims=False)

    def mode_parts(pieces, count):
        if split == 1:
            return pieces
        stacked = jnp.stack(pieces)[(shard - jnp.arange(shards)) % shards]
        stacked = stacked.reshape(MX, split, count, 2, per, width)
        stacked = jnp.moveaxis(stacked, 1, 3).reshape(MX, count * 16, width)
        return [stacked[(-d) % MX] for d in range(MX)]

    came = rotations(shard_parts(parts, slots), "fsdp", shards)
    own_rows = slots * 2 * per
    coeff, own_spectrum = pl.pallas_call(
        functools.partial(mix_kernel, slots, per, shards),
        in_specs=whole_vmem(shards + 1),
        out_specs=whole_vmem(2),
        out_shape=[jax.ShapeDtypeStruct((own_rows, width), bf16)] * 2,
        scratch_shapes=[pltpu.VMEM((own_rows, width), f32)] * 2,
        compiler_params=params(),
        name="mix_modes",
    )(*came, spectral_w)
    spectrum = mode_parts(rotations(lambda d: own_spectrum, "fsdp", shards), slots)
    coeffs = rotations(lambda d: coeff, "dp", lanes)

    local_rows = width // MX
    eye = np.eye(128, dtype=ml_dtypes.bfloat16)
    ones = np.ones((128, 128), ml_dtypes.bfloat16)
    ones = np.concatenate([ones, -ones], axis=0)
    results = pl.pallas_call(
        functools.partial(backward_kernel, slots, planes, step_planes, 64, float(MODES) ** (-0.5)),
        grid_spec=pltpu.PrefetchScalarGridSpec(
            num_scalar_prefetch=2,
            grid=(slots, blocks),
            in_specs=[field_spec, pl.BlockSpec((1, 1, planes, cells), target_block)]
            + [fixed(part_rows, width)] * MX
            + [
                fixed(width, width),
                fixed(1, width),
                fixed(*inverse.shape),
                fixed(*basis.shape),
                fixed(*eye.shape),
                fixed(*ones.shape),
            ],
            out_specs=[fixed(part_rows + local_rows, width)] * MX,
            scratch_shapes=[
                pltpu.VMEM((2, 256, width), bf16),
                pltpu.VMEM((2, cells // 3, width), f32),
                pltpu.VMEM((2, cells // 3, width), f32),
                pltpu.VMEM((2, cells // 3, 2 * width), bf16),
                pltpu.VMEM((2, cells // 3, width), bf16),
                pltpu.VMEM((width, width), f32),
                pltpu.VMEM((planes, 16, width), f32),
                pltpu.VMEM((planes, 16, cells), bf16),
                pltpu.VMEM((MX, 16, width), f32),
            ],
        ),
        out_shape=[jax.ShapeDtypeStruct((part_rows + local_rows, width), f32)] * MX,
        compiler_params=params(),
        cost_estimate=pl.CostEstimate(
            flops=4 * slots * planes * cells * 256 * 256,
            bytes_accessed=slots * planes * cells * width * 2,
            transcendentals=0,
        ),
        name="backward_modes",
    )(
        meta, xtab, fields, targets, *spectrum, local_w, proj.reshape(1, width), inverse, basis, eye, ones
    )

    if split == 1:
        chunk = lambda d: results[d]
    else:
        backs = shard_parts([r[:part_rows] for r in results], slots)
        local = jnp.concatenate([r[part_rows:] for r in results], axis=0)
        rows = width // shards
        chunk = lambda d: jnp.concatenate(
            [backs(d), lax.dynamic_slice_in_dim(local, (shard + d) % shards * rows, rows, 0)], axis=0
        )
    came = rotations(chunk, "fsdp", shards)
    own_sum = pl.pallas_call(
        functools.partial(sum_kernel, shards),
        in_specs=whole_vmem(shards),
        out_specs=pl.BlockSpec(memory_space=pltpu.VMEM),
        out_shape=jax.ShapeDtypeStruct(came[0].shape, f32),
        compiler_params=params(),
        name="sum_shards",
    )(*came)
    sums = rotations(lambda d: own_sum, "dp", lanes)
    own_local = pl.pallas_call(
        functools.partial(local_sum_kernel, lanes, own_rows),
        in_specs=whole_vmem(lanes),
        out_specs=pl.BlockSpec(memory_space=pltpu.VMEM),
        out_shape=jax.ShapeDtypeStruct((width // shards, width), f32),
        compiler_params=params(),
        name="sum_local",
    )(*sums)
    locals_ = rotations(lambda d: own_local, "fsdp", shards)
    grad_spectral = pl.pallas_call(
        functools.partial(weight_kernel, lanes, slots, per),
        in_specs=whole_vmem(2 * lanes),
        out_specs=pl.BlockSpec(memory_space=pltpu.VMEM),
        out_shape=jax.ShapeDtypeStruct((per, 2, width, width), f32),
        scratch_shapes=[pltpu.VMEM((lanes * own_rows, width), f32)] * 2,
        compiler_params=params(),
        cost_estimate=pl.CostEstimate(
            flops=2 * per * 192 * 128 * 256, bytes_accessed=2 * per * 2 * width * width * 4, transcendentals=0
        ),
        name="weight_grad",
    )(*coeffs, *sums)
    grad_local = pl.pallas_call(
        functools.partial(place_kernel, shards),
        in_specs=[pl.BlockSpec(memory_space=pltpu.SMEM)] + whole_vmem(shards),
        out_specs=pl.BlockSpec(memory_space=pltpu.VMEM),
        out_shape=jax.ShapeDtypeStruct((width, width), f32),
        compiler_params=params(),
        name="place_local",
    )(shard[None], *locals_)
    return (grad_spectral, grad_local)


def solution(mesh):
    return jax.shard_map(
        functools.partial(body, mesh.shape["dp"], mesh.shape["fsdp"]),
        mesh=mesh,
        in_specs=(
            P("dp", None, "fsdp", None, None, None),
            P("dp", None, "fsdp", None),
            P("dp", None),
            P(),
            P("fsdp", None, None, None),
            P(),
            P(),
        ),
        out_specs=(P("fsdp", None, None, None), P()),
        check_vma=False,
    )
```

```python
import functools
import math

import jax
import jax.numpy as jnp
import ml_dtypes
import numpy as np
from jax import lax
from jax.experimental import pallas as pl
from jax.experimental.pallas import tpu as pltpu
from jax.sharding import PartitionSpec as P

MX = 4
MY = 4
MZ = 2
MODES = MX * MY * MZ
VMEM_BYTES = 40 * 1024 * 1024
f32 = jnp.float32
bf16 = jnp.bfloat16
inv_root_two_pi = 0.3989422804014327
half_log2e = 0.7213475204444817
root_half = 0.7071067811865476


def split_bf16(values):
    high = values.astype(ml_dtypes.bfloat16)
    low = (values - high.astype(np.float64)).astype(ml_dtypes.bfloat16)
    return high, low


def angles(mode_ids, length):
    product = np.outer(mode_ids, np.arange(length)) % length
    return product * (2.0 * math.pi / length)


def phase_constants(length):
    y_angle = angles(np.arange(MY) - MY // 2, length)
    z_angle = angles(np.arange(MZ), length)
    rounded = lambda v: v.astype(np.float32).astype(ml_dtypes.bfloat16).astype(np.float64)
    cz, sz = rounded(np.cos(z_angle)), rounded(-np.sin(z_angle))
    cy, sy = np.cos(y_angle), -np.sin(y_angle)
    both = lambda a, b: (a[:, None, :, None] * b[None, :, None, :]).reshape(MY * MZ, length * length)
    fwd = np.concatenate([both(cy, cz) - both(sy, sz), both(sy, cz) + both(cy, sz)], axis=0)
    fwd = np.concatenate(split_bf16(fwd), axis=0)
    cz, sz = np.cos(z_angle), np.sin(z_angle)
    cy, sy = np.cos(y_angle), np.sin(y_angle)
    inv = np.concatenate([both(cy, cz) - both(sy, sz), -(both(sy, cz) + both(cy, sz))], axis=0).T
    high, low = split_bf16(inv)
    pad = np.zeros((length * length, 128 - 4 * high.shape[1]), ml_dtypes.bfloat16)
    inv = np.concatenate([high, low, high, low, pad], axis=1)
    x_angle = angles(np.arange(MX) - MX // 2, length).T
    xtab = np.stack([np.cos(x_angle), np.sin(x_angle)], axis=2).astype(np.float32)
    return fwd, inv, xtab.reshape(-1)


def scalar_places(slots):
    return dict(count=slots, total=slots + 1, shard=slots + 2, first=slots + 3, partner=slots + 4)


def combine_planes(q_ref, xtab_ref, cell0, shard, planes, scale, store):
    for d in range(MX):
        i = lax.rem(shard + d, MX)
        re = jnp.zeros((8, 128), f32)
        im = jnp.zeros((8, 128), f32)
        for a in range(planes):
            at = ((cell0 + a) * MX + i) * 2
            c = xtab_ref[at]
            s = xtab_ref[at + 1]
            q_re = q_ref[a, 0:8, :]
            q_im = q_ref[a, 8:16, :]
            re = re + (q_re * c + q_im * s)
            im = im + (q_im * c - q_re * s)
        store(d, re * scale, im * scale)


def forward_kernel(
    slots, base, sends, planes, step_planes, scale, meta_ref, xtab_ref, f_ref, basis_ref, *rest
):
    if sends:
        t_ref, outs, send_ref, t_out_ref, q_ref = rest[0], rest[1 : MX + 1], *rest[MX + 1 :]
    else:
        given, outs, q_ref = rest[:MX], rest[MX : 2 * MX], rest[2 * MX]
    place = scalar_places(slots)
    g, blk = pl.program_id(0), pl.program_id(1)
    live = base + g < meta_ref[place["count"]]
    row = pl.multiple_of(g * 16, 16)

    if not sends:

        @pl.when((g == 0) & (blk == 0))
        def _():
            rows = given[0].shape[0]
            for d in range(MX):
                outs[d][rows : 2 * rows, :] = given[d][...]

    @pl.when(live)
    def _():
        cells = f_ref.shape[3] * f_ref.shape[4]
        for p in range(step_planes):
            field = f_ref[0, 0, p].reshape(cells, 128)
            part = jnp.dot(basis_ref[...], field, preferred_element_type=f32)
            q_ref[blk * step_planes + p] = part[0:16] + part[16:32]
            if sends:
                send_ref[0, p] = f_ref[0, 0, p]
        if sends:

            @pl.when(blk == 0)
            def _():
                t_out_ref[0] = t_ref[0, 0]

        @pl.when(blk == planes // step_planes - 1)
        def _():
            def store(d, re, im):
                outs[d][pl.ds(row, 8), :] = re
                outs[d][pl.ds(row + 8, 8), :] = im

            combine_planes(
                q_ref, xtab_ref, meta_ref[place["first"]], meta_ref[place["shard"]], planes, scale, store
            )

    @pl.when(jnp.logical_not(live) & (blk == 0))
    def _():
        for out in outs:
            out[pl.ds(row, 16), :] = jnp.zeros((16, 128), f32)


def gelu_parts(pre):
    bell = jnp.exp2(pre * pre * (-half_log2e))
    cdf = 0.5 + 0.5 * lax.erf(pre * root_half)
    return cdf, bell


def shared_live(slots, kept, blocks, count, partner, g, blk):
    return (kept + g < count) & ((g > 0) | ((blk == blocks - 1) & (partner <= 1)))


def backward_kernel(
    slots, own, planes, step_planes, rows_step, scale, meta_ref, xtab_ref, f_ref, t_ref, *rest
):
    specs = rest[:MX]
    w_ref, proj_ref, inv_ref, basis_ref, eye_ref, ones_ref = rest[MX : MX + 6]
    rest = rest[MX + 6 :]
    if not own:
        given, rest = rest[:MX], rest[MX:]
    outs = rest[:MX]
    rhs_ref, pre_ref, slope_ref, both_ref, d_ref, total_ref, q_ref, t16_ref, spec_ref = rest[MX:]
    place = scalar_places(slots)
    kept = slots - 3
    g, blk = pl.program_id(0), pl.program_id(1)
    blocks = planes // step_planes
    count, partner = meta_ref[place["count"]], meta_ref[place["partner"]]
    if own:
        some = g < count
        away = (g >= kept) & shared_live(slots, kept, blocks, count, partner, g - kept, blk)
        live = some & jnp.logical_not(away)
        positions, spec_row, out_row = kept + 1, g * 16, g * 16
        field_at = lambda p: f_ref[0, 0, p].reshape(cells, 128)
        lines_of = lambda: t_ref[0, 0].astype(f32)
    else:
        some = kept + g < partner
        live = shared_live(slots, kept, blocks, partner, count, g, blk)
        positions, spec_row, out_row = 3, (kept + g) * 16, (kept + 1 + g) * 16
        field_at = lambda p: f_ref[0, p].reshape(cells, 128)
        lines_of = lambda: t_ref[0].astype(f32)
    row = pl.multiple_of(out_row, 16)
    shard = meta_ref[place["shard"]]
    cell0 = meta_ref[place["first"]]
    cells = inv_ref.shape[0]
    third = cells // 3
    half = third // 2
    unroll = 2 if step_planes % 2 == 0 else 1

    @pl.when((g == 0) & (blk == 0))
    def _():
        total_ref[...] = jnp.zeros_like(total_ref)
        for n in range(2):
            rhs_ref[n, 0:128, :] = w_ref[...]
            rhs_ref[n, 128:256, :] = jnp.zeros((128, 128), bf16)
        if not own:
            rows = (kept + 1) * 16
            for d in range(MX):
                outs[d][0:rows, :] = given[d][0:rows, :]

    @pl.when(some & (blk == 0))
    def _():
        q_ref[...] = jnp.zeros_like(q_ref)
        lines = lines_of()
        for a in range(planes):
            line = jnp.broadcast_to(lines[a : a + 1, :], (16, cells))
            t16_ref[a] = line.astype(bf16)
        for d in range(MX):
            spec_ref[d] = specs[d][pl.ds(pl.multiple_of(spec_row, 16), 16), :].astype(f32)

    @pl.when(live)
    def _():
        grids = meta_ref[place["total"]].astype(f32)
        proj = proj_ref[...]
        proj_scaled = proj / jnp.full((1, 128), grids, f32)

        def first_rows(a, rhs):
            re = jnp.zeros((8, 128), f32)
            im = jnp.zeros((8, 128), f32)
            for d in range(MX):
                i = lax.rem(shard - d + MX, MX)
                at = ((cell0 + a) * MX + i) * 2
                c = xtab_ref[at]
                s = xtab_ref[at + 1]
                s_re = spec_ref[d, 0:8, :]
                s_im = spec_ref[d, 8:16, :]
                re = re + (s_re * c - s_im * s)
                im = im + (s_re * s + s_im * c)
            first = jnp.concatenate([re, im], axis=0) * scale
            high = first.astype(bf16)
            low = (first - high.astype(f32)).astype(bf16)
            rhs[128:144, :] = high
            rhs[144:160, :] = high
            rhs[160:176, :] = low
            rhs[176:192, :] = low

        def planes_together(n, carry):
            units = [(u, k) for u in range(unroll) for k in range(3)]
            q = [jnp.zeros((32, 128), f32) for _ in range(unroll)]

            def before(s):
                u, k = units[s]
                rhs = rhs_ref.at[u % 2]
                if k == 0:
                    first_rows(blk * step_planes + n * unroll + u, rhs)
                field = field_at(n * unroll + u)
                for r0 in (0, half):
                    part = slice(k * third + r0, k * third + r0 + half)
                    lhs = jnp.concatenate([field[part], inv_ref[part, :]], axis=1)
                    pre_ref[s % 2, r0 : r0 + half, :] = jnp.dot(
                        lhs, rhs[...], preferred_element_type=f32
                    )

            def elementwise(s):
                u, k = units[s]
                a = blk * step_planes + n * unroll + u
                for r0 in range(0, third, rows_step):
                    rows = slice(r0, r0 + rows_step)
                    pre = pre_ref[s % 2, rows, :]
                    cdf, bell = gelu_parts(pre)
                    slope_ref[s % 2, rows, :] = (cdf + pre * bell * inv_root_two_pi) * proj_scaled
                    both_ref[s % 2, rows, 0:128] = (pre * cdf * proj).astype(bf16)
                    for r1 in range(r0, r0 + rows_step, 16):
                        n1 = r1 % 128
                        at = k * third + r1 - n1
                        line = t16_ref[a, :, at : at + 128]
                        both_ref[s % 2, r1 : r1 + 16, 128:256] = line * eye_ref[n1 : n1 + 16, :]

            def after(s):
                for r0 in (0, half):
                    rows = slice(r0, r0 + half)
                    resid = jnp.dot(both_ref[s % 2, rows, :], ones_ref[...], preferred_element_type=f32)
                    d_ref[s % 2, rows, :] = (resid * slope_ref[s % 2, rows, :]).astype(bf16)

            def last(s):
                u, k = units[s]
                field = field_at(n * unroll + u)
                part = slice(k * third, (k + 1) * third)
                lhs = jnp.concatenate([field[part].T, basis_ref[:, part]], axis=0)
                sums = jnp.dot(lhs, d_ref[s % 2], preferred_element_type=f32)
                total_ref[...] += sums[0:128]
                q[u] = q[u] + sums[128:160]
                if k == 2:
                    q_ref[blk * step_planes + n * unroll + u] = q[u][0:16] + q[u][16:32]

            for s in range(len(units) + 3):
                if s >= 3:
                    last(s - 3)
                if 0 <= s - 2 < len(units):
                    after(s - 2)
                if 0 <= s - 1 < len(units):
                    elementwise(s - 1)
                if s < len(units):
                    before(s)
            return carry

        lax.fori_loop(0, step_planes // unroll, planes_together, 0)

    @pl.when(some & (blk == blocks - 1))
    def _():
        def store(d, re, im):
            outs[d][pl.ds(row, 8), :] = re
            outs[d][pl.ds(row + 8, 8), :] = im

        combine_planes(q_ref, xtab_ref, cell0, shard, planes, scale, store)

    @pl.when(jnp.logical_not(some) & (blk == 0))
    def _():
        for out in outs:
            out[pl.ds(row, 16), :] = jnp.zeros((16, 128), f32)

    @pl.when((g == positions - 1) & (blk == blocks - 1))
    def _():
        size = 128 // MX
        for d in range(MX):
            i = lax.rem(shard + d, MX)
            at = pl.multiple_of(i * size, size)
            part = total_ref[pl.ds(at, size), :]
            if not own:
                part = part + given[d][(kept + 1) * 16 : (kept + 1) * 16 + size, :]
            rows = outs[d].shape[0]
            outs[d][rows - size : rows, :] = part


def mix_kernel(slots, per, shards, *refs):
    parts = refs[:shards]
    w_ref, coeff_out, spec_out, c_ref, s_ref = refs[shards:]
    total = parts[0][...]
    for part in parts[1:]:
        total = total + part[...]
    coeff = total.astype(bf16)
    coeff_out[...] = coeff
    c_ref[...] = coeff.astype(f32)
    for m in range(per):
        re_rows = pl.ds(m, slots, stride=2 * per)
        im_rows = pl.ds(per + m, slots, stride=2 * per)
        re = c_ref[re_rows, :].astype(bf16)
        im = c_ref[im_rows, :].astype(bf16)
        weight = w_ref[m].reshape(256, 128)
        s_ref[re_rows, :] = jnp.dot(
            jnp.concatenate([re, -im], axis=1), weight, preferred_element_type=f32
        )
        s_ref[im_rows, :] = jnp.dot(
            jnp.concatenate([im, re], axis=1), weight, preferred_element_type=f32
        )
    spec_out[...] = s_ref[...].astype(bf16)


def sum_kernel(count, *refs):
    total = refs[0][...]
    for part in refs[1:count]:
        total = total + part[...]
    refs[count][...] = total


def local_sum_kernel(count, rows, *refs):
    size = refs[count].shape[0]
    total = refs[0][rows : rows + size, :]
    for part in refs[1:count]:
        total = total + part[rows : rows + size, :]
    refs[count][...] = total


def weight_kernel(lanes, slots, per, lane_ref, *refs):
    coeffs, backs = refs[:lanes], refs[lanes : 2 * lanes]
    out_ref, all_ref, c_ref, b_ref = refs[2 * lanes :]
    each = 2 * per
    kept = slots - 3
    rows = (slots + 1) * each
    for n in range(lanes):
        coeff = coeffs[n][...].astype(f32)
        c_ref[n * rows : n * rows + (kept + 1) * each, :] = coeff[0 : (kept + 1) * each]
        all_ref[n] = coeff[kept * each :]
        b_ref[n * rows : (n + 1) * rows, :] = backs[n][0:rows, :]
    for n in range(lanes):
        source = lax.rem(lane_ref[0] - n + lanes, lanes)
        other = lax.rem(n - 1 + 2 * lax.rem(source, 2) + lanes, lanes)
        c_ref[n * rows + (kept + 1) * each : (n + 1) * rows, :] = all_ref[other]
    slots = slots + 1
    for m in range(per):
        re_rows = pl.ds(m, lanes * slots, stride=2 * per)
        im_rows = pl.ds(per + m, lanes * slots, stride=2 * per)
        c_re = c_ref[re_rows, :].astype(bf16)
        c_im = c_ref[im_rows, :].astype(bf16)
        b_re = b_ref[re_rows, :]
        b_im = b_ref[im_rows, :]
        left = jnp.concatenate([c_re, c_im], axis=0)
        right = jnp.concatenate(
            [jnp.concatenate([b_re, b_im], axis=1), jnp.concatenate([b_im, -b_re], axis=1)], axis=0
        )
        high = right.astype(bf16)
        low = (right - high.astype(f32)).astype(bf16)
        left = jnp.concatenate([left, left], axis=0)
        right = jnp.concatenate([high, low], axis=0)
        grad = lax.dot_general(
            left, right, (((0,), (0,)), ((), ())), preferred_element_type=f32
        )
        out_ref[m, 0] = grad[:, 0:128]
        out_ref[m, 1] = grad[:, 128:256]


def place_kernel(shards, meta_ref, *refs):
    out_ref = refs[shards]
    size = refs[0].shape[0]
    for d in range(shards):
        i = lax.rem(meta_ref[0] - d + shards, shards)
        out_ref[pl.ds(pl.multiple_of(i * size, size), size), :] = refs[d][...]


def whole_vmem(count):
    return [pl.BlockSpec(memory_space=pltpu.VMEM)] * count


def params():
    return pltpu.CompilerParams(vmem_limit_bytes=VMEM_BYTES)


def rotations(value_of, axis, size):
    got = [value_of(0)]
    for d in range(1, size):
        perm = [(s, (s + d) % size) for s in range(size)]
        got.append(lax.ppermute(value_of(d), axis, perm))
    return got


def body(lanes, shards, fields, targets, lists, counts, spectral_w, local_w, proj):
    _, slots, planes, grid_len, _, width = fields.shape
    per = MODES // shards
    split = shards // MX
    cells = grid_len * grid_len
    step_planes = max(n for n in (1, 2, 3, 4) if planes % n == 0)
    blocks = planes // step_planes
    basis, inverse, xtab = phase_constants(grid_len)
    lane = lax.axis_index("dp").astype(jnp.int32)
    shard = lax.axis_index("fsdp").astype(jnp.int32)
    turn = shard if split == 1 else jnp.int32(0)
    meta = jnp.concatenate(
        [
            lists[0],
            counts[lane][None],
            jnp.sum(counts)[None],
            turn[None],
            (shard * planes)[None],
            counts[lane ^ 1][None],
        ]
    ).astype(jnp.int32)
    place = scalar_places(slots)

    kept = slots - 3

    def field_block(base):
        def block(g, blk, meta_ref, xtab_ref):
            count = meta_ref[place["count"]]
            slot = meta_ref[jnp.minimum(base + g, count - 1)]
            return (0, slot, jnp.where(base + g < count, blk, blocks - 1), 0, 0, 0)

        return pl.BlockSpec((1, 1, step_planes, grid_len, grid_len, width), block)

    def target_block(base):
        def block(g, blk, meta_ref, xtab_ref):
            count = meta_ref[place["count"]]
            return (0, meta_ref[jnp.minimum(base + g, count - 1)], 0, 0)

        return pl.BlockSpec((1, 1, planes, cells), block)

    def shared_item(g, blk):
        return jnp.maximum(g * blocks + blk - (blocks - 1), 0)

    def fixed(*shape):
        return pl.BlockSpec(shape, lambda g, blk, meta_ref, xtab_ref: (0,) * len(shape))

    items = 2 * blocks + 1
    shared_fields = pl.BlockSpec(
        (1, step_planes, grid_len, grid_len, width),
        lambda g, blk, meta_ref, xtab_ref: (shared_item(g, blk), 0, 0, 0, 0),
    )
    shared_targets = pl.BlockSpec((1, planes, cells), lambda g, blk, meta_ref, xtab_ref: (g, 0, 0))
    part_rows = slots * 16
    forward_scale = float(grid_len) ** (-1.5)
    *late_parts, sent_fields, sent_targets = pl.pallas_call(
        functools.partial(forward_kernel, slots, kept, True, planes, step_planes, forward_scale),
        grid_spec=pltpu.PrefetchScalarGridSpec(
            num_scalar_prefetch=2,
            grid=(3, blocks),
            in_specs=[field_block(kept), fixed(*basis.shape), target_block(kept)],
            out_specs=[fixed(3 * 16, width)] * MX + [shared_fields, shared_targets],
            scratch_shapes=[pltpu.VMEM((planes, 16, width), f32)],
        ),
        out_shape=[jax.ShapeDtypeStruct((3 * 16, width), f32)] * MX
        + [
            jax.ShapeDtypeStruct((items, step_planes, grid_len, grid_len, width), bf16),
            jax.ShapeDtypeStruct((3, planes, cells), bf16),
        ],
        compiler_params=params(),
        name="forward_shared",
    )(meta, xtab, fields, basis, targets)
    swap = lambda x: lax.ppermute(x, "dp", [(s, s ^ 1) for s in range(lanes)])
    came_fields = swap(sent_fields)
    came_targets = swap(sent_targets)
    parts = pl.pallas_call(
        functools.partial(forward_kernel, slots, 0, False, planes, step_planes, forward_scale),
        grid_spec=pltpu.PrefetchScalarGridSpec(
            num_scalar_prefetch=2,
            grid=(3, blocks),
            in_specs=[field_block(0), fixed(*basis.shape)] + [fixed(3 * 16, width)] * MX,
            out_specs=[fixed(part_rows, width)] * MX,
            scratch_shapes=[pltpu.VMEM((planes, 16, width), f32)],
        ),
        out_shape=[jax.ShapeDtypeStruct((part_rows, width), f32)] * MX,
        compiler_params=params(),
        cost_estimate=pl.CostEstimate(
            flops=3 * planes * cells * 256 * 256,
            bytes_accessed=3 * planes * cells * width * 2,
            transcendentals=0,
        ),
        name="forward_modes",
    )(meta, xtab, fields, basis, *late_parts)

    def shard_parts(pieces, count):
        if split == 1:
            return lambda d: pieces[d]
        stacked = jnp.stack(pieces).reshape(MX, count, 2, split, per, width)
        stacked = jnp.moveaxis(stacked, 3, 1).reshape(shards, count * 2 * per, width)
        return lambda d: lax.dynamic_index_in_dim(stacked, (shard + d) % shards, 0, keepdims=False)

    def mode_parts(pieces, count):
        if split == 1:
            return pieces
        stacked = jnp.stack(pieces)[(shard - jnp.arange(shards)) % shards]
        stacked = stacked.reshape(MX, split, count, 2, per, width)
        stacked = jnp.moveaxis(stacked, 1, 3).reshape(MX, count * 16, width)
        return [stacked[(-d) % MX] for d in range(MX)]

    came = rotations(shard_parts(parts, slots), "fsdp", shards)
    own_rows = slots * 2 * per
    coeff, own_spectrum = pl.pallas_call(
        functools.partial(mix_kernel, slots, per, shards),
        in_specs=whole_vmem(shards + 1),
        out_specs=whole_vmem(2),
        out_shape=[jax.ShapeDtypeStruct((own_rows, width), bf16)] * 2,
        scratch_shapes=[pltpu.VMEM((own_rows, width), f32)] * 2,
        compiler_params=params(),
        name="mix_modes",
    )(*came, spectral_w)
    spectrum = mode_parts(rotations(lambda d: own_spectrum, "fsdp", shards), slots)
    coeffs = rotations(lambda d: coeff, "dp", lanes)

    local_rows = width // MX
    eye = np.eye(128, dtype=ml_dtypes.bfloat16)
    ones = np.ones((128, 128), ml_dtypes.bfloat16)
    ones = np.concatenate([ones, -ones], axis=0)

    def own_block(g, blk, meta_ref, xtab_ref):
        count, partner = meta_ref[place["count"]], meta_ref[place["partner"]]
        slot = meta_ref[jnp.minimum(g, count - 1)]
        away = (g >= kept) & shared_live(slots, kept, blocks, count, partner, g - kept, blk)
        blk = jnp.where(away, max(blocks - 2, 0), blk)
        return (0, slot, jnp.where(g < count, blk, blocks - 1), 0, 0, 0)

    def backward(own, fields_, targets_, spectrum_, given):
        positions = kept + 1 if own else 3
        rows = (kept + 1 if own else slots + 1) * 16 + local_rows
        own_fields = pl.BlockSpec((1, 1, step_planes, grid_len, grid_len, width), own_block)
        return pl.pallas_call(
            functools.partial(
                backward_kernel, slots, own, planes, step_planes, 64, float(MODES) ** (-0.5)
            ),
            grid_spec=pltpu.PrefetchScalarGridSpec(
                num_scalar_prefetch=2,
                grid=(positions, blocks),
                in_specs=([own_fields, target_block(0)] if own else [shared_fields, shared_targets])
                + [fixed(part_rows, width)] * MX
                + [
                    fixed(width, width),
                    fixed(1, width),
                    fixed(*inverse.shape),
                    fixed(*basis.shape),
                    fixed(*eye.shape),
                    fixed(*ones.shape),
                ]
                + [fixed(*g.shape) for g in given],
                out_specs=[fixed(rows, width)] * MX,
                scratch_shapes=[
                    pltpu.VMEM((2, 256, width), bf16),
                    pltpu.VMEM((2, cells // 3, width), f32),
                    pltpu.VMEM((2, cells // 3, width), f32),
                    pltpu.VMEM((2, cells // 3, 2 * width), bf16),
                    pltpu.VMEM((2, cells // 3, width), bf16),
                    pltpu.VMEM((width, width), f32),
                    pltpu.VMEM((planes, 16, width), f32),
                    pltpu.VMEM((planes, 16, cells), bf16),
                    pltpu.VMEM((MX, 16, width), f32),
                ],
            ),
            out_shape=[jax.ShapeDtypeStruct((rows, width), f32)] * MX,
            compiler_params=params(),
            cost_estimate=pl.CostEstimate(
                flops=4 * positions * planes * cells * 256 * 256,
                bytes_accessed=positions * planes * cells * width * 2,
                transcendentals=0,
            ),
            name="backward_own" if own else "backward_shared",
        )(
            meta, xtab, fields_, targets_, *spectrum_, local_w, proj.reshape(1, width),
            inverse, basis, eye, ones, *given,
        )

    came_spectrum = [swap(piece) for piece in spectrum]
    own_results = backward(True, fields, targets, spectrum, [])
    results = backward(False, came_fields, came_targets, came_spectrum, own_results)
    places = slots + 1
    part_rows = places * 16
    place_rows = places * 2 * per

    if split == 1:
        chunk = lambda d: results[d]
    else:
        backs = shard_parts([r[:part_rows] for r in results], places)
        local = jnp.concatenate([r[part_rows:] for r in results], axis=0)
        rows = width // shards
        chunk = lambda d: jnp.concatenate(
            [backs(d), lax.dynamic_slice_in_dim(local, (shard + d) % shards * rows, rows, 0)], axis=0
        )
    came = rotations(chunk, "fsdp", shards)
    own_sum = pl.pallas_call(
        functools.partial(sum_kernel, shards),
        in_specs=whole_vmem(shards),
        out_specs=pl.BlockSpec(memory_space=pltpu.VMEM),
        out_shape=jax.ShapeDtypeStruct(came[0].shape, f32),
        compiler_params=params(),
        name="sum_shards",
    )(*came)
    sums = rotations(lambda d: own_sum, "dp", lanes)
    own_local = pl.pallas_call(
        functools.partial(local_sum_kernel, lanes, place_rows),
        in_specs=whole_vmem(lanes),
        out_specs=pl.BlockSpec(memory_space=pltpu.VMEM),
        out_shape=jax.ShapeDtypeStruct((width // shards, width), f32),
        compiler_params=params(),
        name="sum_local",
    )(*sums)
    locals_ = rotations(lambda d: own_local, "fsdp", shards)
    grad_spectral = pl.pallas_call(
        functools.partial(weight_kernel, lanes, slots, per),
        in_specs=[pl.BlockSpec(memory_space=pltpu.SMEM)] + whole_vmem(2 * lanes),
        out_specs=pl.BlockSpec(memory_space=pltpu.VMEM),
        out_shape=jax.ShapeDtypeStruct((per, 2, width, width), f32),
        scratch_shapes=[pltpu.VMEM((lanes, 3 * 2 * per, width), f32)]
        + [pltpu.VMEM((lanes * place_rows, width), f32)] * 2,
        compiler_params=params(),
        cost_estimate=pl.CostEstimate(
            flops=2 * per * 256 * 128 * 256, bytes_accessed=2 * per * 2 * width * width * 4, transcendentals=0
        ),
        name="weight_grad",
    )(lane[None], *coeffs, *sums)
    grad_local = pl.pallas_call(
        functools.partial(place_kernel, shards),
        in_specs=[pl.BlockSpec(memory_space=pltpu.SMEM)] + whole_vmem(shards),
        out_specs=pl.BlockSpec(memory_space=pltpu.VMEM),
        out_shape=jax.ShapeDtypeStruct((width, width), f32),
        compiler_params=params(),
        name="place_local",
    )(shard[None], *locals_)
    return (grad_spectral, grad_local)


def solution(mesh):
    return jax.shard_map(
        functools.partial(body, mesh.shape["dp"], mesh.shape["fsdp"]),
        mesh=mesh,
        in_specs=(
            P("dp", None, "fsdp", None, None, None),
            P("dp", None, "fsdp", None),
            P("dp", None),
            P(),
            P("fsdp", None, None, None),
            P(),
            P(),
        ),
        out_specs=(P("fsdp", None, None, None), P()),
        check_vma=False,
    )
```

```python
import functools
import math

import jax
import jax.numpy as jnp
import ml_dtypes
import numpy as np
from jax import lax
from jax.experimental import pallas as pl
from jax.experimental.pallas import tpu as pltpu
from jax.sharding import PartitionSpec as P

MX = 4
MY = 4
MZ = 2
MODES = MX * MY * MZ
VMEM_BYTES = 40 * 1024 * 1024
LARGE_VMEM_BYTES = 56 * 1024 * 1024
f32 = jnp.float32
bf16 = jnp.bfloat16
inv_root_two_pi = 0.3989422804014327
half_log2e = 0.7213475204444817
root_half = 0.7071067811865476


def split_bf16(values):
    high = values.astype(ml_dtypes.bfloat16)
    low = (values - high.astype(np.float64)).astype(ml_dtypes.bfloat16)
    return high, low


def angles(mode_ids, length):
    product = np.outer(mode_ids, np.arange(length)) % length
    return product * (2.0 * math.pi / length)


def phase_constants(length):
    y_angle = angles(np.arange(MY) - MY // 2, length)
    z_angle = angles(np.arange(MZ), length)
    rounded = lambda v: v.astype(np.float32).astype(ml_dtypes.bfloat16).astype(np.float64)
    cz, sz = rounded(np.cos(z_angle)), rounded(-np.sin(z_angle))
    cy, sy = np.cos(y_angle), -np.sin(y_angle)
    both = lambda a, b: (a[:, None, :, None] * b[None, :, None, :]).reshape(MY * MZ, length * length)
    fwd = np.concatenate([both(cy, cz) - both(sy, sz), both(sy, cz) + both(cy, sz)], axis=0)
    fwd = np.concatenate(split_bf16(fwd), axis=0)
    cz, sz = np.cos(z_angle), np.sin(z_angle)
    cy, sy = np.cos(y_angle), np.sin(y_angle)
    inv = np.concatenate([both(cy, cz) - both(sy, sz), -(both(sy, cz) + both(cy, sz))], axis=0).T
    high, low = split_bf16(inv)
    pad = np.zeros((length * length, 128 - 4 * high.shape[1]), ml_dtypes.bfloat16)
    inv = np.concatenate([high, low, high, low, pad], axis=1)
    x_angle = angles(np.arange(MX) - MX // 2, length).T
    xtab = np.stack([np.cos(x_angle), np.sin(x_angle)], axis=2).astype(np.float32)
    return fwd, inv, xtab.reshape(-1)


def scalar_places(slots):
    return dict(count=slots, total=slots + 1, shard=slots + 2, first=slots + 3, partner=slots + 4)


def combine_planes(q_ref, xtab_ref, cell0, shard, planes, scale, store):
    for d in range(MX):
        i = lax.rem(shard + d, MX)
        re = jnp.zeros((8, 128), f32)
        im = jnp.zeros((8, 128), f32)
        for a in range(planes):
            at = ((cell0 + a) * MX + i) * 2
            c = xtab_ref[at]
            s = xtab_ref[at + 1]
            q_re = q_ref[a, 0:8, :]
            q_im = q_ref[a, 8:16, :]
            re = re + (q_re * c + q_im * s)
            im = im + (q_im * c - q_re * s)
        store(d, re * scale, im * scale)


def forward_kernel(
    slots, base, sends, planes, step_planes, scale, meta_ref, xtab_ref, f_ref, basis_ref, *rest
):
    if sends:
        t_ref, outs, send_ref, t_out_ref, q_ref = rest[0], rest[1 : MX + 1], *rest[MX + 1 :]
    else:
        given, outs, q_ref = rest[:MX], rest[MX : 2 * MX], rest[2 * MX]
    place = scalar_places(slots)
    g, blk = pl.program_id(0), pl.program_id(1)
    live = base + g < meta_ref[place["count"]]
    row = pl.multiple_of(g * 16, 16)

    if not sends:

        @pl.when((g == 0) & (blk == 0))
        def _():
            rows = given[0].shape[0]
            for d in range(MX):
                outs[d][rows : 2 * rows, :] = given[d][...]

    @pl.when(live)
    def _():
        cells = f_ref.shape[3] * f_ref.shape[4]
        for p in range(step_planes):
            field = f_ref[0, 0, p].reshape(cells, 128)
            part = jnp.dot(basis_ref[...], field, preferred_element_type=f32)
            q_ref[blk * step_planes + p] = part[0:16] + part[16:32]
            if sends:
                send_ref[0, p] = f_ref[0, 0, p]
        if sends:

            @pl.when(blk == 0)
            def _():
                t_out_ref[0] = t_ref[0, 0]

        @pl.when(blk == planes // step_planes - 1)
        def _():
            def store(d, re, im):
                outs[d][pl.ds(row, 8), :] = re
                outs[d][pl.ds(row + 8, 8), :] = im

            combine_planes(
                q_ref, xtab_ref, meta_ref[place["first"]], meta_ref[place["shard"]], planes, scale, store
            )

    @pl.when(jnp.logical_not(live) & (blk == 0))
    def _():
        for out in outs:
            out[pl.ds(row, 16), :] = jnp.zeros((16, 128), f32)


def gelu_parts(pre):
    bell = jnp.exp2(pre * pre * (-half_log2e))
    cdf = 0.5 + 0.5 * lax.erf(pre * root_half)
    return cdf, bell


def shared_live(slots, kept, blocks, count, partner, g, blk):
    return (kept + g < count) & ((g > 0) | ((blk == blocks - 1) & (partner <= 1)))


def backward_kernel(
    slots, own, planes, step_planes, rows_step, scale, meta_ref, xtab_ref, f_ref, t_ref, *rest
):
    specs = rest[:MX]
    w_ref, proj_ref, inv_ref, basis_ref, eye_ref, ones_ref = rest[MX : MX + 6]
    rest = rest[MX + 6 :]
    if not own:
        given, rest = rest[:MX], rest[MX:]
    outs = rest[:MX]
    rhs_ref, pre_ref, slope_ref, both_ref, d_ref, total_ref, q_ref, t16_ref, spec_ref, field_ref, line_ref = rest[MX:]
    place = scalar_places(slots)
    kept = slots - 3
    g, blk = pl.program_id(0), pl.program_id(1)
    blocks = planes // step_planes
    count, partner = meta_ref[place["count"]], meta_ref[place["partner"]]
    if own:
        some = g < count
        away = (g >= kept) & shared_live(slots, kept, blocks, count, partner, g - kept, blk)
        live = some & jnp.logical_not(away)
        positions, spec_row, out_row = kept + 1, g * 16, g * 16
        plane_of = lambda p: f_ref[0, 0, p].reshape(cells, 128)
        lines_of = lambda: t_ref[0, 0].astype(f32)
    else:
        some = kept + g < partner
        live = shared_live(slots, kept, blocks, partner, count, g, blk)
        positions, spec_row, out_row = 3, (kept + g) * 16, (kept + 1 + g) * 16
        plane_of = lambda p: f_ref[0, p].reshape(cells, 128)
        lines_of = lambda: t_ref[0].astype(f32)
    row = pl.multiple_of(out_row, 16)
    shard = meta_ref[place["shard"]]
    cell0 = meta_ref[place["first"]]
    cells = inv_ref.shape[0]
    third = cells // 3
    half = third // 2
    unroll = step_planes

    @pl.when((g == 0) & (blk == 0))
    def _():
        total_ref[...] = jnp.zeros_like(total_ref)
        for n in range(2):
            rhs_ref[n, 0:128, :] = w_ref[...]
            rhs_ref[n, 128:256, :] = jnp.zeros((128, 128), bf16)
        if not own:
            rows = (kept + 1) * 16
            for d in range(MX):
                outs[d][0:rows, :] = given[d][0:rows, :]

    @pl.when(some & (blk == 0))
    def _():
        q_ref[...] = jnp.zeros_like(q_ref)
        lines = lines_of()
        for a in range(planes):
            line = jnp.broadcast_to(lines[a : a + 1, :], (16, cells))
            t16_ref[a] = line.astype(bf16)
        for d in range(MX):
            spec_ref[d] = specs[d][pl.ds(pl.multiple_of(spec_row, 16), 16), :].astype(f32)

    @pl.when(live)
    def _():
        grids = meta_ref[place["total"]].astype(f32)
        proj = proj_ref[...]
        proj_scaled = proj / jnp.full((1, 128), grids, f32)

        def first_rows(a, rhs):
            re = jnp.zeros((8, 128), f32)
            im = jnp.zeros((8, 128), f32)
            for d in range(MX):
                i = lax.rem(shard - d + MX, MX)
                at = ((cell0 + a) * MX + i) * 2
                c = xtab_ref[at]
                s = xtab_ref[at + 1]
                s_re = spec_ref[d, 0:8, :]
                s_im = spec_ref[d, 8:16, :]
                re = re + (s_re * c - s_im * s)
                im = im + (s_re * s + s_im * c)
            first = jnp.concatenate([re, im], axis=0) * scale
            high = first.astype(bf16)
            low = (first - high.astype(f32)).astype(bf16)
            rhs[128:144, :] = high
            rhs[144:160, :] = high
            rhs[160:176, :] = low
            rhs[176:192, :] = low

        def planes_together(n, carry):
            units = [(u, k) for u in range(unroll) for k in range(3)]
            q = [jnp.zeros((32, 128), f32) for _ in range(unroll)]
            for u in range(unroll):
                field_ref[u] = plane_of(n * unroll + u)
                line_ref[u] = t16_ref[blk * step_planes + n * unroll + u]

            def before(s):
                u, k = units[s]
                rhs = rhs_ref.at[u % 2]
                if k == 0:
                    first_rows(blk * step_planes + n * unroll + u, rhs)
                field = field_ref.at[u]
                for r0 in (0, half):
                    part = slice(k * third + r0, k * third + r0 + half)
                    lhs = jnp.concatenate([field[part, :], inv_ref[part, :]], axis=1)
                    pre_ref[s % 2, r0 : r0 + half, :] = jnp.dot(
                        lhs, rhs[...], preferred_element_type=f32
                    )

            def elementwise(s):
                u, k = units[s]
                for r0 in range(0, third, rows_step):
                    rows = slice(r0, r0 + rows_step)
                    pre = pre_ref[s % 2, rows, :]
                    cdf, bell = gelu_parts(pre)
                    slope_ref[s % 2, rows, :] = (cdf + pre * bell * inv_root_two_pi) * proj_scaled
                    both_ref[s % 2, rows, 0:128] = (pre * cdf * proj).astype(bf16)
                    for r1 in range(r0, r0 + rows_step, 16):
                        n1 = r1 % 128
                        at = k * third + r1 - n1
                        line = line_ref[u, :, at : at + 128]
                        both_ref[s % 2, r1 : r1 + 16, 128:256] = line * eye_ref[n1 : n1 + 16, :]

            def after(s):
                for r0 in (0, half):
                    rows = slice(r0, r0 + half)
                    resid = jnp.dot(both_ref[s % 2, rows, :], ones_ref[...], preferred_element_type=f32)
                    d_ref[s % 2, rows, :] = (resid * slope_ref[s % 2, rows, :]).astype(bf16)

            def last(s):
                u, k = units[s]
                part = slice(k * third, (k + 1) * third)
                lhs = jnp.concatenate([field_ref[u, part, :].T, basis_ref[:, part]], axis=0)
                sums = jnp.dot(lhs, d_ref[s % 2], preferred_element_type=f32)
                total_ref[...] += sums[0:128]
                q[u] = q[u] + sums[128:160]
                if k == 2:
                    q_ref[blk * step_planes + n * unroll + u] = q[u][0:16] + q[u][16:32]

            for s in range(len(units) + 3):
                if s < len(units):
                    before(s)
                if 0 <= s - 2 < len(units):
                    after(s - 2)
                if s >= 3:
                    last(s - 3)
                if 0 <= s - 1 < len(units):
                    elementwise(s - 1)
            return carry

        lax.fori_loop(0, step_planes // unroll, planes_together, 0)

    @pl.when(some & (blk == blocks - 1))
    def _():
        def store(d, re, im):
            outs[d][pl.ds(row, 8), :] = re
            outs[d][pl.ds(row + 8, 8), :] = im

        combine_planes(q_ref, xtab_ref, cell0, shard, planes, scale, store)

    @pl.when(jnp.logical_not(some) & (blk == 0))
    def _():
        for out in outs:
            out[pl.ds(row, 16), :] = jnp.zeros((16, 128), f32)

    @pl.when((g == positions - 1) & (blk == blocks - 1))
    def _():
        size = 128 // MX
        for d in range(MX):
            i = lax.rem(shard + d, MX)
            at = pl.multiple_of(i * size, size)
            part = total_ref[pl.ds(at, size), :]
            if not own:
                part = part + given[d][(kept + 1) * 16 : (kept + 1) * 16 + size, :]
            rows = outs[d].shape[0]
            outs[d][rows - size : rows, :] = part


def mix_kernel(slots, per, shards, *refs):
    parts = refs[:shards]
    w_ref, coeff_out, spec_out, c_ref, s_ref = refs[shards:]
    total = parts[0][...]
    for part in parts[1:]:
        total = total + part[...]
    coeff = total.astype(bf16)
    coeff_out[...] = coeff
    c_ref[...] = coeff.astype(f32)
    for m in range(per):
        re_rows = pl.ds(m, slots, stride=2 * per)
        im_rows = pl.ds(per + m, slots, stride=2 * per)
        re = c_ref[re_rows, :].astype(bf16)
        im = c_ref[im_rows, :].astype(bf16)
        weight = w_ref[m].reshape(256, 128)
        s_ref[re_rows, :] = jnp.dot(
            jnp.concatenate([re, -im], axis=1), weight, preferred_element_type=f32
        )
        s_ref[im_rows, :] = jnp.dot(
            jnp.concatenate([im, re], axis=1), weight, preferred_element_type=f32
        )
    spec_out[...] = s_ref[...].astype(bf16)


def sum_kernel(count, *refs):
    total = refs[0][...]
    for part in refs[1:count]:
        total = total + part[...]
    refs[count][...] = total


def local_sum_kernel(count, rows, *refs):
    size = refs[count].shape[0]
    total = refs[0][rows : rows + size, :]
    for part in refs[1:count]:
        total = total + part[rows : rows + size, :]
    refs[count][...] = total


def weight_kernel(lanes, slots, per, lane_ref, *refs):
    coeffs, backs = refs[:lanes], refs[lanes : 2 * lanes]
    out_ref, all_ref, c_ref, b_ref = refs[2 * lanes :]
    each = 2 * per
    kept = slots - 3
    rows = (slots + 1) * each
    for n in range(lanes):
        coeff = coeffs[n][...].astype(f32)
        c_ref[n * rows : n * rows + (kept + 1) * each, :] = coeff[0 : (kept + 1) * each]
        all_ref[n] = coeff[kept * each :]
        b_ref[n * rows : (n + 1) * rows, :] = backs[n][0:rows, :]
    for n in range(lanes):
        source = lax.rem(lane_ref[0] - n + lanes, lanes)
        other = lax.rem(n - 1 + 2 * lax.rem(source, 2) + lanes, lanes)
        c_ref[n * rows + (kept + 1) * each : (n + 1) * rows, :] = all_ref[other]
    slots = slots + 1
    for m in range(per):
        re_rows = pl.ds(m, lanes * slots, stride=2 * per)
        im_rows = pl.ds(per + m, lanes * slots, stride=2 * per)
        c_re = c_ref[re_rows, :].astype(bf16)
        c_im = c_ref[im_rows, :].astype(bf16)
        b_re = b_ref[re_rows, :]
        b_im = b_ref[im_rows, :]
        left = jnp.concatenate([c_re, c_im], axis=0)
        right = jnp.concatenate(
            [jnp.concatenate([b_re, b_im], axis=1), jnp.concatenate([b_im, -b_re], axis=1)], axis=0
        )
        high = right.astype(bf16)
        low = (right - high.astype(f32)).astype(bf16)
        left = jnp.concatenate([left, left], axis=0)
        right = jnp.concatenate([high, low], axis=0)
        grad = lax.dot_general(
            left, right, (((0,), (0,)), ((), ())), preferred_element_type=f32
        )
        out_ref[m, 0] = grad[:, 0:128]
        out_ref[m, 1] = grad[:, 128:256]


def place_kernel(shards, meta_ref, *refs):
    out_ref = refs[shards]
    size = refs[0].shape[0]
    for d in range(shards):
        i = lax.rem(meta_ref[0] - d + shards, shards)
        out_ref[pl.ds(pl.multiple_of(i * size, size), size), :] = refs[d][...]


def whole_vmem(count):
    return [pl.BlockSpec(memory_space=pltpu.VMEM)] * count


def params(limit=VMEM_BYTES):
    return pltpu.CompilerParams(vmem_limit_bytes=limit)


def rotations(value_of, axis, size):
    got = [value_of(0)]
    for d in range(1, size):
        perm = [(s, (s + d) % size) for s in range(size)]
        got.append(lax.ppermute(value_of(d), axis, perm))
    return got


def body(lanes, shards, fields, targets, lists, counts, spectral_w, local_w, proj):
    _, slots, planes, grid_len, _, width = fields.shape
    per = MODES // shards
    split = shards // MX
    cells = grid_len * grid_len
    step_planes = max(n for n in (1, 2, 3, 4) if planes % n == 0)
    blocks = planes // step_planes
    basis, inverse, xtab = phase_constants(grid_len)
    lane = lax.axis_index("dp").astype(jnp.int32)
    shard = lax.axis_index("fsdp").astype(jnp.int32)
    turn = shard if split == 1 else jnp.int32(0)
    meta = jnp.concatenate(
        [
            lists[0],
            counts[lane][None],
            jnp.sum(counts)[None],
            turn[None],
            (shard * planes)[None],
            counts[lane ^ 1][None],
        ]
    ).astype(jnp.int32)
    place = scalar_places(slots)

    kept = slots - 3

    def field_block(base):
        def block(g, blk, meta_ref, xtab_ref):
            count = meta_ref[place["count"]]
            slot = meta_ref[jnp.minimum(base + g, count - 1)]
            return (0, slot, jnp.where(base + g < count, blk, blocks - 1), 0, 0, 0)

        return pl.BlockSpec((1, 1, step_planes, grid_len, grid_len, width), block)

    def target_block(base):
        def block(g, blk, meta_ref, xtab_ref):
            count = meta_ref[place["count"]]
            return (0, meta_ref[jnp.minimum(base + g, count - 1)], 0, 0)

        return pl.BlockSpec((1, 1, planes, cells), block)

    def shared_item(g, blk):
        return jnp.maximum(g * blocks + blk - (blocks - 1), 0)

    def fixed(*shape):
        return pl.BlockSpec(shape, lambda g, blk, meta_ref, xtab_ref: (0,) * len(shape))

    items = 2 * blocks + 1
    shared_fields = pl.BlockSpec(
        (1, step_planes, grid_len, grid_len, width),
        lambda g, blk, meta_ref, xtab_ref: (shared_item(g, blk), 0, 0, 0, 0),
    )
    shared_targets = pl.BlockSpec((1, planes, cells), lambda g, blk, meta_ref, xtab_ref: (g, 0, 0))
    part_rows = slots * 16
    forward_scale = float(grid_len) ** (-1.5)
    *late_parts, sent_fields, sent_targets = pl.pallas_call(
        functools.partial(forward_kernel, slots, kept, True, planes, step_planes, forward_scale),
        grid_spec=pltpu.PrefetchScalarGridSpec(
            num_scalar_prefetch=2,
            grid=(3, blocks),
            in_specs=[field_block(kept), fixed(*basis.shape), target_block(kept)],
            out_specs=[fixed(3 * 16, width)] * MX + [shared_fields, shared_targets],
            scratch_shapes=[pltpu.VMEM((planes, 16, width), f32)],
        ),
        out_shape=[jax.ShapeDtypeStruct((3 * 16, width), f32)] * MX
        + [
            jax.ShapeDtypeStruct((items, step_planes, grid_len, grid_len, width), bf16),
            jax.ShapeDtypeStruct((3, planes, cells), bf16),
        ],
        compiler_params=params(),
        name="forward_shared",
    )(meta, xtab, fields, basis, targets)
    swap = lambda x: lax.ppermute(x, "dp", [(s, s ^ 1) for s in range(lanes)])
    came_fields = swap(sent_fields)
    came_targets = swap(sent_targets)
    parts = pl.pallas_call(
        functools.partial(forward_kernel, slots, 0, False, planes, step_planes, forward_scale),
        grid_spec=pltpu.PrefetchScalarGridSpec(
            num_scalar_prefetch=2,
            grid=(3, blocks),
            in_specs=[field_block(0), fixed(*basis.shape)] + [fixed(3 * 16, width)] * MX,
            out_specs=[fixed(part_rows, width)] * MX,
            scratch_shapes=[pltpu.VMEM((planes, 16, width), f32)],
        ),
        out_shape=[jax.ShapeDtypeStruct((part_rows, width), f32)] * MX,
        compiler_params=params(),
        cost_estimate=pl.CostEstimate(
            flops=3 * planes * cells * 256 * 256,
            bytes_accessed=3 * planes * cells * width * 2,
            transcendentals=0,
        ),
        name="forward_modes",
    )(meta, xtab, fields, basis, *late_parts)

    def shard_parts(pieces, count):
        if split == 1:
            return lambda d: pieces[d]
        stacked = jnp.stack(pieces).reshape(MX, count, 2, split, per, width)
        stacked = jnp.moveaxis(stacked, 3, 1).reshape(shards, count * 2 * per, width)
        return lambda d: lax.dynamic_index_in_dim(stacked, (shard + d) % shards, 0, keepdims=False)

    def mode_parts(pieces, count):
        if split == 1:
            return pieces
        stacked = jnp.stack(pieces)[(shard - jnp.arange(shards)) % shards]
        stacked = stacked.reshape(MX, split, count, 2, per, width)
        stacked = jnp.moveaxis(stacked, 1, 3).reshape(MX, count * 16, width)
        return [stacked[(-d) % MX] for d in range(MX)]

    came = rotations(shard_parts(parts, slots), "fsdp", shards)
    own_rows = slots * 2 * per
    coeff, own_spectrum = pl.pallas_call(
        functools.partial(mix_kernel, slots, per, shards),
        in_specs=whole_vmem(shards + 1),
        out_specs=whole_vmem(2),
        out_shape=[jax.ShapeDtypeStruct((own_rows, width), bf16)] * 2,
        scratch_shapes=[pltpu.VMEM((own_rows, width), f32)] * 2,
        compiler_params=params(),
        name="mix_modes",
    )(*came, spectral_w)
    spectrum = mode_parts(rotations(lambda d: own_spectrum, "fsdp", shards), slots)
    coeffs = rotations(lambda d: coeff, "dp", lanes)

    local_rows = width // MX
    eye = np.eye(128, dtype=ml_dtypes.bfloat16)
    ones = np.ones((128, 128), ml_dtypes.bfloat16)
    ones = np.concatenate([ones, -ones], axis=0)

    def own_block(g, blk, meta_ref, xtab_ref):
        count, partner = meta_ref[place["count"]], meta_ref[place["partner"]]
        slot = meta_ref[jnp.minimum(g, count - 1)]
        away = (g >= kept) & shared_live(slots, kept, blocks, count, partner, g - kept, blk)
        blk = jnp.where(away, max(blocks - 2, 0), blk)
        return (0, slot, jnp.where(g < count, blk, blocks - 1), 0, 0, 0)

    def came_item(g, blk, meta_ref):
        some = kept < meta_ref[place["partner"]]
        return jnp.where(some, shared_item(g, blk), 0), jnp.where(some, g, 0)

    came_block = pl.BlockSpec(
        (1, step_planes, grid_len, grid_len, width),
        lambda g, blk, meta_ref, xtab_ref: (came_item(g, blk, meta_ref)[0], 0, 0, 0, 0),
    )
    came_lines = pl.BlockSpec(
        (1, planes, cells), lambda g, blk, meta_ref, xtab_ref: (came_item(g, blk, meta_ref)[1], 0, 0)
    )

    def backward(own, fields_, targets_, spectrum_, given):
        positions = kept + 1 if own else 3
        rows = (kept + 1 if own else slots + 1) * 16 + local_rows
        own_fields = pl.BlockSpec((1, 1, step_planes, grid_len, grid_len, width), own_block)
        return pl.pallas_call(
            functools.partial(
                backward_kernel, slots, own, planes, step_planes, 64, float(MODES) ** (-0.5)
            ),
            grid_spec=pltpu.PrefetchScalarGridSpec(
                num_scalar_prefetch=2,
                grid=(positions, blocks),
                in_specs=([own_fields, target_block(0)] if own else [came_block, came_lines])
                + [fixed(part_rows, width)] * MX
                + [
                    fixed(width, width),
                    fixed(1, width),
                    fixed(*inverse.shape),
                    fixed(*basis.shape),
                    fixed(*eye.shape),
                    fixed(*ones.shape),
                ]
                + [fixed(*g.shape) for g in given],
                out_specs=[fixed(rows, width)] * MX,
                scratch_shapes=[
                    pltpu.VMEM((2, 256, width), bf16),
                    pltpu.VMEM((2, cells // 3, width), f32),
                    pltpu.VMEM((2, cells // 3, width), f32),
                    pltpu.VMEM((2, cells // 3, 2 * width), bf16),
                    pltpu.VMEM((2, cells // 3, width), bf16),
                    pltpu.VMEM((width, width), f32),
                    pltpu.VMEM((planes, 16, width), f32),
                    pltpu.VMEM((planes, 16, cells), bf16),
                    pltpu.VMEM((MX, 16, width), f32),
                    pltpu.VMEM((step_planes, cells, width), bf16),
                    pltpu.VMEM((step_planes, 16, cells), bf16),
                ],
            ),
            out_shape=[jax.ShapeDtypeStruct((rows, width), f32)] * MX,
            compiler_params=params(LARGE_VMEM_BYTES),
            cost_estimate=pl.CostEstimate(
                flops=4 * positions * planes * cells * 256 * 256,
                bytes_accessed=positions * planes * cells * width * 2,
                transcendentals=0,
            ),
            name="backward_own" if own else "backward_shared",
        )(
            meta, xtab, fields_, targets_, *spectrum_, local_w, proj.reshape(1, width),
            inverse, basis, eye, ones, *given,
        )

    came_spectrum = [swap(piece) for piece in spectrum]
    own_results = backward(True, fields, targets, spectrum, [])
    results = backward(False, came_fields, came_targets, came_spectrum, own_results)
    places = slots + 1
    part_rows = places * 16
    place_rows = places * 2 * per

    if split == 1:
        chunk = lambda d: results[d]
    else:
        backs = shard_parts([r[:part_rows] for r in results], places)
        local = jnp.concatenate([r[part_rows:] for r in results], axis=0)
        rows = width // shards
        chunk = lambda d: jnp.concatenate(
            [backs(d), lax.dynamic_slice_in_dim(local, (shard + d) % shards * rows, rows, 0)], axis=0
        )
    came = rotations(chunk, "fsdp", shards)
    own_sum = pl.pallas_call(
        functools.partial(sum_kernel, shards),
        in_specs=whole_vmem(shards),
        out_specs=pl.BlockSpec(memory_space=pltpu.VMEM),
        out_shape=jax.ShapeDtypeStruct(came[0].shape, f32),
        compiler_params=params(),
        name="sum_shards",
    )(*came)
    sums = rotations(lambda d: own_sum, "dp", lanes)
    own_local = pl.pallas_call(
        functools.partial(local_sum_kernel, lanes, place_rows),
        in_specs=whole_vmem(lanes),
        out_specs=pl.BlockSpec(memory_space=pltpu.VMEM),
        out_shape=jax.ShapeDtypeStruct((width // shards, width), f32),
        compiler_params=params(),
        name="sum_local",
    )(*sums)
    locals_ = rotations(lambda d: own_local, "fsdp", shards)
    grad_spectral = pl.pallas_call(
        functools.partial(weight_kernel, lanes, slots, per),
        in_specs=[pl.BlockSpec(memory_space=pltpu.SMEM)] + whole_vmem(2 * lanes),
        out_specs=pl.BlockSpec(memory_space=pltpu.VMEM),
        out_shape=jax.ShapeDtypeStruct((per, 2, width, width), f32),
        scratch_shapes=[pltpu.VMEM((lanes, 3 * 2 * per, width), f32)]
        + [pltpu.VMEM((lanes * place_rows, width), f32)] * 2,
        compiler_params=params(),
        cost_estimate=pl.CostEstimate(
            flops=2 * per * 256 * 128 * 256, bytes_accessed=2 * per * 2 * width * width * 4, transcendentals=0
        ),
        name="weight_grad",
    )(lane[None], *coeffs, *sums)
    grad_local = pl.pallas_call(
        functools.partial(place_kernel, shards),
        in_specs=[pl.BlockSpec(memory_space=pltpu.SMEM)] + whole_vmem(shards),
        out_specs=pl.BlockSpec(memory_space=pltpu.VMEM),
        out_shape=jax.ShapeDtypeStruct((width, width), f32),
        compiler_params=params(),
        name="place_local",
    )(shard[None], *locals_)
    return (grad_spectral, grad_local)


def solution(mesh):
    return jax.shard_map(
        functools.partial(body, mesh.shape["dp"], mesh.shape["fsdp"]),
        mesh=mesh,
        in_specs=(
            P("dp", None, "fsdp", None, None, None),
            P("dp", None, "fsdp", None),
            P("dp", None),
            P(),
            P("fsdp", None, None, None),
            P(),
            P(),
        ),
        out_specs=(P("fsdp", None, None, None), P()),
        check_vma=False,
    )
```

```python
import functools
import math

import jax
import jax.numpy as jnp
import ml_dtypes
import numpy as np
from jax import lax
from jax.experimental import pallas as pl
from jax.experimental.pallas import tpu as pltpu
from jax.sharding import PartitionSpec as P

MX = 4
MY = 4
MZ = 2
MODES = MX * MY * MZ
VMEM_BYTES = 40 * 1024 * 1024
LARGE_VMEM_BYTES = 56 * 1024 * 1024
f32 = jnp.float32
bf16 = jnp.bfloat16
inv_root_two_pi = 0.3989422804014327
half_log2e = 0.7213475204444817
root_half = 0.7071067811865476


def split_bf16(values):
    high = values.astype(ml_dtypes.bfloat16)
    low = (values - high.astype(np.float64)).astype(ml_dtypes.bfloat16)
    return high, low


def angles(mode_ids, length):
    product = np.outer(mode_ids, np.arange(length)) % length
    return product * (2.0 * math.pi / length)


def phase_constants(length):
    y_angle = angles(np.arange(MY) - MY // 2, length)
    z_angle = angles(np.arange(MZ), length)
    rounded = lambda v: v.astype(np.float32).astype(ml_dtypes.bfloat16).astype(np.float64)
    cz, sz = rounded(np.cos(z_angle)), rounded(-np.sin(z_angle))
    cy, sy = np.cos(y_angle), -np.sin(y_angle)
    both = lambda a, b: (a[:, None, :, None] * b[None, :, None, :]).reshape(MY * MZ, length * length)
    fwd = np.concatenate([both(cy, cz) - both(sy, sz), both(sy, cz) + both(cy, sz)], axis=0)
    fwd = np.concatenate(split_bf16(fwd), axis=0)
    cz, sz = np.cos(z_angle), np.sin(z_angle)
    cy, sy = np.cos(y_angle), np.sin(y_angle)
    inv = np.concatenate([both(cy, cz) - both(sy, sz), -(both(sy, cz) + both(cy, sz))], axis=0).T
    high, low = split_bf16(inv)
    pad = np.zeros((length * length, 128 - 4 * high.shape[1]), ml_dtypes.bfloat16)
    inv = np.concatenate([high, low, high, low, pad], axis=1)
    x_angle = angles(np.arange(MX) - MX // 2, length).T
    xtab = np.stack([np.cos(x_angle), np.sin(x_angle)], axis=2).astype(np.float32)
    return fwd, inv, xtab.reshape(-1)


def scalar_places(slots):
    return dict(count=slots, total=slots + 1, shard=slots + 2, first=slots + 3, partner=slots + 4)


def combine_planes(q_ref, xtab_ref, cell0, shard, planes, scale, store):
    for d in range(MX):
        i = lax.rem(shard + d, MX)
        re = jnp.zeros((8, 128), f32)
        im = jnp.zeros((8, 128), f32)
        for a in range(planes):
            at = ((cell0 + a) * MX + i) * 2
            c = xtab_ref[at]
            s = xtab_ref[at + 1]
            q_re = q_ref[a, 0:8, :]
            q_im = q_ref[a, 8:16, :]
            re = re + (q_re * c + q_im * s)
            im = im + (q_im * c - q_re * s)
        store(d, re * scale, im * scale)


def forward_kernel(
    slots, base, sends, planes, step_planes, scale, meta_ref, xtab_ref, f_ref, basis_ref, *rest
):
    if sends:
        t_ref, outs, send_ref, t_out_ref, q_ref = rest[0], rest[1 : MX + 1], *rest[MX + 1 :]
    else:
        given, outs, q_ref = rest[:MX], rest[MX : 2 * MX], rest[2 * MX]
    place = scalar_places(slots)
    g, blk = pl.program_id(0), pl.program_id(1)
    live = base + g < meta_ref[place["count"]]
    row = pl.multiple_of(g * 16, 16)

    if not sends:

        @pl.when((g == 0) & (blk == 0))
        def _():
            rows = given[0].shape[0]
            for d in range(MX):
                outs[d][rows : 2 * rows, :] = given[d][...]

    @pl.when(live)
    def _():
        cells = f_ref.shape[3] * f_ref.shape[4]
        for p in range(step_planes):
            field = f_ref[0, 0, p].reshape(cells, 128)
            part = jnp.dot(basis_ref[...], field, preferred_element_type=f32)
            q_ref[blk * step_planes + p] = part[0:16] + part[16:32]
            if sends:
                send_ref[0, p] = f_ref[0, 0, p]
        if sends:

            @pl.when(blk == 0)
            def _():
                t_out_ref[0] = t_ref[0, 0]

        @pl.when(blk == planes // step_planes - 1)
        def _():
            def store(d, re, im):
                outs[d][pl.ds(row, 8), :] = re
                outs[d][pl.ds(row + 8, 8), :] = im

            combine_planes(
                q_ref, xtab_ref, meta_ref[place["first"]], meta_ref[place["shard"]], planes, scale, store
            )

    @pl.when(jnp.logical_not(live) & (blk == 0))
    def _():
        for out in outs:
            out[pl.ds(row, 16), :] = jnp.zeros((16, 128), f32)


def gelu_parts(pre):
    bell = jnp.exp2(pre * pre * (-half_log2e))
    cdf = 0.5 + 0.5 * lax.erf(pre * root_half)
    return cdf, bell


def shared_live(slots, kept, blocks, count, partner, g, blk):
    return (kept + g < count) & ((g > 0) | ((blk == blocks - 1) & (partner <= 1)))


def backward_kernel(
    slots, own, planes, step_planes, rows_step, scale, meta_ref, xtab_ref, f_ref, t_ref, *rest
):
    specs = rest[:MX]
    w_ref, proj_ref, inv_ref, basis_ref, eye_ref = rest[MX : MX + 5]
    rest = rest[MX + 5 :]
    if not own:
        given, rest = rest[:MX], rest[MX:]
    outs = rest[:MX]
    rhs_ref, pre_ref, d_ref, total_ref, q_ref, t8_ref, spec_ref, field_ref, line_ref = rest[MX:]
    place = scalar_places(slots)
    kept = slots - 3
    g, blk = pl.program_id(0), pl.program_id(1)
    blocks = planes // step_planes
    count, partner = meta_ref[place["count"]], meta_ref[place["partner"]]
    if own:
        some = g < count
        away = (g >= kept) & shared_live(slots, kept, blocks, count, partner, g - kept, blk)
        live = some & jnp.logical_not(away)
        positions, spec_row, out_row = kept + 1, g * 16, g * 16
        plane_of = lambda p: f_ref[0, 0, p].reshape(cells, 128)
        lines_of = lambda: t_ref[0, 0].astype(f32)
    else:
        some = kept + g < partner
        live = shared_live(slots, kept, blocks, partner, count, g, blk)
        positions, spec_row, out_row = 3, (kept + g) * 16, (kept + 1 + g) * 16
        plane_of = lambda p: f_ref[0, p].reshape(cells, 128)
        lines_of = lambda: t_ref[0].astype(f32)
    row = pl.multiple_of(out_row, 16)
    shard = meta_ref[place["shard"]]
    cell0 = meta_ref[place["first"]]
    cells = inv_ref.shape[0]
    third = cells // 3
    half = third // 2
    unroll = step_planes

    @pl.when((g == 0) & (blk == 0))
    def _():
        total_ref[...] = jnp.zeros_like(total_ref)
        for n in range(2):
            rhs_ref[n, 0:128, :] = w_ref[...]
            rhs_ref[n, 128:256, :] = jnp.zeros((128, 128), bf16)
        if not own:
            rows = (kept + 1) * 16
            for d in range(MX):
                outs[d][0:rows, :] = given[d][0:rows, :]

    @pl.when(some & (blk == 0))
    def _():
        q_ref[...] = jnp.zeros_like(q_ref)
        lines = lines_of()
        for a in range(planes):
            t8_ref[a] = jnp.broadcast_to(lines[a : a + 1, :], (8, cells))
        for d in range(MX):
            spec_ref[d] = specs[d][pl.ds(pl.multiple_of(spec_row, 16), 16), :].astype(f32)

    @pl.when(live)
    def _():
        grids = meta_ref[place["total"]].astype(f32)
        proj = proj_ref[...]
        proj_scaled = proj / jnp.full((1, 128), grids, f32)

        def first_rows(a, rhs):
            re = jnp.zeros((8, 128), f32)
            im = jnp.zeros((8, 128), f32)
            for d in range(MX):
                i = lax.rem(shard - d + MX, MX)
                at = ((cell0 + a) * MX + i) * 2
                c = xtab_ref[at]
                s = xtab_ref[at + 1]
                s_re = spec_ref[d, 0:8, :]
                s_im = spec_ref[d, 8:16, :]
                re = re + (s_re * c - s_im * s)
                im = im + (s_re * s + s_im * c)
            first = jnp.concatenate([re, im], axis=0) * scale
            high = first.astype(bf16)
            low = (first - high.astype(f32)).astype(bf16)
            rhs[128:144, :] = high
            rhs[144:160, :] = high
            rhs[160:176, :] = low
            rhs[176:192, :] = low

        def planes_together(n, carry):
            units = [(u, k) for u in range(unroll) for k in range(3)]
            q = [jnp.zeros((32, 128), f32) for _ in range(unroll)]
            for u in range(unroll):
                field_ref[u] = plane_of(n * unroll + u)
                line_ref[u] = t8_ref[blk * step_planes + n * unroll + u]

            def before(s):
                u, k = units[s]
                rhs = rhs_ref.at[u % 2]
                if k == 0:
                    first_rows(blk * step_planes + n * unroll + u, rhs)
                field = field_ref.at[u]
                for r0 in (0, half):
                    part = slice(k * third + r0, k * third + r0 + half)
                    lhs = jnp.concatenate([field[part, :], inv_ref[part, :]], axis=1)
                    pre_ref[s % 2, r0 : r0 + half, :] = jnp.dot(
                        lhs, rhs[...], preferred_element_type=f32
                    )

            def elementwise(s):
                u, k = units[s]
                for r0 in range(0, third, rows_step):
                    rows = slice(r0, r0 + rows_step)
                    pre = pre_ref[s % 2, rows, :]
                    cdf, bell = gelu_parts(pre)
                    slope = (cdf + pre * bell * inv_root_two_pi) * proj_scaled
                    n1 = r0 % 128
                    at = k * third + r0 - n1
                    line = line_ref[u, :, at : at + 128]
                    wanted = jnp.concatenate([line] * (rows_step // 8), axis=0)
                    active = pre * cdf * proj - wanted * eye_ref[n1 : n1 + rows_step, :]
                    resid = jnp.sum(active, axis=1, keepdims=True)
                    d_ref[s % 2, rows, :] = (resid * slope).astype(bf16)

            def last(s):
                u, k = units[s]
                part = slice(k * third, (k + 1) * third)
                lhs = jnp.concatenate([field_ref[u, part, :].T, basis_ref[:, part]], axis=0)
                sums = jnp.dot(lhs, d_ref[s % 2], preferred_element_type=f32)
                total_ref[...] += sums[0:128]
                q[u] = q[u] + sums[128:160]
                if k == 2:
                    q_ref[blk * step_planes + n * unroll + u] = q[u][0:16] + q[u][16:32]

            for s in range(len(units) + 2):
                if s < len(units):
                    before(s)
                if s >= 2:
                    last(s - 2)
                if 0 <= s - 1 < len(units):
                    elementwise(s - 1)
            return carry

        lax.fori_loop(0, step_planes // unroll, planes_together, 0)

    @pl.when(some & (blk == blocks - 1))
    def _():
        def store(d, re, im):
            outs[d][pl.ds(row, 8), :] = re
            outs[d][pl.ds(row + 8, 8), :] = im

        combine_planes(q_ref, xtab_ref, cell0, shard, planes, scale, store)

    @pl.when(jnp.logical_not(some) & (blk == 0))
    def _():
        for out in outs:
            out[pl.ds(row, 16), :] = jnp.zeros((16, 128), f32)

    @pl.when((g == positions - 1) & (blk == blocks - 1))
    def _():
        size = 128 // MX
        for d in range(MX):
            i = lax.rem(shard + d, MX)
            at = pl.multiple_of(i * size, size)
            part = total_ref[pl.ds(at, size), :]
            if not own:
                part = part + given[d][(kept + 1) * 16 : (kept + 1) * 16 + size, :]
            rows = outs[d].shape[0]
            outs[d][rows - size : rows, :] = part


def mix_kernel(slots, per, shards, *refs):
    parts = refs[:shards]
    w_ref, coeff_out, spec_out, c_ref, s_ref = refs[shards:]
    total = parts[0][...]
    for part in parts[1:]:
        total = total + part[...]
    coeff = total.astype(bf16)
    coeff_out[...] = coeff
    c_ref[...] = coeff.astype(f32)
    for m in range(per):
        re_rows = pl.ds(m, slots, stride=2 * per)
        im_rows = pl.ds(per + m, slots, stride=2 * per)
        re = c_ref[re_rows, :].astype(bf16)
        im = c_ref[im_rows, :].astype(bf16)
        weight = w_ref[m].reshape(256, 128)
        s_ref[re_rows, :] = jnp.dot(
            jnp.concatenate([re, -im], axis=1), weight, preferred_element_type=f32
        )
        s_ref[im_rows, :] = jnp.dot(
            jnp.concatenate([im, re], axis=1), weight, preferred_element_type=f32
        )
    spec_out[...] = s_ref[...].astype(bf16)


def sum_kernel(count, *refs):
    total = refs[0][...]
    for part in refs[1:count]:
        total = total + part[...]
    refs[count][...] = total


def local_sum_kernel(count, rows, *refs):
    size = refs[count].shape[0]
    total = refs[0][rows : rows + size, :]
    for part in refs[1:count]:
        total = total + part[rows : rows + size, :]
    refs[count][...] = total


def weight_kernel(lanes, slots, per, lane_ref, *refs):
    coeffs, backs = refs[:lanes], refs[lanes : 2 * lanes]
    out_ref, all_ref, c_ref, b_ref = refs[2 * lanes :]
    each = 2 * per
    kept = slots - 3
    rows = (slots + 1) * each
    for n in range(lanes):
        coeff = coeffs[n][...].astype(f32)
        c_ref[n * rows : n * rows + (kept + 1) * each, :] = coeff[0 : (kept + 1) * each]
        all_ref[n] = coeff[kept * each :]
        b_ref[n * rows : (n + 1) * rows, :] = backs[n][0:rows, :]
    for n in range(lanes):
        source = lax.rem(lane_ref[0] - n + lanes, lanes)
        other = lax.rem(n - 1 + 2 * lax.rem(source, 2) + lanes, lanes)
        c_ref[n * rows + (kept + 1) * each : (n + 1) * rows, :] = all_ref[other]
    slots = slots + 1
    for m in range(per):
        re_rows = pl.ds(m, lanes * slots, stride=2 * per)
        im_rows = pl.ds(per + m, lanes * slots, stride=2 * per)
        c_re = c_ref[re_rows, :].astype(bf16)
        c_im = c_ref[im_rows, :].astype(bf16)
        b_re = b_ref[re_rows, :]
        b_im = b_ref[im_rows, :]
        left = jnp.concatenate([c_re, c_im], axis=0)
        right = jnp.concatenate(
            [jnp.concatenate([b_re, b_im], axis=1), jnp.concatenate([b_im, -b_re], axis=1)], axis=0
        )
        high = right.astype(bf16)
        low = (right - high.astype(f32)).astype(bf16)
        left = jnp.concatenate([left, left], axis=0)
        right = jnp.concatenate([high, low], axis=0)
        grad = lax.dot_general(
            left, right, (((0,), (0,)), ((), ())), preferred_element_type=f32
        )
        out_ref[m, 0] = grad[:, 0:128]
        out_ref[m, 1] = grad[:, 128:256]


def place_kernel(shards, meta_ref, *refs):
    out_ref = refs[shards]
    size = refs[0].shape[0]
    for d in range(shards):
        i = lax.rem(meta_ref[0] - d + shards, shards)
        out_ref[pl.ds(pl.multiple_of(i * size, size), size), :] = refs[d][...]


def whole_vmem(count):
    return [pl.BlockSpec(memory_space=pltpu.VMEM)] * count


def params(limit=VMEM_BYTES):
    return pltpu.CompilerParams(vmem_limit_bytes=limit)


def rotations(value_of, axis, size):
    got = [value_of(0)]
    for d in range(1, size):
        perm = [(s, (s + d) % size) for s in range(size)]
        got.append(lax.ppermute(value_of(d), axis, perm))
    return got


def body(lanes, shards, fields, targets, lists, counts, spectral_w, local_w, proj):
    _, slots, planes, grid_len, _, width = fields.shape
    per = MODES // shards
    split = shards // MX
    cells = grid_len * grid_len
    step_planes = max(n for n in (1, 2, 3, 4) if planes % n == 0)
    blocks = planes // step_planes
    basis, inverse, xtab = phase_constants(grid_len)
    lane = lax.axis_index("dp").astype(jnp.int32)
    shard = lax.axis_index("fsdp").astype(jnp.int32)
    turn = shard if split == 1 else jnp.int32(0)
    meta = jnp.concatenate(
        [
            lists[0],
            counts[lane][None],
            jnp.sum(counts)[None],
            turn[None],
            (shard * planes)[None],
            counts[lane ^ 1][None],
        ]
    ).astype(jnp.int32)
    place = scalar_places(slots)

    kept = slots - 3

    def field_block(base):
        def block(g, blk, meta_ref, xtab_ref):
            count = meta_ref[place["count"]]
            slot = meta_ref[jnp.minimum(base + g, count - 1)]
            return (0, slot, jnp.where(base + g < count, blk, blocks - 1), 0, 0, 0)

        return pl.BlockSpec((1, 1, step_planes, grid_len, grid_len, width), block)

    def target_block(base):
        def block(g, blk, meta_ref, xtab_ref):
            count = meta_ref[place["count"]]
            return (0, meta_ref[jnp.minimum(base + g, count - 1)], 0, 0)

        return pl.BlockSpec((1, 1, planes, cells), block)

    def shared_item(g, blk):
        return jnp.maximum(g * blocks + blk - (blocks - 1), 0)

    def fixed(*shape):
        return pl.BlockSpec(shape, lambda g, blk, meta_ref, xtab_ref: (0,) * len(shape))

    items = 2 * blocks + 1
    shared_fields = pl.BlockSpec(
        (1, step_planes, grid_len, grid_len, width),
        lambda g, blk, meta_ref, xtab_ref: (shared_item(g, blk), 0, 0, 0, 0),
    )
    shared_targets = pl.BlockSpec((1, planes, cells), lambda g, blk, meta_ref, xtab_ref: (g, 0, 0))
    part_rows = slots * 16
    forward_scale = float(grid_len) ** (-1.5)
    *late_parts, sent_fields, sent_targets = pl.pallas_call(
        functools.partial(forward_kernel, slots, kept, True, planes, step_planes, forward_scale),
        grid_spec=pltpu.PrefetchScalarGridSpec(
            num_scalar_prefetch=2,
            grid=(3, blocks),
            in_specs=[field_block(kept), fixed(*basis.shape), target_block(kept)],
            out_specs=[fixed(3 * 16, width)] * MX + [shared_fields, shared_targets],
            scratch_shapes=[pltpu.VMEM((planes, 16, width), f32)],
        ),
        out_shape=[jax.ShapeDtypeStruct((3 * 16, width), f32)] * MX
        + [
            jax.ShapeDtypeStruct((items, step_planes, grid_len, grid_len, width), bf16),
            jax.ShapeDtypeStruct((3, planes, cells), bf16),
        ],
        compiler_params=params(),
        name="forward_shared",
    )(meta, xtab, fields, basis, targets)
    swap = lambda x: lax.ppermute(x, "dp", [(s, s ^ 1) for s in range(lanes)])
    came_fields = swap(sent_fields)
    came_targets = swap(sent_targets)
    parts = pl.pallas_call(
        functools.partial(forward_kernel, slots, 0, False, planes, step_planes, forward_scale),
        grid_spec=pltpu.PrefetchScalarGridSpec(
            num_scalar_prefetch=2,
            grid=(3, blocks),
            in_specs=[field_block(0), fixed(*basis.shape)] + [fixed(3 * 16, width)] * MX,
            out_specs=[fixed(part_rows, width)] * MX,
            scratch_shapes=[pltpu.VMEM((planes, 16, width), f32)],
        ),
        out_shape=[jax.ShapeDtypeStruct((part_rows, width), f32)] * MX,
        compiler_params=params(),
        cost_estimate=pl.CostEstimate(
            flops=3 * planes * cells * 256 * 256,
            bytes_accessed=3 * planes * cells * width * 2,
            transcendentals=0,
        ),
        name="forward_modes",
    )(meta, xtab, fields, basis, *late_parts)

    def shard_parts(pieces, count):
        if split == 1:
            return lambda d: pieces[d]
        stacked = jnp.stack(pieces).reshape(MX, count, 2, split, per, width)
        stacked = jnp.moveaxis(stacked, 3, 1).reshape(shards, count * 2 * per, width)
        return lambda d: lax.dynamic_index_in_dim(stacked, (shard + d) % shards, 0, keepdims=False)

    def mode_parts(pieces, count):
        if split == 1:
            return pieces
        stacked = jnp.stack(pieces)[(shard - jnp.arange(shards)) % shards]
        stacked = stacked.reshape(MX, split, count, 2, per, width)
        stacked = jnp.moveaxis(stacked, 1, 3).reshape(MX, count * 16, width)
        return [stacked[(-d) % MX] for d in range(MX)]

    came = rotations(shard_parts(parts, slots), "fsdp", shards)
    own_rows = slots * 2 * per
    coeff, own_spectrum = pl.pallas_call(
        functools.partial(mix_kernel, slots, per, shards),
        in_specs=whole_vmem(shards + 1),
        out_specs=whole_vmem(2),
        out_shape=[jax.ShapeDtypeStruct((own_rows, width), bf16)] * 2,
        scratch_shapes=[pltpu.VMEM((own_rows, width), f32)] * 2,
        compiler_params=params(),
        name="mix_modes",
    )(*came, spectral_w)
    spectrum = mode_parts(rotations(lambda d: own_spectrum, "fsdp", shards), slots)
    coeffs = rotations(lambda d: coeff, "dp", lanes)

    local_rows = width // MX
    eye = np.eye(128, dtype=np.float32)

    def own_block(g, blk, meta_ref, xtab_ref):
        count, partner = meta_ref[place["count"]], meta_ref[place["partner"]]
        slot = meta_ref[jnp.minimum(g, count - 1)]
        away = (g >= kept) & shared_live(slots, kept, blocks, count, partner, g - kept, blk)
        blk = jnp.where(away, max(blocks - 2, 0), blk)
        return (0, slot, jnp.where(g < count, blk, blocks - 1), 0, 0, 0)

    def came_item(g, blk, meta_ref):
        some = kept < meta_ref[place["partner"]]
        return jnp.where(some, shared_item(g, blk), 0), jnp.where(some, g, 0)

    came_block = pl.BlockSpec(
        (1, step_planes, grid_len, grid_len, width),
        lambda g, blk, meta_ref, xtab_ref: (came_item(g, blk, meta_ref)[0], 0, 0, 0, 0),
    )
    came_lines = pl.BlockSpec(
        (1, planes, cells), lambda g, blk, meta_ref, xtab_ref: (came_item(g, blk, meta_ref)[1], 0, 0)
    )

    def backward(own, fields_, targets_, spectrum_, given):
        positions = kept + 1 if own else 3
        rows = (kept + 1 if own else slots + 1) * 16 + local_rows
        own_fields = pl.BlockSpec((1, 1, step_planes, grid_len, grid_len, width), own_block)
        return pl.pallas_call(
            functools.partial(
                backward_kernel, slots, own, planes, step_planes, 64, float(MODES) ** (-0.5)
            ),
            grid_spec=pltpu.PrefetchScalarGridSpec(
                num_scalar_prefetch=2,
                grid=(positions, blocks),
                in_specs=([own_fields, target_block(0)] if own else [came_block, came_lines])
                + [fixed(part_rows, width)] * MX
                + [
                    fixed(width, width),
                    fixed(1, width),
                    fixed(*inverse.shape),
                    fixed(*basis.shape),
                    fixed(*eye.shape),
                ]
                + [fixed(*g.shape) for g in given],
                out_specs=[fixed(rows, width)] * MX,
                scratch_shapes=[
                    pltpu.VMEM((2, 256, width), bf16),
                    pltpu.VMEM((2, cells // 3, width), f32),
                    pltpu.VMEM((2, cells // 3, width), bf16),
                    pltpu.VMEM((width, width), f32),
                    pltpu.VMEM((planes, 16, width), f32),
                    pltpu.VMEM((planes, 8, cells), f32),
                    pltpu.VMEM((MX, 16, width), f32),
                    pltpu.VMEM((step_planes, cells, width), bf16),
                    pltpu.VMEM((step_planes, 8, cells), f32),
                ],
            ),
            out_shape=[jax.ShapeDtypeStruct((rows, width), f32)] * MX,
            compiler_params=params(LARGE_VMEM_BYTES),
            cost_estimate=pl.CostEstimate(
                flops=4 * positions * planes * cells * 256 * 256,
                bytes_accessed=positions * planes * cells * width * 2,
                transcendentals=0,
            ),
            name="backward_own" if own else "backward_shared",
        )(
            meta, xtab, fields_, targets_, *spectrum_, local_w, proj.reshape(1, width),
            inverse, basis, eye, *given,
        )

    came_spectrum = [swap(piece) for piece in spectrum]
    own_results = backward(True, fields, targets, spectrum, [])
    results = backward(False, came_fields, came_targets, came_spectrum, own_results)
    places = slots + 1
    part_rows = places * 16
    place_rows = places * 2 * per

    if split == 1:
        chunk = lambda d: results[d]
    else:
        backs = shard_parts([r[:part_rows] for r in results], places)
        local = jnp.concatenate([r[part_rows:] for r in results], axis=0)
        rows = width // shards
        chunk = lambda d: jnp.concatenate(
            [backs(d), lax.dynamic_slice_in_dim(local, (shard + d) % shards * rows, rows, 0)], axis=0
        )
    came = rotations(chunk, "fsdp", shards)
    own_sum = pl.pallas_call(
        functools.partial(sum_kernel, shards),
        in_specs=whole_vmem(shards),
        out_specs=pl.BlockSpec(memory_space=pltpu.VMEM),
        out_shape=jax.ShapeDtypeStruct(came[0].shape, f32),
        compiler_params=params(),
        name="sum_shards",
    )(*came)
    sums = rotations(lambda d: own_sum, "dp", lanes)
    own_local = pl.pallas_call(
        functools.partial(local_sum_kernel, lanes, place_rows),
        in_specs=whole_vmem(lanes),
        out_specs=pl.BlockSpec(memory_space=pltpu.VMEM),
        out_shape=jax.ShapeDtypeStruct((width // shards, width), f32),
        compiler_params=params(),
        name="sum_local",
    )(*sums)
    locals_ = rotations(lambda d: own_local, "fsdp", shards)
    grad_spectral = pl.pallas_call(
        functools.partial(weight_kernel, lanes, slots, per),
        in_specs=[pl.BlockSpec(memory_space=pltpu.SMEM)] + whole_vmem(2 * lanes),
        out_specs=pl.BlockSpec(memory_space=pltpu.VMEM),
        out_shape=jax.ShapeDtypeStruct((per, 2, width, width), f32),
        scratch_shapes=[pltpu.VMEM((lanes, 3 * 2 * per, width), f32)]
        + [pltpu.VMEM((lanes * place_rows, width), f32)] * 2,
        compiler_params=params(),
        cost_estimate=pl.CostEstimate(
            flops=2 * per * 256 * 128 * 256, bytes_accessed=2 * per * 2 * width * width * 4, transcendentals=0
        ),
        name="weight_grad",
    )(lane[None], *coeffs, *sums)
    grad_local = pl.pallas_call(
        functools.partial(place_kernel, shards),
        in_specs=[pl.BlockSpec(memory_space=pltpu.SMEM)] + whole_vmem(shards),
        out_specs=pl.BlockSpec(memory_space=pltpu.VMEM),
        out_shape=jax.ShapeDtypeStruct((width, width), f32),
        compiler_params=params(),
        name="place_local",
    )(shard[None], *locals_)
    return (grad_spectral, grad_local)


def solution(mesh):
    return jax.shard_map(
        functools.partial(body, mesh.shape["dp"], mesh.shape["fsdp"]),
        mesh=mesh,
        in_specs=(
            P("dp", None, "fsdp", None, None, None),
            P("dp", None, "fsdp", None),
            P("dp", None),
            P(),
            P("fsdp", None, None, None),
            P(),
            P(),
        ),
        out_specs=(P("fsdp", None, None, None), P()),
        check_vma=False,
    )
```

```python
import functools
import math

import jax
import jax.numpy as jnp
import ml_dtypes
import numpy as np
from jax import lax
from jax.experimental import pallas as pl
from jax.experimental.pallas import tpu as pltpu
from jax.sharding import PartitionSpec as P

MX = 4
MY = 4
MZ = 2
MODES = MX * MY * MZ
VMEM_BYTES = 40 * 1024 * 1024
LARGE_VMEM_BYTES = 56 * 1024 * 1024
f32 = jnp.float32
bf16 = jnp.bfloat16
inv_root_two_pi = 0.3989422804014327
half_log2e = 0.7213475204444817
root_half = 0.7071067811865476


def split_bf16(values):
    high = values.astype(ml_dtypes.bfloat16)
    low = (values - high.astype(np.float64)).astype(ml_dtypes.bfloat16)
    return high, low


def angles(mode_ids, length):
    product = np.outer(mode_ids, np.arange(length)) % length
    return product * (2.0 * math.pi / length)


def phase_constants(length):
    y_angle = angles(np.arange(MY) - MY // 2, length)
    z_angle = angles(np.arange(MZ), length)
    rounded = lambda v: v.astype(np.float32).astype(ml_dtypes.bfloat16).astype(np.float64)
    cz, sz = rounded(np.cos(z_angle)), rounded(-np.sin(z_angle))
    cy, sy = np.cos(y_angle), -np.sin(y_angle)
    both = lambda a, b: (a[:, None, :, None] * b[None, :, None, :]).reshape(MY * MZ, length * length)
    fwd = np.concatenate([both(cy, cz) - both(sy, sz), both(sy, cz) + both(cy, sz)], axis=0)
    fwd = np.concatenate(split_bf16(fwd), axis=0)
    cz, sz = np.cos(z_angle), np.sin(z_angle)
    cy, sy = np.cos(y_angle), np.sin(y_angle)
    inv = np.concatenate([both(cy, cz) - both(sy, sz), -(both(sy, cz) + both(cy, sz))], axis=0).T
    high, low = split_bf16(inv)
    pad = np.zeros((length * length, 128 - 4 * high.shape[1]), ml_dtypes.bfloat16)
    inv = np.concatenate([high, low, high, low, pad], axis=1)
    x_angle = angles(np.arange(MX) - MX // 2, length).T
    xtab = np.stack([np.cos(x_angle), np.sin(x_angle)], axis=2).astype(np.float32)
    return fwd, inv, xtab.reshape(-1)


def scalar_places(slots):
    return dict(count=slots, total=slots + 1, shard=slots + 2, first=slots + 3, partner=slots + 4)


def combine_planes(q_ref, xtab_ref, cell0, shard, planes, scale, store):
    for d in range(MX):
        i = lax.rem(shard + d, MX)
        re = jnp.zeros((8, 128), f32)
        im = jnp.zeros((8, 128), f32)
        for a in range(planes):
            at = ((cell0 + a) * MX + i) * 2
            c = xtab_ref[at]
            s = xtab_ref[at + 1]
            q_re = q_ref[a, 0:8, :]
            q_im = q_ref[a, 8:16, :]
            re = re + (q_re * c + q_im * s)
            im = im + (q_im * c - q_re * s)
        store(d, re * scale, im * scale)


def forward_kernel(
    slots, base, sends, planes, step_planes, scale, meta_ref, xtab_ref, f_ref, basis_ref, *rest
):
    if sends:
        t_ref, outs, send_ref, t_out_ref, q_ref = rest[0], rest[1 : MX + 1], *rest[MX + 1 :]
    else:
        given, outs, q_ref = rest[:MX], rest[MX : 2 * MX], rest[2 * MX]
    place = scalar_places(slots)
    g, blk = pl.program_id(0), pl.program_id(1)
    live = base + g < meta_ref[place["count"]]
    row = pl.multiple_of(g * 16, 16)

    if not sends:

        @pl.when((g == 0) & (blk == 0))
        def _():
            rows = given[0].shape[0]
            for d in range(MX):
                outs[d][rows : 2 * rows, :] = given[d][...]

    @pl.when(live)
    def _():
        cells = f_ref.shape[3] * f_ref.shape[4]
        for p in range(step_planes):
            field = f_ref[0, 0, p].reshape(cells, 128)
            part = jnp.dot(basis_ref[...], field, preferred_element_type=f32)
            q_ref[blk * step_planes + p] = part[0:16] + part[16:32]
            if sends:
                send_ref[0, p] = f_ref[0, 0, p]
        if sends:

            @pl.when(blk == 0)
            def _():
                t_out_ref[0] = t_ref[0, 0]

        @pl.when(blk == planes // step_planes - 1)
        def _():
            def store(d, re, im):
                outs[d][pl.ds(row, 8), :] = re
                outs[d][pl.ds(row + 8, 8), :] = im

            combine_planes(
                q_ref, xtab_ref, meta_ref[place["first"]], meta_ref[place["shard"]], planes, scale, store
            )

    @pl.when(jnp.logical_not(live) & (blk == 0))
    def _():
        for out in outs:
            out[pl.ds(row, 16), :] = jnp.zeros((16, 128), f32)


def gelu_parts(pre):
    bell = jnp.exp2(pre * pre * (-half_log2e))
    return 1.0 + lax.erf(pre * root_half), bell


def shared_live(slots, kept, blocks, count, partner, g, blk):
    return (kept + g < count) & ((g > 0) | ((blk == blocks - 1) & (partner <= 1)))


def backward_kernel(
    slots, own, planes, step_planes, rows_step, scale, meta_ref, xtab_ref, f_ref, t_ref, *rest
):
    specs = rest[:MX]
    w_ref, proj_ref, inv_ref, basis_ref, eye_ref = rest[MX : MX + 5]
    rest = rest[MX + 5 :]
    if not own:
        given, rest = rest[:MX], rest[MX:]
    outs = rest[:MX]
    rhs_ref, pre_ref, slope_ref, resid_ref, d_ref, total_ref, q_ref, t8_ref, spec_ref, field_ref, line_ref, near_ref = rest[MX:]
    place = scalar_places(slots)
    kept = slots - 3
    g, blk = pl.program_id(0), pl.program_id(1)
    blocks = planes // step_planes
    count, partner = meta_ref[place["count"]], meta_ref[place["partner"]]
    if own:
        some = g < count
        away = (g >= kept) & shared_live(slots, kept, blocks, count, partner, g - kept, blk)
        live = some & jnp.logical_not(away)
        positions, spec_row, out_row = kept + 1, g * 16, g * 16
        plane_of = lambda p: f_ref[0, 0, p].reshape(cells, 128)
        lines_of = lambda: t_ref[0, 0].astype(f32)
    else:
        some = kept + g < partner
        live = shared_live(slots, kept, blocks, partner, count, g, blk)
        positions, spec_row, out_row = 3, (kept + g) * 16, (kept + 1 + g) * 16
        plane_of = lambda p: f_ref[0, p].reshape(cells, 128)
        lines_of = lambda: t_ref[0].astype(f32)
    row = pl.multiple_of(out_row, 16)
    shard = meta_ref[place["shard"]]
    cell0 = meta_ref[place["first"]]
    cells = inv_ref.shape[0]
    third = cells // 3
    half = third // 2
    unroll = step_planes

    @pl.when((g == 0) & (blk == 0))
    def _():
        total_ref[...] = jnp.zeros_like(total_ref)
        for n in range(2):
            rhs_ref[n, 0:128, :] = w_ref[...]
            rhs_ref[n, 128:256, :] = jnp.zeros((128, 128), bf16)
        if not own:
            rows = (kept + 1) * 16
            for d in range(MX):
                outs[d][0:rows, :] = given[d][0:rows, :]

    @pl.when(some & (blk == 0))
    def _():
        q_ref[...] = jnp.zeros_like(q_ref)
        lines = lines_of()
        for a in range(planes):
            t8_ref[a] = jnp.broadcast_to(lines[a : a + 1, :], (8, cells))
        for d in range(MX):
            spec_ref[d] = specs[d][pl.ds(pl.multiple_of(spec_row, 16), 16), :].astype(f32)

    @pl.when(live)
    def _():
        grids = meta_ref[place["total"]].astype(f32)
        proj = 0.5 * proj_ref[...]
        proj_scaled = proj / jnp.full((1, 128), grids, f32)

        def first_rows(a, rhs):
            re = jnp.zeros((8, 128), f32)
            im = jnp.zeros((8, 128), f32)
            for d in range(MX):
                i = lax.rem(shard - d + MX, MX)
                at = ((cell0 + a) * MX + i) * 2
                c = xtab_ref[at]
                s = xtab_ref[at + 1]
                s_re = spec_ref[d, 0:8, :]
                s_im = spec_ref[d, 8:16, :]
                re = re + (s_re * c - s_im * s)
                im = im + (s_re * s + s_im * c)
            first = jnp.concatenate([re, im], axis=0) * scale
            high = first.astype(bf16)
            low = (first - high.astype(f32)).astype(bf16)
            rhs[128:144, :] = high
            rhs[144:160, :] = high
            rhs[160:176, :] = low
            rhs[176:192, :] = low

        def planes_together(n, carry):
            units = [(u, k) for u in range(unroll) for k in range(3)]
            for u in range(unroll):
                field_ref[u] = plane_of(n * unroll + u)
                line_ref[u] = t8_ref[blk * step_planes + n * unroll + u]

            def before(s, r0):
                u, k = units[s]
                rhs = rhs_ref.at[u % 2]
                if k == 0 and r0 == 0:
                    first_rows(blk * step_planes + n * unroll + u, rhs)
                part = slice(k * third + r0, k * third + r0 + half)
                lhs = jnp.concatenate([field_ref[u, part, :], inv_ref[part, :]], axis=1)
                pre_ref[s % 2, r0 : r0 + half, :] = jnp.dot(lhs, rhs[...], preferred_element_type=f32)

            def elementwise(s, r0):
                u, k = units[s]
                rows = slice(r0, r0 + rows_step)
                pre = pre_ref[s % 2, rows, :]
                twice, bell = gelu_parts(pre)
                slope_ref[s % 2, rows, :] = (twice + pre * bell * (2.0 * inv_root_two_pi)) * proj_scaled
                at = k * third + r0
                line = line_ref[u, :, at : at + 128]
                wanted = jnp.concatenate([line] * (rows_step // 8), axis=0)
                active = pre * twice * proj - wanted * eye_ref[...]
                resid = jnp.sum(active, axis=1, keepdims=True)
                resid_ref[s % 2, rows, :] = jnp.broadcast_to(resid, (rows_step, 128))

            def product(s, r0):
                rows = slice(r0, r0 + rows_step)
                d_ref[s % 2, rows, :] = (resid_ref[s % 2, rows, :] * slope_ref[s % 2, rows, :]).astype(bf16)

            def last(s, r0):
                u, k = units[s]
                part = slice(k * third + r0, k * third + r0 + third // 3)
                lhs = jnp.concatenate([field_ref[u, part, :].T, basis_ref[:, part]], axis=0)
                sums = jnp.dot(lhs, d_ref[s % 2, r0 : r0 + third // 3, :], preferred_element_type=f32)
                total_ref[...] += sums[0:128]
                back = sums[128:144] + sums[144:160]
                near_ref[u] = back if k == 0 and r0 == 0 else near_ref[u] + back

            pieces = third // rows_step
            for s in range(len(units) + 3):
                for piece in range(pieces):
                    r0 = piece * rows_step
                    if s < len(units) and r0 % half == 0:
                        before(s, r0)
                    if 0 <= s - 3 and piece % 2 == 0:
                        last(s - 3, r0)
                    if 0 <= s - 2 < len(units):
                        product(s - 2, r0)
                    if 0 <= s - 1 < len(units):
                        elementwise(s - 1, r0)
            for u in range(unroll):
                q_ref[blk * step_planes + n * unroll + u] = near_ref[u]
            return carry

        lax.fori_loop(0, step_planes // unroll, planes_together, 0)

    @pl.when(some & (blk == blocks - 1))
    def _():
        def store(d, re, im):
            outs[d][pl.ds(row, 8), :] = re
            outs[d][pl.ds(row + 8, 8), :] = im

        combine_planes(q_ref, xtab_ref, cell0, shard, planes, scale, store)

    @pl.when(jnp.logical_not(some) & (blk == 0))
    def _():
        for out in outs:
            out[pl.ds(row, 16), :] = jnp.zeros((16, 128), f32)

    @pl.when((g == positions - 1) & (blk == blocks - 1))
    def _():
        size = 128 // MX
        for d in range(MX):
            i = lax.rem(shard + d, MX)
            at = pl.multiple_of(i * size, size)
            part = total_ref[pl.ds(at, size), :]
            if not own:
                part = part + given[d][(kept + 1) * 16 : (kept + 1) * 16 + size, :]
            rows = outs[d].shape[0]
            outs[d][rows - size : rows, :] = part


def mix_kernel(slots, per, shards, *refs):
    parts = refs[:shards]
    w_ref, coeff_out, spec_out, c_ref, s_ref = refs[shards:]
    total = parts[0][...]
    for part in parts[1:]:
        total = total + part[...]
    coeff = total.astype(bf16)
    coeff_out[...] = coeff
    c_ref[...] = coeff.astype(f32)
    for m in range(per):
        re_rows = pl.ds(m, slots, stride=2 * per)
        im_rows = pl.ds(per + m, slots, stride=2 * per)
        re = c_ref[re_rows, :].astype(bf16)
        im = c_ref[im_rows, :].astype(bf16)
        weight = w_ref[m].reshape(256, 128)
        s_ref[re_rows, :] = jnp.dot(
            jnp.concatenate([re, -im], axis=1), weight, preferred_element_type=f32
        )
        s_ref[im_rows, :] = jnp.dot(
            jnp.concatenate([im, re], axis=1), weight, preferred_element_type=f32
        )
    spec_out[...] = s_ref[...].astype(bf16)


def sum_kernel(count, *refs):
    total = refs[0][...]
    for part in refs[1:count]:
        total = total + part[...]
    refs[count][...] = total


def local_sum_kernel(count, rows, *refs):
    size = refs[count].shape[0]
    total = refs[0][rows : rows + size, :]
    for part in refs[1:count]:
        total = total + part[rows : rows + size, :]
    refs[count][...] = total


def weight_kernel(lanes, slots, per, lane_ref, *refs):
    coeffs, backs = refs[:lanes], refs[lanes : 2 * lanes]
    out_ref, all_ref, c_ref, b_ref = refs[2 * lanes :]
    each = 2 * per
    kept = slots - 3
    rows = (slots + 1) * each
    for n in range(lanes):
        coeff = coeffs[n][...].astype(f32)
        c_ref[n * rows : n * rows + (kept + 1) * each, :] = coeff[0 : (kept + 1) * each]
        all_ref[n] = coeff[kept * each :]
        b_ref[n * rows : (n + 1) * rows, :] = backs[n][0:rows, :]
    for n in range(lanes):
        source = lax.rem(lane_ref[0] - n + lanes, lanes)
        other = lax.rem(n - 1 + 2 * lax.rem(source, 2) + lanes, lanes)
        c_ref[n * rows + (kept + 1) * each : (n + 1) * rows, :] = all_ref[other]
    slots = slots + 1
    for m in range(per):
        re_rows = pl.ds(m, lanes * slots, stride=2 * per)
        im_rows = pl.ds(per + m, lanes * slots, stride=2 * per)
        c_re = c_ref[re_rows, :].astype(bf16)
        c_im = c_ref[im_rows, :].astype(bf16)
        b_re = b_ref[re_rows, :]
        b_im = b_ref[im_rows, :]
        left = jnp.concatenate([c_re, c_im], axis=0)
        right = jnp.concatenate(
            [jnp.concatenate([b_re, b_im], axis=1), jnp.concatenate([b_im, -b_re], axis=1)], axis=0
        )
        high = right.astype(bf16)
        low = (right - high.astype(f32)).astype(bf16)
        left = jnp.concatenate([left, left], axis=0)
        right = jnp.concatenate([high, low], axis=0)
        grad = lax.dot_general(
            left, right, (((0,), (0,)), ((), ())), preferred_element_type=f32
        )
        out_ref[m, 0] = grad[:, 0:128]
        out_ref[m, 1] = grad[:, 128:256]


def place_kernel(shards, meta_ref, *refs):
    out_ref = refs[shards]
    size = refs[0].shape[0]
    for d in range(shards):
        i = lax.rem(meta_ref[0] - d + shards, shards)
        out_ref[pl.ds(pl.multiple_of(i * size, size), size), :] = refs[d][...]


def whole_vmem(count):
    return [pl.BlockSpec(memory_space=pltpu.VMEM)] * count


def params(limit=VMEM_BYTES):
    return pltpu.CompilerParams(vmem_limit_bytes=limit)


def rotations(value_of, axis, size):
    got = [value_of(0)]
    for d in range(1, size):
        perm = [(s, (s + d) % size) for s in range(size)]
        got.append(lax.ppermute(value_of(d), axis, perm))
    return got


def body(lanes, shards, fields, targets, lists, counts, spectral_w, local_w, proj):
    _, slots, planes, grid_len, _, width = fields.shape
    per = MODES // shards
    split = shards // MX
    cells = grid_len * grid_len
    step_planes = max(n for n in (1, 2, 3, 4) if planes % n == 0)
    blocks = planes // step_planes
    basis, inverse, xtab = phase_constants(grid_len)
    lane = lax.axis_index("dp").astype(jnp.int32)
    shard = lax.axis_index("fsdp").astype(jnp.int32)
    turn = shard if split == 1 else jnp.int32(0)
    meta = jnp.concatenate(
        [
            lists[0],
            counts[lane][None],
            jnp.sum(counts)[None],
            turn[None],
            (shard * planes)[None],
            counts[lane ^ 1][None],
        ]
    ).astype(jnp.int32)
    place = scalar_places(slots)

    kept = slots - 3

    def field_block(base):
        def block(g, blk, meta_ref, xtab_ref):
            count = meta_ref[place["count"]]
            slot = meta_ref[jnp.minimum(base + g, count - 1)]
            return (0, slot, jnp.where(base + g < count, blk, blocks - 1), 0, 0, 0)

        return pl.BlockSpec((1, 1, step_planes, grid_len, grid_len, width), block)

    def target_block(base):
        def block(g, blk, meta_ref, xtab_ref):
            count = meta_ref[place["count"]]
            return (0, meta_ref[jnp.minimum(base + g, count - 1)], 0, 0)

        return pl.BlockSpec((1, 1, planes, cells), block)

    def shared_item(g, blk):
        return jnp.maximum(g * blocks + blk - (blocks - 1), 0)

    def fixed(*shape):
        return pl.BlockSpec(shape, lambda g, blk, meta_ref, xtab_ref: (0,) * len(shape))

    items = 2 * blocks + 1
    shared_fields = pl.BlockSpec(
        (1, step_planes, grid_len, grid_len, width),
        lambda g, blk, meta_ref, xtab_ref: (shared_item(g, blk), 0, 0, 0, 0),
    )
    shared_targets = pl.BlockSpec((1, planes, cells), lambda g, blk, meta_ref, xtab_ref: (g, 0, 0))
    part_rows = slots * 16
    forward_scale = float(grid_len) ** (-1.5)
    *late_parts, sent_fields, sent_targets = pl.pallas_call(
        functools.partial(forward_kernel, slots, kept, True, planes, step_planes, forward_scale),
        grid_spec=pltpu.PrefetchScalarGridSpec(
            num_scalar_prefetch=2,
            grid=(3, blocks),
            in_specs=[field_block(kept), fixed(*basis.shape), target_block(kept)],
            out_specs=[fixed(3 * 16, width)] * MX + [shared_fields, shared_targets],
            scratch_shapes=[pltpu.VMEM((planes, 16, width), f32)],
        ),
        out_shape=[jax.ShapeDtypeStruct((3 * 16, width), f32)] * MX
        + [
            jax.ShapeDtypeStruct((items, step_planes, grid_len, grid_len, width), bf16),
            jax.ShapeDtypeStruct((3, planes, cells), bf16),
        ],
        compiler_params=params(),
        name="forward_shared",
    )(meta, xtab, fields, basis, targets)
    swap = lambda x: lax.ppermute(x, "dp", [(s, s ^ 1) for s in range(lanes)])
    came_fields = swap(sent_fields)
    came_targets = swap(sent_targets)
    parts = pl.pallas_call(
        functools.partial(forward_kernel, slots, 0, False, planes, step_planes, forward_scale),
        grid_spec=pltpu.PrefetchScalarGridSpec(
            num_scalar_prefetch=2,
            grid=(3, blocks),
            in_specs=[field_block(0), fixed(*basis.shape)] + [fixed(3 * 16, width)] * MX,
            out_specs=[fixed(part_rows, width)] * MX,
            scratch_shapes=[pltpu.VMEM((planes, 16, width), f32)],
        ),
        out_shape=[jax.ShapeDtypeStruct((part_rows, width), f32)] * MX,
        compiler_params=params(),
        cost_estimate=pl.CostEstimate(
            flops=3 * planes * cells * 256 * 256,
            bytes_accessed=3 * planes * cells * width * 2,
            transcendentals=0,
        ),
        name="forward_modes",
    )(meta, xtab, fields, basis, *late_parts)

    def shard_parts(pieces, count):
        if split == 1:
            return lambda d: pieces[d]
        stacked = jnp.stack(pieces).reshape(MX, count, 2, split, per, width)
        stacked = jnp.moveaxis(stacked, 3, 1).reshape(shards, count * 2 * per, width)
        return lambda d: lax.dynamic_index_in_dim(stacked, (shard + d) % shards, 0, keepdims=False)

    def mode_parts(pieces, count):
        if split == 1:
            return pieces
        stacked = jnp.stack(pieces)[(shard - jnp.arange(shards)) % shards]
        stacked = stacked.reshape(MX, split, count, 2, per, width)
        stacked = jnp.moveaxis(stacked, 1, 3).reshape(MX, count * 16, width)
        return [stacked[(-d) % MX] for d in range(MX)]

    came = rotations(shard_parts(parts, slots), "fsdp", shards)
    own_rows = slots * 2 * per
    coeff, own_spectrum = pl.pallas_call(
        functools.partial(mix_kernel, slots, per, shards),
        in_specs=whole_vmem(shards + 1),
        out_specs=whole_vmem(2),
        out_shape=[jax.ShapeDtypeStruct((own_rows, width), bf16)] * 2,
        scratch_shapes=[pltpu.VMEM((own_rows, width), f32)] * 2,
        compiler_params=params(),
        name="mix_modes",
    )(*came, spectral_w)
    spectrum = mode_parts(rotations(lambda d: own_spectrum, "fsdp", shards), slots)
    coeffs = rotations(lambda d: coeff, "dp", lanes)

    local_rows = width // MX
    eye = np.eye(128, dtype=np.float32)

    def own_block(g, blk, meta_ref, xtab_ref):
        count, partner = meta_ref[place["count"]], meta_ref[place["partner"]]
        slot = meta_ref[jnp.minimum(g, count - 1)]
        away = (g >= kept) & shared_live(slots, kept, blocks, count, partner, g - kept, blk)
        blk = jnp.where(away, max(blocks - 2, 0), blk)
        return (0, slot, jnp.where(g < count, blk, blocks - 1), 0, 0, 0)

    def came_item(g, blk, meta_ref):
        some = kept < meta_ref[place["partner"]]
        return jnp.where(some, shared_item(g, blk), 0), jnp.where(some, g, 0)

    came_block = pl.BlockSpec(
        (1, step_planes, grid_len, grid_len, width),
        lambda g, blk, meta_ref, xtab_ref: (came_item(g, blk, meta_ref)[0], 0, 0, 0, 0),
    )
    came_lines = pl.BlockSpec(
        (1, planes, cells), lambda g, blk, meta_ref, xtab_ref: (came_item(g, blk, meta_ref)[1], 0, 0)
    )

    def backward(own, fields_, targets_, spectrum_, given):
        positions = kept + 1 if own else 3
        rows = (kept + 1 if own else slots + 1) * 16 + local_rows
        own_fields = pl.BlockSpec((1, 1, step_planes, grid_len, grid_len, width), own_block)
        return pl.pallas_call(
            functools.partial(
                backward_kernel, slots, own, planes, step_planes, 128, float(MODES) ** (-0.5)
            ),
            grid_spec=pltpu.PrefetchScalarGridSpec(
                num_scalar_prefetch=2,
                grid=(positions, blocks),
                in_specs=([own_fields, target_block(0)] if own else [came_block, came_lines])
                + [fixed(part_rows, width)] * MX
                + [
                    fixed(width, width),
                    fixed(1, width),
                    fixed(*inverse.shape),
                    fixed(*basis.shape),
                    fixed(*eye.shape),
                ]
                + [fixed(*g.shape) for g in given],
                out_specs=[fixed(rows, width)] * MX,
                scratch_shapes=[
                    pltpu.VMEM((2, 256, width), bf16),
                    pltpu.VMEM((2, cells // 3, width), f32),
                    pltpu.VMEM((2, cells // 3, width), f32),
                    pltpu.VMEM((2, cells // 3, width), f32),
                    pltpu.VMEM((2, cells // 3, width), bf16),
                    pltpu.VMEM((width, width), f32),
                    pltpu.VMEM((planes, 16, width), f32),
                    pltpu.VMEM((planes, 8, cells), f32),
                    pltpu.VMEM((MX, 16, width), f32),
                    pltpu.VMEM((step_planes, cells, width), bf16),
                    pltpu.VMEM((step_planes, 8, cells), f32),
                    pltpu.VMEM((step_planes, 16, width), f32),
                ],
            ),
            out_shape=[jax.ShapeDtypeStruct((rows, width), f32)] * MX,
            compiler_params=params(LARGE_VMEM_BYTES),
            cost_estimate=pl.CostEstimate(
                flops=4 * positions * planes * cells * 256 * 256,
                bytes_accessed=positions * planes * cells * width * 2,
                transcendentals=0,
            ),
            name="backward_own" if own else "backward_shared",
        )(
            meta, xtab, fields_, targets_, *spectrum_, local_w, proj.reshape(1, width),
            inverse, basis, eye, *given,
        )

    came_spectrum = [swap(piece) for piece in spectrum]
    own_results = backward(True, fields, targets, spectrum, [])
    results = backward(False, came_fields, came_targets, came_spectrum, own_results)
    places = slots + 1
    part_rows = places * 16
    place_rows = places * 2 * per

    if split == 1:
        chunk = lambda d: results[d]
    else:
        backs = shard_parts([r[:part_rows] for r in results], places)
        local = jnp.concatenate([r[part_rows:] for r in results], axis=0)
        rows = width // shards
        chunk = lambda d: jnp.concatenate(
            [backs(d), lax.dynamic_slice_in_dim(local, (shard + d) % shards * rows, rows, 0)], axis=0
        )
    came = rotations(chunk, "fsdp", shards)
    own_sum = pl.pallas_call(
        functools.partial(sum_kernel, shards),
        in_specs=whole_vmem(shards),
        out_specs=pl.BlockSpec(memory_space=pltpu.VMEM),
        out_shape=jax.ShapeDtypeStruct(came[0].shape, f32),
        compiler_params=params(),
        name="sum_shards",
    )(*came)
    sums = rotations(lambda d: own_sum, "dp", lanes)
    own_local = pl.pallas_call(
        functools.partial(local_sum_kernel, lanes, place_rows),
        in_specs=whole_vmem(lanes),
        out_specs=pl.BlockSpec(memory_space=pltpu.VMEM),
        out_shape=jax.ShapeDtypeStruct((width // shards, width), f32),
        compiler_params=params(),
        name="sum_local",
    )(*sums)
    locals_ = rotations(lambda d: own_local, "fsdp", shards)
    grad_spectral = pl.pallas_call(
        functools.partial(weight_kernel, lanes, slots, per),
        in_specs=[pl.BlockSpec(memory_space=pltpu.SMEM)] + whole_vmem(2 * lanes),
        out_specs=pl.BlockSpec(memory_space=pltpu.VMEM),
        out_shape=jax.ShapeDtypeStruct((per, 2, width, width), f32),
        scratch_shapes=[pltpu.VMEM((lanes, 3 * 2 * per, width), f32)]
        + [pltpu.VMEM((lanes * place_rows, width), f32)] * 2,
        compiler_params=params(),
        cost_estimate=pl.CostEstimate(
            flops=2 * per * 256 * 128 * 256, bytes_accessed=2 * per * 2 * width * width * 4, transcendentals=0
        ),
        name="weight_grad",
    )(lane[None], *coeffs, *sums)
    grad_local = pl.pallas_call(
        functools.partial(place_kernel, shards),
        in_specs=[pl.BlockSpec(memory_space=pltpu.SMEM)] + whole_vmem(shards),
        out_specs=pl.BlockSpec(memory_space=pltpu.VMEM),
        out_shape=jax.ShapeDtypeStruct((width, width), f32),
        compiler_params=params(),
        name="place_local",
    )(shard[None], *locals_)
    return (grad_spectral, grad_local)


def solution(mesh):
    return jax.shard_map(
        functools.partial(body, mesh.shape["dp"], mesh.shape["fsdp"]),
        mesh=mesh,
        in_specs=(
            P("dp", None, "fsdp", None, None, None),
            P("dp", None, "fsdp", None),
            P("dp", None),
            P(),
            P("fsdp", None, None, None),
            P(),
            P(),
        ),
        out_specs=(P("fsdp", None, None, None), P()),
        check_vma=False,
    )
```

```python
import functools
import math

import jax
import jax.numpy as jnp
import ml_dtypes
import numpy as np
from jax import lax
from jax.experimental import pallas as pl
from jax.experimental.pallas import tpu as pltpu
from jax.sharding import PartitionSpec as P

MX = 4
MY = 4
MZ = 2
MODES = MX * MY * MZ
VMEM_BYTES = 40 * 1024 * 1024
LARGE_VMEM_BYTES = 56 * 1024 * 1024
f32 = jnp.float32
bf16 = jnp.bfloat16
inv_root_two_pi = 0.3989422804014327
half_log2e = 0.7213475204444817
root_half = 0.7071067811865476


def split_bf16(values):
    high = values.astype(ml_dtypes.bfloat16)
    low = (values - high.astype(np.float64)).astype(ml_dtypes.bfloat16)
    return high, low


def angles(mode_ids, length):
    product = np.outer(mode_ids, np.arange(length)) % length
    return product * (2.0 * math.pi / length)


def phase_constants(length):
    y_angle = angles(np.arange(MY) - MY // 2, length)
    z_angle = angles(np.arange(MZ), length)
    rounded = lambda v: v.astype(np.float32).astype(ml_dtypes.bfloat16).astype(np.float64)
    cz, sz = rounded(np.cos(z_angle)), rounded(-np.sin(z_angle))
    cy, sy = np.cos(y_angle), -np.sin(y_angle)
    both = lambda a, b: (a[:, None, :, None] * b[None, :, None, :]).reshape(MY * MZ, length * length)
    fwd = np.concatenate([both(cy, cz) - both(sy, sz), both(sy, cz) + both(cy, sz)], axis=0)
    fwd = np.concatenate(split_bf16(fwd), axis=0)
    cz, sz = np.cos(z_angle), np.sin(z_angle)
    cy, sy = np.cos(y_angle), np.sin(y_angle)
    inv = np.concatenate([both(cy, cz) - both(sy, sz), -(both(sy, cz) + both(cy, sz))], axis=0).T
    high, low = split_bf16(inv)
    pad = np.zeros((length * length, 128 - 4 * high.shape[1]), ml_dtypes.bfloat16)
    inv = np.concatenate([high, low, high, low, pad], axis=1)
    x_angle = angles(np.arange(MX) - MX // 2, length).T
    xtab = np.stack([np.cos(x_angle), np.sin(x_angle)], axis=2).astype(np.float32)
    return fwd, inv, xtab.reshape(-1)


def scalar_places(slots):
    return dict(count=slots, total=slots + 1, shard=slots + 2, first=slots + 3, partner=slots + 4)


def combine_planes(q_ref, xtab_ref, cell0, shard, planes, scale, store):
    for d in range(MX):
        i = lax.rem(shard + d, MX)
        re = jnp.zeros((8, 128), f32)
        im = jnp.zeros((8, 128), f32)
        for a in range(planes):
            at = ((cell0 + a) * MX + i) * 2
            c = xtab_ref[at]
            s = xtab_ref[at + 1]
            q_re = q_ref[a, 0:8, :]
            q_im = q_ref[a, 8:16, :]
            re = re + (q_re * c + q_im * s)
            im = im + (q_im * c - q_re * s)
        store(d, re * scale, im * scale)


def forward_kernel(
    slots, base, sends, planes, step_planes, scale, meta_ref, xtab_ref, f_ref, basis_ref, *rest
):
    if sends:
        t_ref, outs, send_ref, t_out_ref, q_ref = rest[0], rest[1 : MX + 1], *rest[MX + 1 :]
    else:
        given, outs, q_ref = rest[:MX], rest[MX : 2 * MX], rest[2 * MX]
    place = scalar_places(slots)
    g, blk = pl.program_id(0), pl.program_id(1)
    live = base + g < meta_ref[place["count"]]
    row = pl.multiple_of(g * 16, 16)

    if not sends:

        @pl.when((g == 0) & (blk == 0))
        def _():
            rows = given[0].shape[0]
            for d in range(MX):
                outs[d][rows : 2 * rows, :] = given[d][...]

    @pl.when(live)
    def _():
        cells = f_ref.shape[3] * f_ref.shape[4]
        for p in range(step_planes):
            field = f_ref[0, 0, p].reshape(cells, 128)
            part = jnp.dot(basis_ref[...], field, preferred_element_type=f32)
            q_ref[blk * step_planes + p] = part[0:16] + part[16:32]
            if sends:
                send_ref[0, p] = f_ref[0, 0, p]
        if sends:

            @pl.when(blk == 0)
            def _():
                t_out_ref[0] = t_ref[0, 0]

        @pl.when(blk == planes // step_planes - 1)
        def _():
            def store(d, re, im):
                outs[d][pl.ds(row, 8), :] = re
                outs[d][pl.ds(row + 8, 8), :] = im

            combine_planes(
                q_ref, xtab_ref, meta_ref[place["first"]], meta_ref[place["shard"]], planes, scale, store
            )

    @pl.when(jnp.logical_not(live) & (blk == 0))
    def _():
        for out in outs:
            out[pl.ds(row, 16), :] = jnp.zeros((16, 128), f32)


def shared_live(slots, kept, blocks, count, partner, g, blk):
    return (kept + g < count) & ((g > 0) | ((blk == blocks - 1) & (partner <= 1)))


def backward_kernel(
    slots, own, planes, step_planes, rows_step, scale, meta_ref, xtab_ref, f_ref, t_ref, *rest
):
    specs = rest[:MX]
    w_ref, proj_ref, inv_ref, basis_ref, eye_ref, ones_ref = rest[MX : MX + 6]
    rest = rest[MX + 6 :]
    if not own:
        given, rest = rest[:MX], rest[MX:]
    outs = rest[:MX]
    rhs_ref, pre_ref, slope_ref, both_ref, d_ref, total_ref, q_ref, t16_ref, spec_ref, field_ref, line_ref, near_ref = rest[MX:]
    place = scalar_places(slots)
    kept = slots - 3
    g, blk = pl.program_id(0), pl.program_id(1)
    blocks = planes // step_planes
    count, partner = meta_ref[place["count"]], meta_ref[place["partner"]]
    if own:
        some = g < count
        away = (g >= kept) & shared_live(slots, kept, blocks, count, partner, g - kept, blk)
        live = some & jnp.logical_not(away)
        positions, spec_row, out_row = kept + 1, g * 16, g * 16
        plane_of = lambda p: f_ref[0, 0, p].reshape(cells, 128)
        lines_of = lambda: t_ref[0, 0].astype(f32)
    else:
        some = kept + g < partner
        live = shared_live(slots, kept, blocks, partner, count, g, blk)
        positions, spec_row, out_row = 3, (kept + g) * 16, (kept + 1 + g) * 16
        plane_of = lambda p: f_ref[0, p].reshape(cells, 128)
        lines_of = lambda: t_ref[0].astype(f32)
    row = pl.multiple_of(out_row, 16)
    shard = meta_ref[place["shard"]]
    cell0 = meta_ref[place["first"]]
    cells = inv_ref.shape[0]
    third = cells // 3
    half = third // 2
    unroll = step_planes

    grids = jnp.full((1, 128), meta_ref[place["total"]].astype(f32), f32)
    root = lax.rsqrt(grids)
    root = root * (1.5 - 0.5 * grids * root * root)

    @pl.when((g == 0) & (blk == 0))
    def _():
        total_ref[...] = jnp.zeros_like(total_ref)
        for n in range(2):
            rhs_ref[n, 0:128, :] = w_ref[...]
            rhs_ref[n, 128:256, :] = jnp.zeros((128, 128), bf16)
        if not own:
            rows = (kept + 1) * 16
            for d in range(MX):
                outs[d][0:rows, :] = given[d][0:rows, :]

    @pl.when(some & (blk == 0))
    def _():
        q_ref[...] = jnp.zeros_like(q_ref)
        lines = lines_of() * root[:, 0:1]
        high = lines.astype(bf16).astype(f32)
        low = lines - high
        early = lax.broadcasted_iota(jnp.int32, (planes, 128), 1) < 64
        for at in range(0, cells, 128):
            part_h, part_l = high[:, at : at + 128], low[:, at : at + 128]
            turned_h, turned_l = pltpu.roll(part_h, 64, 1), pltpu.roll(part_l, 64, 1)
            both = (jnp.where(early, part_h, turned_l), jnp.where(early, turned_h, part_l))
            for n in range(2):
                for a in range(planes):
                    line = jnp.broadcast_to(both[n][a : a + 1, :], (16, 128))
                    t16_ref[a, :, 2 * at + 128 * n : 2 * at + 128 * (n + 1)] = line.astype(bf16)
        for d in range(MX):
            spec_ref[d] = specs[d][pl.ds(pl.multiple_of(spec_row, 16), 16), :].astype(f32)

    @pl.when(live)
    def _():
        gate = proj_ref[...] * root * 0.5
        edge = proj_ref[...] * root * inv_root_two_pi

        def first_rows(a, rhs):
            re = jnp.zeros((8, 128), f32)
            im = jnp.zeros((8, 128), f32)
            for d in range(MX):
                i = lax.rem(shard - d + MX, MX)
                at = ((cell0 + a) * MX + i) * 2
                c = xtab_ref[at]
                s = xtab_ref[at + 1]
                s_re = spec_ref[d, 0:8, :]
                s_im = spec_ref[d, 8:16, :]
                re = re + (s_re * c - s_im * s)
                im = im + (s_re * s + s_im * c)
            first = jnp.concatenate([re, im], axis=0) * scale
            high = first.astype(bf16)
            low = (first - high.astype(f32)).astype(bf16)
            rhs[128:144, :] = high
            rhs[144:160, :] = high
            rhs[160:176, :] = low
            rhs[176:192, :] = low

        def planes_together(n, carry):
            units = [(u, k) for u in range(unroll) for k in range(3)]
            for u in range(unroll):
                field_ref[u] = plane_of(n * unroll + u)
                line_ref[u] = t16_ref[blk * step_planes + n * unroll + u]

            def before(s, r0):
                u, k = units[s]
                rhs = rhs_ref.at[u % 2]
                if k == 0 and r0 == 0:
                    first_rows(blk * step_planes + n * unroll + u, rhs)
                part = slice(k * third + r0, k * third + r0 + half)
                lhs = jnp.concatenate([field_ref[u, part, :], inv_ref[part, :]], axis=1)
                pre_ref[s % 2, r0 : r0 + half, :] = jnp.dot(lhs, rhs[...], preferred_element_type=f32)

            def elementwise(s, r0):
                u, k = units[s]
                rows = slice(r0, r0 + rows_step)
                pre = pre_ref[s % 2, rows, :]
                bell = jnp.exp2(pre * pre * (-half_log2e))
                gated = (1.0 + lax.erf(pre * root_half)) * gate
                slope_ref[s % 2, rows, :] = gated + pre * bell * edge
                both_ref[s % 2, rows, 0:128] = (pre * gated).astype(bf16)
                for r1 in range(r0, r0 + rows_step, 16):
                    at = 2 * (k * third + r1 - r1 % 64)
                    line = line_ref[u, :, at : at + 128]
                    both_ref[s % 2, r1 : r1 + 16, 128:256] = line * eye_ref[r1 % 64 : r1 % 64 + 16, :]

            def after(s, r0):
                rows = slice(r0, r0 + half)
                resid = jnp.dot(both_ref[s % 2, rows, :], ones_ref[...], preferred_element_type=f32)
                d_ref[s % 2, rows, :] = (resid * slope_ref[s % 2, rows, :]).astype(bf16)

            def last(s):
                u, k = units[s]
                part = slice(k * third, (k + 1) * third)
                lhs = jnp.concatenate([field_ref[u, part, :].T, basis_ref[:, part]], axis=0)
                sums = jnp.dot(lhs, d_ref[s % 2], preferred_element_type=f32)
                total_ref[...] += sums[0:128]
                back = sums[128:144] + sums[144:160]
                near_ref[u] = back if k == 0 else near_ref[u] + back

            pieces = third // rows_step
            for s in range(len(units) + 3):
                for piece in range(pieces):
                    r0 = piece * rows_step
                    if s < len(units) and r0 % half == 0:
                        before(s, r0)
                    if 0 <= s - 2 < len(units) and r0 % half == 0:
                        after(s - 2, r0)
                    if 0 <= s - 3 and piece == pieces // 2 - 1:
                        last(s - 3)
                    if 0 <= s - 1 < len(units):
                        elementwise(s - 1, r0)
            for u in range(unroll):
                q_ref[blk * step_planes + n * unroll + u] = near_ref[u]
            return carry

        lax.fori_loop(0, step_planes // unroll, planes_together, 0)

    @pl.when(some & (blk == blocks - 1))
    def _():
        def store(d, re, im):
            outs[d][pl.ds(row, 8), :] = re
            outs[d][pl.ds(row + 8, 8), :] = im

        combine_planes(q_ref, xtab_ref, cell0, shard, planes, scale, store)

    @pl.when(jnp.logical_not(some) & (blk == 0))
    def _():
        for out in outs:
            out[pl.ds(row, 16), :] = jnp.zeros((16, 128), f32)

    @pl.when((g == positions - 1) & (blk == blocks - 1))
    def _():
        size = 128 // MX
        for d in range(MX):
            i = lax.rem(shard + d, MX)
            at = pl.multiple_of(i * size, size)
            part = total_ref[pl.ds(at, size), :]
            if not own:
                part = part + given[d][(kept + 1) * 16 : (kept + 1) * 16 + size, :]
            rows = outs[d].shape[0]
            outs[d][rows - size : rows, :] = part


def mix_kernel(slots, per, shards, *refs):
    parts = refs[:shards]
    w_ref, coeff_out, spec_out, c_ref, s_ref = refs[shards:]
    total = parts[0][...]
    for part in parts[1:]:
        total = total + part[...]
    coeff = total.astype(bf16)
    coeff_out[...] = coeff
    c_ref[...] = coeff.astype(f32)
    for m in range(per):
        re_rows = pl.ds(m, slots, stride=2 * per)
        im_rows = pl.ds(per + m, slots, stride=2 * per)
        re = c_ref[re_rows, :].astype(bf16)
        im = c_ref[im_rows, :].astype(bf16)
        weight = w_ref[m].reshape(256, 128)
        s_ref[re_rows, :] = jnp.dot(
            jnp.concatenate([re, -im], axis=1), weight, preferred_element_type=f32
        )
        s_ref[im_rows, :] = jnp.dot(
            jnp.concatenate([im, re], axis=1), weight, preferred_element_type=f32
        )
    spec_out[...] = s_ref[...].astype(bf16)


def sum_kernel(count, *refs):
    total = refs[0][...]
    for part in refs[1:count]:
        total = total + part[...]
    refs[count][...] = total


def local_sum_kernel(count, rows, *refs):
    size = refs[count].shape[0]
    total = refs[0][rows : rows + size, :]
    for part in refs[1:count]:
        total = total + part[rows : rows + size, :]
    refs[count][...] = total


def weight_kernel(lanes, slots, per, lane_ref, *refs):
    coeffs, backs = refs[:lanes], refs[lanes : 2 * lanes]
    out_ref, all_ref, c_ref, b_ref = refs[2 * lanes :]
    each = 2 * per
    kept = slots - 3
    rows = (slots + 1) * each
    for n in range(lanes):
        coeff = coeffs[n][...].astype(f32)
        c_ref[n * rows : n * rows + (kept + 1) * each, :] = coeff[0 : (kept + 1) * each]
        all_ref[n] = coeff[kept * each :]
        b_ref[n * rows : (n + 1) * rows, :] = backs[n][0:rows, :]
    for n in range(lanes):
        source = lax.rem(lane_ref[0] - n + lanes, lanes)
        other = lax.rem(n - 1 + 2 * lax.rem(source, 2) + lanes, lanes)
        c_ref[n * rows + (kept + 1) * each : (n + 1) * rows, :] = all_ref[other]
    slots = slots + 1
    for m in range(per):
        re_rows = pl.ds(m, lanes * slots, stride=2 * per)
        im_rows = pl.ds(per + m, lanes * slots, stride=2 * per)
        c_re = c_ref[re_rows, :].astype(bf16)
        c_im = c_ref[im_rows, :].astype(bf16)
        b_re = b_ref[re_rows, :]
        b_im = b_ref[im_rows, :]
        left = jnp.concatenate([c_re, c_im], axis=0)
        right = jnp.concatenate(
            [jnp.concatenate([b_re, b_im], axis=1), jnp.concatenate([b_im, -b_re], axis=1)], axis=0
        )
        high = right.astype(bf16)
        low = (right - high.astype(f32)).astype(bf16)
        left = jnp.concatenate([left, left], axis=0)
        right = jnp.concatenate([high, low], axis=0)
        grad = lax.dot_general(
            left, right, (((0,), (0,)), ((), ())), preferred_element_type=f32
        )
        out_ref[m, 0] = grad[:, 0:128]
        out_ref[m, 1] = grad[:, 128:256]


def place_kernel(shards, meta_ref, *refs):
    out_ref = refs[shards]
    size = refs[0].shape[0]
    for d in range(shards):
        i = lax.rem(meta_ref[0] - d + shards, shards)
        out_ref[pl.ds(pl.multiple_of(i * size, size), size), :] = refs[d][...]


def whole_vmem(count):
    return [pl.BlockSpec(memory_space=pltpu.VMEM)] * count


def params(limit=VMEM_BYTES):
    return pltpu.CompilerParams(vmem_limit_bytes=limit)


def rotations(value_of, axis, size):
    got = [value_of(0)]
    for d in range(1, size):
        perm = [(s, (s + d) % size) for s in range(size)]
        got.append(lax.ppermute(value_of(d), axis, perm))
    return got


def body(lanes, shards, fields, targets, lists, counts, spectral_w, local_w, proj):
    _, slots, planes, grid_len, _, width = fields.shape
    per = MODES // shards
    split = shards // MX
    cells = grid_len * grid_len
    step_planes = max(n for n in (1, 2, 3, 4) if planes % n == 0)
    blocks = planes // step_planes
    basis, inverse, xtab = phase_constants(grid_len)
    lane = lax.axis_index("dp").astype(jnp.int32)
    shard = lax.axis_index("fsdp").astype(jnp.int32)
    turn = shard if split == 1 else jnp.int32(0)
    meta = jnp.concatenate(
        [
            lists[0],
            counts[lane][None],
            jnp.sum(counts)[None],
            turn[None],
            (shard * planes)[None],
            counts[lane ^ 1][None],
        ]
    ).astype(jnp.int32)
    place = scalar_places(slots)

    kept = slots - 3

    def field_block(base):
        def block(g, blk, meta_ref, xtab_ref):
            count = meta_ref[place["count"]]
            slot = meta_ref[jnp.minimum(base + g, count - 1)]
            return (0, slot, jnp.where(base + g < count, blk, blocks - 1), 0, 0, 0)

        return pl.BlockSpec((1, 1, step_planes, grid_len, grid_len, width), block)

    def target_block(base):
        def block(g, blk, meta_ref, xtab_ref):
            count = meta_ref[place["count"]]
            return (0, meta_ref[jnp.minimum(base + g, count - 1)], 0, 0)

        return pl.BlockSpec((1, 1, planes, cells), block)

    def shared_item(g, blk):
        return jnp.maximum(g * blocks + blk - (blocks - 1), 0)

    def fixed(*shape):
        return pl.BlockSpec(shape, lambda g, blk, meta_ref, xtab_ref: (0,) * len(shape))

    items = 2 * blocks + 1
    shared_fields = pl.BlockSpec(
        (1, step_planes, grid_len, grid_len, width),
        lambda g, blk, meta_ref, xtab_ref: (shared_item(g, blk), 0, 0, 0, 0),
    )
    shared_targets = pl.BlockSpec((1, planes, cells), lambda g, blk, meta_ref, xtab_ref: (g, 0, 0))
    part_rows = slots * 16
    forward_scale = float(grid_len) ** (-1.5)
    *late_parts, sent_fields, sent_targets = pl.pallas_call(
        functools.partial(forward_kernel, slots, kept, True, planes, step_planes, forward_scale),
        grid_spec=pltpu.PrefetchScalarGridSpec(
            num_scalar_prefetch=2,
            grid=(3, blocks),
            in_specs=[field_block(kept), fixed(*basis.shape), target_block(kept)],
            out_specs=[fixed(3 * 16, width)] * MX + [shared_fields, shared_targets],
            scratch_shapes=[pltpu.VMEM((planes, 16, width), f32)],
        ),
        out_shape=[jax.ShapeDtypeStruct((3 * 16, width), f32)] * MX
        + [
            jax.ShapeDtypeStruct((items, step_planes, grid_len, grid_len, width), bf16),
            jax.ShapeDtypeStruct((3, planes, cells), bf16),
        ],
        compiler_params=params(),
        name="forward_shared",
    )(meta, xtab, fields, basis, targets)
    swap = lambda x: lax.ppermute(x, "dp", [(s, s ^ 1) for s in range(lanes)])
    came_fields = swap(sent_fields)
    came_targets = swap(sent_targets)
    parts = pl.pallas_call(
        functools.partial(forward_kernel, slots, 0, False, planes, step_planes, forward_scale),
        grid_spec=pltpu.PrefetchScalarGridSpec(
            num_scalar_prefetch=2,
            grid=(3, blocks),
            in_specs=[field_block(0), fixed(*basis.shape)] + [fixed(3 * 16, width)] * MX,
            out_specs=[fixed(part_rows, width)] * MX,
            scratch_shapes=[pltpu.VMEM((planes, 16, width), f32)],
        ),
        out_shape=[jax.ShapeDtypeStruct((part_rows, width), f32)] * MX,
        compiler_params=params(),
        cost_estimate=pl.CostEstimate(
            flops=3 * planes * cells * 256 * 256,
            bytes_accessed=3 * planes * cells * width * 2,
            transcendentals=0,
        ),
        name="forward_modes",
    )(meta, xtab, fields, basis, *late_parts)

    def shard_parts(pieces, count):
        if split == 1:
            return lambda d: pieces[d]
        stacked = jnp.stack(pieces).reshape(MX, count, 2, split, per, width)
        stacked = jnp.moveaxis(stacked, 3, 1).reshape(shards, count * 2 * per, width)
        return lambda d: lax.dynamic_index_in_dim(stacked, (shard + d) % shards, 0, keepdims=False)

    def mode_parts(pieces, count):
        if split == 1:
            return pieces
        stacked = jnp.stack(pieces)[(shard - jnp.arange(shards)) % shards]
        stacked = stacked.reshape(MX, split, count, 2, per, width)
        stacked = jnp.moveaxis(stacked, 1, 3).reshape(MX, count * 16, width)
        return [stacked[(-d) % MX] for d in range(MX)]

    came = rotations(shard_parts(parts, slots), "fsdp", shards)
    own_rows = slots * 2 * per
    coeff, own_spectrum = pl.pallas_call(
        functools.partial(mix_kernel, slots, per, shards),
        in_specs=whole_vmem(shards + 1),
        out_specs=whole_vmem(2),
        out_shape=[jax.ShapeDtypeStruct((own_rows, width), bf16)] * 2,
        scratch_shapes=[pltpu.VMEM((own_rows, width), f32)] * 2,
        compiler_params=params(),
        name="mix_modes",
    )(*came, spectral_w)
    spectrum = mode_parts(rotations(lambda d: own_spectrum, "fsdp", shards), slots)
    coeffs = rotations(lambda d: coeff, "dp", lanes)

    local_rows = width // MX
    eye = np.tile(np.eye(64, dtype=ml_dtypes.bfloat16), (1, 2))
    ones = np.ones((128, 128), ml_dtypes.bfloat16)
    ones = np.concatenate([ones, -ones], axis=0)

    def own_block(g, blk, meta_ref, xtab_ref):
        count, partner = meta_ref[place["count"]], meta_ref[place["partner"]]
        slot = meta_ref[jnp.minimum(g, count - 1)]
        away = (g >= kept) & shared_live(slots, kept, blocks, count, partner, g - kept, blk)
        blk = jnp.where(away, max(blocks - 2, 0), blk)
        return (0, slot, jnp.where(g < count, blk, blocks - 1), 0, 0, 0)

    def came_item(g, blk, meta_ref):
        some = kept < meta_ref[place["partner"]]
        return jnp.where(some, shared_item(g, blk), 0), jnp.where(some, g, 0)

    came_block = pl.BlockSpec(
        (1, step_planes, grid_len, grid_len, width),
        lambda g, blk, meta_ref, xtab_ref: (came_item(g, blk, meta_ref)[0], 0, 0, 0, 0),
    )
    came_lines = pl.BlockSpec(
        (1, planes, cells), lambda g, blk, meta_ref, xtab_ref: (came_item(g, blk, meta_ref)[1], 0, 0)
    )

    def backward(own, fields_, targets_, spectrum_, given):
        positions = kept + 1 if own else 3
        rows = (kept + 1 if own else slots + 1) * 16 + local_rows
        own_fields = pl.BlockSpec((1, 1, step_planes, grid_len, grid_len, width), own_block)
        return pl.pallas_call(
            functools.partial(
                backward_kernel, slots, own, planes, step_planes, 128, float(MODES) ** (-0.5)
            ),
            grid_spec=pltpu.PrefetchScalarGridSpec(
                num_scalar_prefetch=2,
                grid=(positions, blocks),
                in_specs=([own_fields, target_block(0)] if own else [came_block, came_lines])
                + [fixed(part_rows, width)] * MX
                + [
                    fixed(width, width),
                    fixed(1, width),
                    fixed(*inverse.shape),
                    fixed(*basis.shape),
                    fixed(*eye.shape),
                    fixed(*ones.shape),
                ]
                + [fixed(*g.shape) for g in given],
                out_specs=[fixed(rows, width)] * MX,
                scratch_shapes=[
                    pltpu.VMEM((2, 256, width), bf16),
                    pltpu.VMEM((2, cells // 3, width), f32),
                    pltpu.VMEM((2, cells // 3, width), f32),
                    pltpu.VMEM((2, cells // 3, 2 * width), bf16),
                    pltpu.VMEM((2, cells // 3, width), bf16),
                    pltpu.VMEM((width, width), f32),
                    pltpu.VMEM((planes, 16, width), f32),
                    pltpu.VMEM((planes, 16, 2 * cells), bf16),
                    pltpu.VMEM((MX, 16, width), f32),
                    pltpu.VMEM((step_planes, cells, width), bf16),
                    pltpu.VMEM((step_planes, 16, 2 * cells), bf16),
                    pltpu.VMEM((step_planes, 16, width), f32),
                ],
            ),
            out_shape=[jax.ShapeDtypeStruct((rows, width), f32)] * MX,
            compiler_params=params(LARGE_VMEM_BYTES),
            cost_estimate=pl.CostEstimate(
                flops=4 * positions * planes * cells * 256 * 256,
                bytes_accessed=positions * planes * cells * width * 2,
                transcendentals=0,
            ),
            name="backward_own" if own else "backward_shared",
        )(
            meta, xtab, fields_, targets_, *spectrum_, local_w, proj.reshape(1, width),
            inverse, basis, eye, ones, *given,
        )

    came_spectrum = [swap(piece) for piece in spectrum]
    own_results = backward(True, fields, targets, spectrum, [])
    results = backward(False, came_fields, came_targets, came_spectrum, own_results)
    places = slots + 1
    part_rows = places * 16
    place_rows = places * 2 * per

    if split == 1:
        chunk = lambda d: results[d]
    else:
        backs = shard_parts([r[:part_rows] for r in results], places)
        local = jnp.concatenate([r[part_rows:] for r in results], axis=0)
        rows = width // shards
        chunk = lambda d: jnp.concatenate(
            [backs(d), lax.dynamic_slice_in_dim(local, (shard + d) % shards * rows, rows, 0)], axis=0
        )
    came = rotations(chunk, "fsdp", shards)
    own_sum = pl.pallas_call(
        functools.partial(sum_kernel, shards),
        in_specs=whole_vmem(shards),
        out_specs=pl.BlockSpec(memory_space=pltpu.VMEM),
        out_shape=jax.ShapeDtypeStruct(came[0].shape, f32),
        compiler_params=params(),
        name="sum_shards",
    )(*came)
    sums = rotations(lambda d: own_sum, "dp", lanes)
    own_local = pl.pallas_call(
        functools.partial(local_sum_kernel, lanes, place_rows),
        in_specs=whole_vmem(lanes),
        out_specs=pl.BlockSpec(memory_space=pltpu.VMEM),
        out_shape=jax.ShapeDtypeStruct((width // shards, width), f32),
        compiler_params=params(),
        name="sum_local",
    )(*sums)
    locals_ = rotations(lambda d: own_local, "fsdp", shards)
    grad_spectral = pl.pallas_call(
        functools.partial(weight_kernel, lanes, slots, per),
        in_specs=[pl.BlockSpec(memory_space=pltpu.SMEM)] + whole_vmem(2 * lanes),
        out_specs=pl.BlockSpec(memory_space=pltpu.VMEM),
        out_shape=jax.ShapeDtypeStruct((per, 2, width, width), f32),
        scratch_shapes=[pltpu.VMEM((lanes, 3 * 2 * per, width), f32)]
        + [pltpu.VMEM((lanes * place_rows, width), f32)] * 2,
        compiler_params=params(),
        cost_estimate=pl.CostEstimate(
            flops=2 * per * 256 * 128 * 256, bytes_accessed=2 * per * 2 * width * width * 4, transcendentals=0
        ),
        name="weight_grad",
    )(lane[None], *coeffs, *sums)
    grad_local = pl.pallas_call(
        functools.partial(place_kernel, shards),
        in_specs=[pl.BlockSpec(memory_space=pltpu.SMEM)] + whole_vmem(shards),
        out_specs=pl.BlockSpec(memory_space=pltpu.VMEM),
        out_shape=jax.ShapeDtypeStruct((width, width), f32),
        compiler_params=params(),
        name="place_local",
    )(shard[None], *locals_)
    return (grad_spectral, grad_local)


def solution(mesh):
    return jax.shard_map(
        functools.partial(body, mesh.shape["dp"], mesh.shape["fsdp"]),
        mesh=mesh,
        in_specs=(
            P("dp", None, "fsdp", None, None, None),
            P("dp", None, "fsdp", None),
            P("dp", None),
            P(),
            P("fsdp", None, None, None),
            P(),
            P(),
        ),
        out_specs=(P("fsdp", None, None, None), P()),
        check_vma=False,
    )
```

```python
import functools
import math

import jax
import jax.numpy as jnp
import ml_dtypes
import numpy as np
from jax import lax
from jax.experimental import pallas as pl
from jax.experimental.pallas import tpu as pltpu
from jax.sharding import PartitionSpec as P

MX = 4
MY = 4
MZ = 2
MODES = MX * MY * MZ
VMEM_BYTES = 40 * 1024 * 1024
LARGE_VMEM_BYTES = 56 * 1024 * 1024
f32 = jnp.float32
bf16 = jnp.bfloat16
inv_root_two_pi = 0.3989422804014327
half_log2e = 0.7213475204444817
root_half = 0.7071067811865476


def split_bf16(values):
    high = values.astype(ml_dtypes.bfloat16)
    low = (values - high.astype(np.float64)).astype(ml_dtypes.bfloat16)
    return high, low


def angles(mode_ids, length):
    product = np.outer(mode_ids, np.arange(length)) % length
    return product * (2.0 * math.pi / length)


def phase_constants(length):
    y_angle = angles(np.arange(MY) - MY // 2, length)
    z_angle = angles(np.arange(MZ), length)
    rounded = lambda v: v.astype(np.float32).astype(ml_dtypes.bfloat16).astype(np.float64)
    cz, sz = rounded(np.cos(z_angle)), rounded(-np.sin(z_angle))
    cy, sy = np.cos(y_angle), -np.sin(y_angle)
    both = lambda a, b: (a[:, None, :, None] * b[None, :, None, :]).reshape(MY * MZ, length * length)
    fwd = np.concatenate([both(cy, cz) - both(sy, sz), both(sy, cz) + both(cy, sz)], axis=0)
    fwd = np.concatenate(split_bf16(fwd), axis=0)
    cz, sz = np.cos(z_angle), np.sin(z_angle)
    cy, sy = np.cos(y_angle), np.sin(y_angle)
    inv = np.concatenate([both(cy, cz) - both(sy, sz), -(both(sy, cz) + both(cy, sz))], axis=0).T
    high, low = split_bf16(inv)
    pad = np.zeros((length * length, 128 - 4 * high.shape[1]), ml_dtypes.bfloat16)
    inv = np.concatenate([high, low, high, low, pad], axis=1)
    x_angle = angles(np.arange(MX) - MX // 2, length).T
    xtab = np.stack([np.cos(x_angle), np.sin(x_angle)], axis=2).astype(np.float32)
    return fwd, inv, xtab.reshape(-1)


def scalar_places(slots):
    return dict(count=slots, total=slots + 1, shard=slots + 2, first=slots + 3, partner=slots + 4)


def combine_planes(q_ref, xtab_ref, cell0, shard, planes, scale, store):
    for d in range(MX):
        i = lax.rem(shard + d, MX)
        re = jnp.zeros((8, 128), f32)
        im = jnp.zeros((8, 128), f32)
        for a in range(planes):
            at = ((cell0 + a) * MX + i) * 2
            c = xtab_ref[at]
            s = xtab_ref[at + 1]
            q_re = q_ref[a, 0:8, :]
            q_im = q_ref[a, 8:16, :]
            re = re + (q_re * c + q_im * s)
            im = im + (q_im * c - q_re * s)
        store(d, re * scale, im * scale)


def forward_kernel(
    slots, base, sends, planes, step_planes, scale, meta_ref, xtab_ref, f_ref, basis_ref, *rest
):
    if sends:
        t_ref, outs, send_ref, t_out_ref, q_ref = rest[0], rest[1 : MX + 1], *rest[MX + 1 :]
    else:
        given, outs, q_ref = rest[:MX], rest[MX : 2 * MX], rest[2 * MX]
    place = scalar_places(slots)
    g, blk = pl.program_id(0), pl.program_id(1)
    live = base + g < meta_ref[place["count"]]
    row = pl.multiple_of(g * 16, 16)

    if not sends:

        @pl.when((g == 0) & (blk == 0))
        def _():
            rows = given[0].shape[0]
            for d in range(MX):
                outs[d][rows : 2 * rows, :] = given[d][...]

    @pl.when(live)
    def _():
        cells = f_ref.shape[3] * f_ref.shape[4]
        for p in range(step_planes):
            field = f_ref[0, 0, p].reshape(cells, 128)
            part = jnp.dot(basis_ref[...], field, preferred_element_type=f32)
            q_ref[blk * step_planes + p] = part[0:16] + part[16:32]
            if sends:
                send_ref[0, p] = f_ref[0, 0, p]
        if sends:

            @pl.when(blk == 0)
            def _():
                t_out_ref[0] = t_ref[0, 0]

        @pl.when(blk == planes // step_planes - 1)
        def _():
            def store(d, re, im):
                outs[d][pl.ds(row, 8), :] = re
                outs[d][pl.ds(row + 8, 8), :] = im

            combine_planes(
                q_ref, xtab_ref, meta_ref[place["first"]], meta_ref[place["shard"]], planes, scale, store
            )

    @pl.when(jnp.logical_not(live) & (blk == 0))
    def _():
        for out in outs:
            out[pl.ds(row, 16), :] = jnp.zeros((16, 128), f32)


def shared_live(slots, kept, blocks, count, partner, g, blk):
    return (kept + g < count) & ((g > 0) | ((blk == blocks - 1) & (partner <= 1)))


def backward_kernel(
    slots, own, planes, step_planes, rows_step, scale, meta_ref, xtab_ref, f_ref, t_ref, *rest
):
    specs = rest[:MX]
    w_ref, proj_ref, inv_ref, basis_ref, eye_ref, wide_eye_ref, ones_ref = rest[MX : MX + 7]
    rest = rest[MX + 7 :]
    if not own:
        given, rest = rest[:MX], rest[MX:]
    outs = rest[:MX]
    rhs_ref, pre_ref, slope_ref, both_ref, resid_ref, d_ref, total_ref, q_ref, t16_ref, spec_ref, field_ref, line_ref, near_ref, far_t_ref, far_line_ref = rest[MX:]
    place = scalar_places(slots)
    kept = slots - 3
    g, blk = pl.program_id(0), pl.program_id(1)
    blocks = planes // step_planes
    count, partner = meta_ref[place["count"]], meta_ref[place["partner"]]
    if own:
        some = g < count
        away = (g >= kept) & shared_live(slots, kept, blocks, count, partner, g - kept, blk)
        live = some & jnp.logical_not(away)
        positions, spec_row, out_row = kept + 1, g * 16, g * 16
        plane_of = lambda p: f_ref[0, 0, p].reshape(cells, 128)
        lines_of = lambda: t_ref[0, 0].astype(f32)
    else:
        some = kept + g < partner
        live = shared_live(slots, kept, blocks, partner, count, g, blk)
        positions, spec_row, out_row = 3, (kept + g) * 16, (kept + 1 + g) * 16
        plane_of = lambda p: f_ref[0, p].reshape(cells, 128)
        lines_of = lambda: t_ref[0].astype(f32)
    row = pl.multiple_of(out_row, 16)
    shard = meta_ref[place["shard"]]
    cell0 = meta_ref[place["first"]]
    cells = inv_ref.shape[0]
    third = cells // 3
    half = third // 2
    unroll = step_planes

    grids = jnp.full((1, 128), meta_ref[place["total"]].astype(f32), f32)
    root = lax.rsqrt(grids)
    root = root * (1.5 - 0.5 * grids * root * root)

    @pl.when((g == 0) & (blk == 0))
    def _():
        total_ref[...] = jnp.zeros_like(total_ref)
        for n in range(2):
            rhs_ref[n, 0:128, :] = w_ref[...]
            rhs_ref[n, 128:256, :] = jnp.zeros((128, 128), bf16)
        if not own:
            rows = (kept + 1) * 16
            for d in range(MX):
                outs[d][0:rows, :] = given[d][0:rows, :]

    @pl.when(some & (blk == 0))
    def _():
        q_ref[...] = jnp.zeros_like(q_ref)
        lines = lines_of() * root[:, 0:1]
        for a in range(planes):
            far_t_ref[a] = jnp.broadcast_to(lines[a : a + 1, :], (8, cells))
        high = lines.astype(bf16).astype(f32)
        low = lines - high
        early = lax.broadcasted_iota(jnp.int32, (planes, 128), 1) < 64
        for at in range(0, cells, 128):
            part_h, part_l = high[:, at : at + 128], low[:, at : at + 128]
            turned_h, turned_l = pltpu.roll(part_h, 64, 1), pltpu.roll(part_l, 64, 1)
            both = (jnp.where(early, part_h, turned_l), jnp.where(early, turned_h, part_l))
            for n in range(2):
                for a in range(planes):
                    line = jnp.broadcast_to(both[n][a : a + 1, :], (16, 128))
                    t16_ref[a, :, 2 * at + 128 * n : 2 * at + 128 * (n + 1)] = line.astype(bf16)
        for d in range(MX):
            spec_ref[d] = specs[d][pl.ds(pl.multiple_of(spec_row, 16), 16), :].astype(f32)

    @pl.when(live)
    def _():
        gate = proj_ref[...] * root * 0.5
        edge = proj_ref[...] * root * inv_root_two_pi

        def first_rows(a, rhs):
            re = jnp.zeros((8, 128), f32)
            im = jnp.zeros((8, 128), f32)
            for d in range(MX):
                i = lax.rem(shard - d + MX, MX)
                at = ((cell0 + a) * MX + i) * 2
                c = xtab_ref[at]
                s = xtab_ref[at + 1]
                s_re = spec_ref[d, 0:8, :]
                s_im = spec_ref[d, 8:16, :]
                re = re + (s_re * c - s_im * s)
                im = im + (s_re * s + s_im * c)
            first = jnp.concatenate([re, im], axis=0) * scale
            high = first.astype(bf16)
            low = (first - high.astype(f32)).astype(bf16)
            rhs[128:144, :] = high
            rhs[144:160, :] = high
            rhs[160:176, :] = low
            rhs[176:192, :] = low

        def planes_together(n, carry):
            units = [(u, k) for u in range(unroll) for k in range(3)]
            for u in range(unroll):
                field_ref[u] = plane_of(n * unroll + u)
                line_ref[u] = t16_ref[blk * step_planes + n * unroll + u]
                far_line_ref[u] = far_t_ref[blk * step_planes + n * unroll + u]

            def before(s, r0):
                u, k = units[s]
                rhs = rhs_ref.at[u % 2]
                if k == 0 and r0 == 0:
                    first_rows(blk * step_planes + n * unroll + u, rhs)
                part = slice(k * third + r0, k * third + r0 + half)
                lhs = jnp.concatenate([field_ref[u, part, :], inv_ref[part, :]], axis=1)
                pre_ref[s % 2, r0 : r0 + half, :] = jnp.dot(lhs, rhs[...], preferred_element_type=f32)

            def elementwise(s, r0):
                u, k = units[s]
                rows = slice(r0, r0 + rows_step)
                pre = pre_ref[s % 2, rows, :]
                bell = jnp.exp2(pre * pre * (-half_log2e))
                gated = (1.0 + lax.erf(pre * root_half)) * gate
                slope_ref[s % 2, rows, :] = gated + pre * bell * edge
                active = pre * gated
                if r0 >= half:
                    at = k * third + r0
                    line = far_line_ref[u, :, at : at + 128]
                    wanted = jnp.concatenate([line] * (rows_step // 8), axis=0)
                    resid = jnp.sum(active - wanted * wide_eye_ref[...], axis=1, keepdims=True)
                    resid_ref[s % 2, r0 - half : r0 - half + rows_step, :] = jnp.broadcast_to(
                        resid, (rows_step, 128)
                    )
                    return
                both_ref[s % 2, rows, 0:128] = active.astype(bf16)
                for r1 in range(r0, r0 + rows_step, 16):
                    at = 2 * (k * third + r1 - r1 % 64)
                    line = line_ref[u, :, at : at + 128]
                    both_ref[s % 2, r1 : r1 + 16, 128:256] = line * eye_ref[r1 % 64 : r1 % 64 + 16, :]

            def after(s, r0):
                rows = slice(r0, r0 + half)
                if r0 >= half:
                    resid = resid_ref[s % 2]
                else:
                    resid = jnp.dot(both_ref[s % 2], ones_ref[...], preferred_element_type=f32)
                d_ref[s % 2, rows, :] = (resid * slope_ref[s % 2, rows, :]).astype(bf16)

            def last(s):
                u, k = units[s]
                part = slice(k * third, (k + 1) * third)
                lhs = jnp.concatenate([field_ref[u, part, :].T, basis_ref[:, part]], axis=0)
                sums = jnp.dot(lhs, d_ref[s % 2], preferred_element_type=f32)
                total_ref[...] += sums[0:128]
                back = sums[128:144] + sums[144:160]
                near_ref[u] = back if k == 0 else near_ref[u] + back

            pieces = third // rows_step
            for s in range(len(units) + 3):
                for piece in range(pieces):
                    r0 = piece * rows_step
                    if s < len(units) and r0 % half == 0:
                        before(s, r0)
                    if 0 <= s - 2 < len(units) and r0 % half == 0:
                        after(s - 2, r0)
                    if 0 <= s - 3 and piece == pieces // 2 - 1:
                        last(s - 3)
                    if 0 <= s - 1 < len(units):
                        elementwise(s - 1, r0)
            for u in range(unroll):
                q_ref[blk * step_planes + n * unroll + u] = near_ref[u]
            return carry

        lax.fori_loop(0, step_planes // unroll, planes_together, 0)

    @pl.when(some & (blk == blocks - 1))
    def _():
        def store(d, re, im):
            outs[d][pl.ds(row, 8), :] = re
            outs[d][pl.ds(row + 8, 8), :] = im

        combine_planes(q_ref, xtab_ref, cell0, shard, planes, scale, store)

    @pl.when(jnp.logical_not(some) & (blk == 0))
    def _():
        for out in outs:
            out[pl.ds(row, 16), :] = jnp.zeros((16, 128), f32)

    @pl.when((g == positions - 1) & (blk == blocks - 1))
    def _():
        size = 128 // MX
        for d in range(MX):
            i = lax.rem(shard + d, MX)
            at = pl.multiple_of(i * size, size)
            part = total_ref[pl.ds(at, size), :]
            if not own:
                part = part + given[d][(kept + 1) * 16 : (kept + 1) * 16 + size, :]
            rows = outs[d].shape[0]
            outs[d][rows - size : rows, :] = part


def mix_kernel(slots, per, shards, *refs):
    parts = refs[:shards]
    w_ref, coeff_out, spec_out, c_ref, s_ref = refs[shards:]
    total = parts[0][...]
    for part in parts[1:]:
        total = total + part[...]
    coeff = total.astype(bf16)
    coeff_out[...] = coeff
    c_ref[...] = coeff.astype(f32)
    for m in range(per):
        re_rows = pl.ds(m, slots, stride=2 * per)
        im_rows = pl.ds(per + m, slots, stride=2 * per)
        re = c_ref[re_rows, :].astype(bf16)
        im = c_ref[im_rows, :].astype(bf16)
        weight = w_ref[m].reshape(256, 128)
        s_ref[re_rows, :] = jnp.dot(
            jnp.concatenate([re, -im], axis=1), weight, preferred_element_type=f32
        )
        s_ref[im_rows, :] = jnp.dot(
            jnp.concatenate([im, re], axis=1), weight, preferred_element_type=f32
        )
    spec_out[...] = s_ref[...].astype(bf16)


def sum_kernel(count, *refs):
    total = refs[0][...]
    for part in refs[1:count]:
        total = total + part[...]
    refs[count][...] = total


def local_sum_kernel(count, rows, *refs):
    size = refs[count].shape[0]
    total = refs[0][rows : rows + size, :]
    for part in refs[1:count]:
        total = total + part[rows : rows + size, :]
    refs[count][...] = total


def weight_kernel(lanes, slots, per, lane_ref, *refs):
    coeffs, backs = refs[:lanes], refs[lanes : 2 * lanes]
    out_ref, all_ref, c_ref, b_ref = refs[2 * lanes :]
    each = 2 * per
    kept = slots - 3
    rows = (slots + 1) * each
    for n in range(lanes):
        coeff = coeffs[n][...].astype(f32)
        c_ref[n * rows : n * rows + (kept + 1) * each, :] = coeff[0 : (kept + 1) * each]
        all_ref[n] = coeff[kept * each :]
        b_ref[n * rows : (n + 1) * rows, :] = backs[n][0:rows, :]
    for n in range(lanes):
        source = lax.rem(lane_ref[0] - n + lanes, lanes)
        other = lax.rem(n - 1 + 2 * lax.rem(source, 2) + lanes, lanes)
        c_ref[n * rows + (kept + 1) * each : (n + 1) * rows, :] = all_ref[other]
    slots = slots + 1
    for m in range(per):
        re_rows = pl.ds(m, lanes * slots, stride=2 * per)
        im_rows = pl.ds(per + m, lanes * slots, stride=2 * per)
        c_re = c_ref[re_rows, :].astype(bf16)
        c_im = c_ref[im_rows, :].astype(bf16)
        b_re = b_ref[re_rows, :]
        b_im = b_ref[im_rows, :]
        left = jnp.concatenate([c_re, c_im], axis=0)
        right = jnp.concatenate(
            [jnp.concatenate([b_re, b_im], axis=1), jnp.concatenate([b_im, -b_re], axis=1)], axis=0
        )
        high = right.astype(bf16)
        low = (right - high.astype(f32)).astype(bf16)
        left = jnp.concatenate([left, left], axis=0)
        right = jnp.concatenate([high, low], axis=0)
        grad = lax.dot_general(
            left, right, (((0,), (0,)), ((), ())), preferred_element_type=f32
        )
        out_ref[m, 0] = grad[:, 0:128]
        out_ref[m, 1] = grad[:, 128:256]


def place_kernel(shards, meta_ref, *refs):
    out_ref = refs[shards]
    size = refs[0].shape[0]
    for d in range(shards):
        i = lax.rem(meta_ref[0] - d + shards, shards)
        out_ref[pl.ds(pl.multiple_of(i * size, size), size), :] = refs[d][...]


def whole_vmem(count):
    return [pl.BlockSpec(memory_space=pltpu.VMEM)] * count


def params(limit=VMEM_BYTES):
    return pltpu.CompilerParams(vmem_limit_bytes=limit)


def rotations(value_of, axis, size):
    got = [value_of(0)]
    for d in range(1, size):
        perm = [(s, (s + d) % size) for s in range(size)]
        got.append(lax.ppermute(value_of(d), axis, perm))
    return got


def body(lanes, shards, fields, targets, lists, counts, spectral_w, local_w, proj):
    _, slots, planes, grid_len, _, width = fields.shape
    per = MODES // shards
    split = shards // MX
    cells = grid_len * grid_len
    step_planes = max(n for n in (1, 2, 3, 4) if planes % n == 0)
    blocks = planes // step_planes
    basis, inverse, xtab = phase_constants(grid_len)
    lane = lax.axis_index("dp").astype(jnp.int32)
    shard = lax.axis_index("fsdp").astype(jnp.int32)
    turn = shard if split == 1 else jnp.int32(0)
    meta = jnp.concatenate(
        [
            lists[0],
            counts[lane][None],
            jnp.sum(counts)[None],
            turn[None],
            (shard * planes)[None],
            counts[lane ^ 1][None],
        ]
    ).astype(jnp.int32)
    place = scalar_places(slots)

    kept = slots - 3

    def field_block(base):
        def block(g, blk, meta_ref, xtab_ref):
            count = meta_ref[place["count"]]
            slot = meta_ref[jnp.minimum(base + g, count - 1)]
            return (0, slot, jnp.where(base + g < count, blk, blocks - 1), 0, 0, 0)

        return pl.BlockSpec((1, 1, step_planes, grid_len, grid_len, width), block)

    def target_block(base):
        def block(g, blk, meta_ref, xtab_ref):
            count = meta_ref[place["count"]]
            return (0, meta_ref[jnp.minimum(base + g, count - 1)], 0, 0)

        return pl.BlockSpec((1, 1, planes, cells), block)

    def shared_item(g, blk):
        return jnp.maximum(g * blocks + blk - (blocks - 1), 0)

    def fixed(*shape):
        return pl.BlockSpec(shape, lambda g, blk, meta_ref, xtab_ref: (0,) * len(shape))

    items = 2 * blocks + 1
    shared_fields = pl.BlockSpec(
        (1, step_planes, grid_len, grid_len, width),
        lambda g, blk, meta_ref, xtab_ref: (shared_item(g, blk), 0, 0, 0, 0),
    )
    shared_targets = pl.BlockSpec((1, planes, cells), lambda g, blk, meta_ref, xtab_ref: (g, 0, 0))
    part_rows = slots * 16
    forward_scale = float(grid_len) ** (-1.5)
    *late_parts, sent_fields, sent_targets = pl.pallas_call(
        functools.partial(forward_kernel, slots, kept, True, planes, step_planes, forward_scale),
        grid_spec=pltpu.PrefetchScalarGridSpec(
            num_scalar_prefetch=2,
            grid=(3, blocks),
            in_specs=[field_block(kept), fixed(*basis.shape), target_block(kept)],
            out_specs=[fixed(3 * 16, width)] * MX + [shared_fields, shared_targets],
            scratch_shapes=[pltpu.VMEM((planes, 16, width), f32)],
        ),
        out_shape=[jax.ShapeDtypeStruct((3 * 16, width), f32)] * MX
        + [
            jax.ShapeDtypeStruct((items, step_planes, grid_len, grid_len, width), bf16),
            jax.ShapeDtypeStruct((3, planes, cells), bf16),
        ],
        compiler_params=params(),
        name="forward_shared",
    )(meta, xtab, fields, basis, targets)
    swap = lambda x: lax.ppermute(x, "dp", [(s, s ^ 1) for s in range(lanes)])
    came_fields = swap(sent_fields)
    came_targets = swap(sent_targets)
    parts = pl.pallas_call(
        functools.partial(forward_kernel, slots, 0, False, planes, step_planes, forward_scale),
        grid_spec=pltpu.PrefetchScalarGridSpec(
            num_scalar_prefetch=2,
            grid=(3, blocks),
            in_specs=[field_block(0), fixed(*basis.shape)] + [fixed(3 * 16, width)] * MX,
            out_specs=[fixed(part_rows, width)] * MX,
            scratch_shapes=[pltpu.VMEM((planes, 16, width), f32)],
        ),
        out_shape=[jax.ShapeDtypeStruct((part_rows, width), f32)] * MX,
        compiler_params=params(),
        cost_estimate=pl.CostEstimate(
            flops=3 * planes * cells * 256 * 256,
            bytes_accessed=3 * planes * cells * width * 2,
            transcendentals=0,
        ),
        name="forward_modes",
    )(meta, xtab, fields, basis, *late_parts)

    def shard_parts(pieces, count):
        if split == 1:
            return lambda d: pieces[d]
        stacked = jnp.stack(pieces).reshape(MX, count, 2, split, per, width)
        stacked = jnp.moveaxis(stacked, 3, 1).reshape(shards, count * 2 * per, width)
        return lambda d: lax.dynamic_index_in_dim(stacked, (shard + d) % shards, 0, keepdims=False)

    def mode_parts(pieces, count):
        if split == 1:
            return pieces
        stacked = jnp.stack(pieces)[(shard - jnp.arange(shards)) % shards]
        stacked = stacked.reshape(MX, split, count, 2, per, width)
        stacked = jnp.moveaxis(stacked, 1, 3).reshape(MX, count * 16, width)
        return [stacked[(-d) % MX] for d in range(MX)]

    came = rotations(shard_parts(parts, slots), "fsdp", shards)
    own_rows = slots * 2 * per
    coeff, own_spectrum = pl.pallas_call(
        functools.partial(mix_kernel, slots, per, shards),
        in_specs=whole_vmem(shards + 1),
        out_specs=whole_vmem(2),
        out_shape=[jax.ShapeDtypeStruct((own_rows, width), bf16)] * 2,
        scratch_shapes=[pltpu.VMEM((own_rows, width), f32)] * 2,
        compiler_params=params(),
        name="mix_modes",
    )(*came, spectral_w)
    spectrum = mode_parts(rotations(lambda d: own_spectrum, "fsdp", shards), slots)
    coeffs = rotations(lambda d: coeff, "dp", lanes)

    local_rows = width // MX
    eye = np.tile(np.eye(64, dtype=ml_dtypes.bfloat16), (1, 2))
    wide_eye = np.eye(128, dtype=np.float32)
    ones = np.ones((128, 128), ml_dtypes.bfloat16)
    ones = np.concatenate([ones, -ones], axis=0)

    def own_block(g, blk, meta_ref, xtab_ref):
        count, partner = meta_ref[place["count"]], meta_ref[place["partner"]]
        slot = meta_ref[jnp.minimum(g, count - 1)]
        away = (g >= kept) & shared_live(slots, kept, blocks, count, partner, g - kept, blk)
        blk = jnp.where(away, max(blocks - 2, 0), blk)
        return (0, slot, jnp.where(g < count, blk, blocks - 1), 0, 0, 0)

    def came_item(g, blk, meta_ref):
        some = kept < meta_ref[place["partner"]]
        return jnp.where(some, shared_item(g, blk), 0), jnp.where(some, g, 0)

    came_block = pl.BlockSpec(
        (1, step_planes, grid_len, grid_len, width),
        lambda g, blk, meta_ref, xtab_ref: (came_item(g, blk, meta_ref)[0], 0, 0, 0, 0),
    )
    came_lines = pl.BlockSpec(
        (1, planes, cells), lambda g, blk, meta_ref, xtab_ref: (came_item(g, blk, meta_ref)[1], 0, 0)
    )

    def backward(own, fields_, targets_, spectrum_, given):
        positions = kept + 1 if own else 3
        rows = (kept + 1 if own else slots + 1) * 16 + local_rows
        own_fields = pl.BlockSpec((1, 1, step_planes, grid_len, grid_len, width), own_block)
        return pl.pallas_call(
            functools.partial(
                backward_kernel, slots, own, planes, step_planes, 128, float(MODES) ** (-0.5)
            ),
            grid_spec=pltpu.PrefetchScalarGridSpec(
                num_scalar_prefetch=2,
                grid=(positions, blocks),
                in_specs=([own_fields, target_block(0)] if own else [came_block, came_lines])
                + [fixed(part_rows, width)] * MX
                + [
                    fixed(width, width),
                    fixed(1, width),
                    fixed(*inverse.shape),
                    fixed(*basis.shape),
                    fixed(*eye.shape),
                    fixed(*wide_eye.shape),
                    fixed(*ones.shape),
                ]
                + [fixed(*g.shape) for g in given],
                out_specs=[fixed(rows, width)] * MX,
                scratch_shapes=[
                    pltpu.VMEM((2, 256, width), bf16),
                    pltpu.VMEM((2, cells // 3, width), f32),
                    pltpu.VMEM((2, cells // 3, width), f32),
                    pltpu.VMEM((2, cells // 6, 2 * width), bf16),
                    pltpu.VMEM((2, cells // 6, width), f32),
                    pltpu.VMEM((2, cells // 3, width), bf16),
                    pltpu.VMEM((width, width), f32),
                    pltpu.VMEM((planes, 16, width), f32),
                    pltpu.VMEM((planes, 16, 2 * cells), bf16),
                    pltpu.VMEM((MX, 16, width), f32),
                    pltpu.VMEM((step_planes, cells, width), bf16),
                    pltpu.VMEM((step_planes, 16, 2 * cells), bf16),
                    pltpu.VMEM((step_planes, 16, width), f32),
                    pltpu.VMEM((planes, 8, cells), f32),
                    pltpu.VMEM((step_planes, 8, cells), f32),
                ],
            ),
            out_shape=[jax.ShapeDtypeStruct((rows, width), f32)] * MX,
            compiler_params=params(LARGE_VMEM_BYTES),
            cost_estimate=pl.CostEstimate(
                flops=4 * positions * planes * cells * 256 * 256,
                bytes_accessed=positions * planes * cells * width * 2,
                transcendentals=0,
            ),
            name="backward_own" if own else "backward_shared",
        )(
            meta, xtab, fields_, targets_, *spectrum_, local_w, proj.reshape(1, width),
            inverse, basis, eye, wide_eye, ones, *given,
        )

    came_spectrum = [swap(piece) for piece in spectrum]
    own_results = backward(True, fields, targets, spectrum, [])
    results = backward(False, came_fields, came_targets, came_spectrum, own_results)
    places = slots + 1
    part_rows = places * 16
    place_rows = places * 2 * per

    if split == 1:
        chunk = lambda d: results[d]
    else:
        backs = shard_parts([r[:part_rows] for r in results], places)
        local = jnp.concatenate([r[part_rows:] for r in results], axis=0)
        rows = width // shards
        chunk = lambda d: jnp.concatenate(
            [backs(d), lax.dynamic_slice_in_dim(local, (shard + d) % shards * rows, rows, 0)], axis=0
        )
    came = rotations(chunk, "fsdp", shards)
    own_sum = pl.pallas_call(
        functools.partial(sum_kernel, shards),
        in_specs=whole_vmem(shards),
        out_specs=pl.BlockSpec(memory_space=pltpu.VMEM),
        out_shape=jax.ShapeDtypeStruct(came[0].shape, f32),
        compiler_params=params(),
        name="sum_shards",
    )(*came)
    sums = rotations(lambda d: own_sum, "dp", lanes)
    own_local = pl.pallas_call(
        functools.partial(local_sum_kernel, lanes, place_rows),
        in_specs=whole_vmem(lanes),
        out_specs=pl.BlockSpec(memory_space=pltpu.VMEM),
        out_shape=jax.ShapeDtypeStruct((width // shards, width), f32),
        compiler_params=params(),
        name="sum_local",
    )(*sums)
    locals_ = rotations(lambda d: own_local, "fsdp", shards)
    grad_spectral = pl.pallas_call(
        functools.partial(weight_kernel, lanes, slots, per),
        in_specs=[pl.BlockSpec(memory_space=pltpu.SMEM)] + whole_vmem(2 * lanes),
        out_specs=pl.BlockSpec(memory_space=pltpu.VMEM),
        out_shape=jax.ShapeDtypeStruct((per, 2, width, width), f32),
        scratch_shapes=[pltpu.VMEM((lanes, 3 * 2 * per, width), f32)]
        + [pltpu.VMEM((lanes * place_rows, width), f32)] * 2,
        compiler_params=params(),
        cost_estimate=pl.CostEstimate(
            flops=2 * per * 256 * 128 * 256, bytes_accessed=2 * per * 2 * width * width * 4, transcendentals=0
        ),
        name="weight_grad",
    )(lane[None], *coeffs, *sums)
    grad_local = pl.pallas_call(
        functools.partial(place_kernel, shards),
        in_specs=[pl.BlockSpec(memory_space=pltpu.SMEM)] + whole_vmem(shards),
        out_specs=pl.BlockSpec(memory_space=pltpu.VMEM),
        out_shape=jax.ShapeDtypeStruct((width, width), f32),
        compiler_params=params(),
        name="place_local",
    )(shard[None], *locals_)
    return (grad_spectral, grad_local)


def solution(mesh):
    return jax.shard_map(
        functools.partial(body, mesh.shape["dp"], mesh.shape["fsdp"]),
        mesh=mesh,
        in_specs=(
            P("dp", None, "fsdp", None, None, None),
            P("dp", None, "fsdp", None),
            P("dp", None),
            P(),
            P("fsdp", None, None, None),
            P(),
            P(),
        ),
        out_specs=(P("fsdp", None, None, None), P()),
        check_vma=False,
    )
```

```python
import functools
import math

import jax
import jax.numpy as jnp
import ml_dtypes
import numpy as np
from jax import lax
from jax.experimental import pallas as pl
from jax.experimental.pallas import tpu as pltpu
from jax.sharding import PartitionSpec as P

MX = 4
MY = 4
MZ = 2
MODES = MX * MY * MZ
VMEM_BYTES = 40 * 1024 * 1024
LARGE_VMEM_BYTES = 56 * 1024 * 1024
f32 = jnp.float32
bf16 = jnp.bfloat16
inv_root_two_pi = 0.3989422804014327
half_log2e = 0.7213475204444817
root_half = 0.7071067811865476


def split_bf16(values):
    high = values.astype(ml_dtypes.bfloat16)
    low = (values - high.astype(np.float64)).astype(ml_dtypes.bfloat16)
    return high, low


def angles(mode_ids, length):
    product = np.outer(mode_ids, np.arange(length)) % length
    return product * (2.0 * math.pi / length)


def phase_constants(length):
    y_angle = angles(np.arange(MY) - MY // 2, length)
    z_angle = angles(np.arange(MZ), length)
    rounded = lambda v: v.astype(np.float32).astype(ml_dtypes.bfloat16).astype(np.float64)
    cz, sz = rounded(np.cos(z_angle)), rounded(-np.sin(z_angle))
    cy, sy = np.cos(y_angle), -np.sin(y_angle)
    both = lambda a, b: (a[:, None, :, None] * b[None, :, None, :]).reshape(MY * MZ, length * length)
    fwd = np.concatenate([both(cy, cz) - both(sy, sz), both(sy, cz) + both(cy, sz)], axis=0)
    fwd = np.concatenate(split_bf16(fwd), axis=0)
    cz, sz = np.cos(z_angle), np.sin(z_angle)
    cy, sy = np.cos(y_angle), np.sin(y_angle)
    inv = np.concatenate([both(cy, cz) - both(sy, sz), -(both(sy, cz) + both(cy, sz))], axis=0).T
    high, low = split_bf16(inv)
    pad = np.zeros((length * length, 128 - 4 * high.shape[1]), ml_dtypes.bfloat16)
    inv = np.concatenate([high, low, high, low, pad], axis=1)
    x_angle = angles(np.arange(MX) - MX // 2, length).T
    xtab = np.stack([np.cos(x_angle), np.sin(x_angle)], axis=2).astype(np.float32)
    return fwd, inv, xtab.reshape(-1)


class Scalars:
    def __init__(self, planes, shards, lists_ref, counts_ref):
        self.lists, self.counts = lists_ref, counts_ref
        self.lane = lax.axis_index("dp")
        shard = lax.axis_index("fsdp")
        self.shard = shard if shards == MX else 0 * shard
        self.first = shard * planes

    @property
    def count(self):
        return self.counts[self.lane]

    @property
    def partner(self):
        return self.counts[self.lane ^ 1]

    def total(self, lanes):
        total = self.counts[0]
        for lane in range(1, lanes):
            total = total + self.counts[lane]
        return total

    def slot(self, position):
        return self.lists[0, jnp.minimum(position, self.count - 1)]


def combine_planes(q_ref, xtab_ref, cell0, shard, planes, scale, store):
    for d in range(MX):
        i = lax.rem(shard + d, MX)
        re = jnp.zeros((8, 128), f32)
        im = jnp.zeros((8, 128), f32)
        for a in range(planes):
            at = ((cell0 + a) * MX + i) * 2
            c = xtab_ref[at]
            s = xtab_ref[at + 1]
            q_re = q_ref[a, 0:8, :]
            q_im = q_ref[a, 8:16, :]
            re = re + (q_re * c + q_im * s)
            im = im + (q_im * c - q_re * s)
        store(d, re * scale, im * scale)


def forward_kernel(
    base, sends, scalars, planes, step_planes, scale, lists_ref, counts_ref, xtab_ref, f_ref, basis_ref, *rest
):
    if sends:
        t_ref, outs, send_ref, t_out_ref, q_ref = rest[0], rest[1 : MX + 1], *rest[MX + 1 :]
    else:
        given, outs, q_ref = rest[:MX], rest[MX : 2 * MX], rest[2 * MX]
    known = scalars(lists_ref, counts_ref)
    g, blk = pl.program_id(0), pl.program_id(1)
    live = base + g < known.count
    row = pl.multiple_of(g * 16, 16)

    if not sends:

        @pl.when((g == 0) & (blk == 0))
        def _():
            rows = given[0].shape[0]
            for d in range(MX):
                outs[d][rows : 2 * rows, :] = given[d][...]

    @pl.when(live)
    def _():
        cells = f_ref.shape[3] * f_ref.shape[4]
        for p in range(step_planes):
            field = f_ref[0, 0, p].reshape(cells, 128)
            part = jnp.dot(basis_ref[...], field, preferred_element_type=f32)
            q_ref[blk * step_planes + p] = part[0:16] + part[16:32]
            if sends:
                send_ref[0, p] = f_ref[0, 0, p]
        if sends:

            @pl.when(blk == 0)
            def _():
                t_out_ref[0] = t_ref[0, 0]

        @pl.when(blk == planes // step_planes - 1)
        def _():
            def store(d, re, im):
                outs[d][pl.ds(row, 8), :] = re
                outs[d][pl.ds(row + 8, 8), :] = im

            combine_planes(
                q_ref, xtab_ref, known.first, known.shard, planes, scale, store
            )

    @pl.when(jnp.logical_not(live) & (blk == 0))
    def _():
        for out in outs:
            out[pl.ds(row, 16), :] = jnp.zeros((16, 128), f32)


def shared_live(slots, kept, blocks, count, partner, g, blk):
    return (kept + g < count) & ((g > 0) | ((blk == blocks - 1) & (partner <= 1)))


def backward_kernel(
    slots, own, scalars, lanes, planes, step_planes, rows_step, scale,
    lists_ref, counts_ref, xtab_ref, f_ref, t_ref, *rest
):
    specs = rest[:MX]
    w_ref, proj_ref, inv_ref, basis_ref, eye_ref, wide_eye_ref, ones_ref = rest[MX : MX + 7]
    rest = rest[MX + 7 :]
    if not own:
        given, rest = rest[:MX], rest[MX:]
    outs = rest[:MX]
    rhs_ref, pre_ref, slope_ref, both_ref, resid_ref, d_ref, total_ref, q_ref, t16_ref, spec_ref, field_ref, line_ref, near_ref, far_t_ref, far_line_ref = rest[MX:]
    known = scalars(lists_ref, counts_ref)
    kept = slots - 3
    g, blk = pl.program_id(0), pl.program_id(1)
    blocks = planes // step_planes
    count, partner = known.count, known.partner
    if own:
        some = g < count
        away = (g >= kept) & shared_live(slots, kept, blocks, count, partner, g - kept, blk)
        live = some & jnp.logical_not(away)
        positions, spec_row, out_row = kept + 1, g * 16, g * 16
        plane_of = lambda p: f_ref[0, 0, p].reshape(cells, 128)
        lines_of = lambda: t_ref[0, 0].astype(f32)
    else:
        some = kept + g < partner
        live = shared_live(slots, kept, blocks, partner, count, g, blk)
        positions, spec_row, out_row = 3, (kept + g) * 16, (kept + 1 + g) * 16
        plane_of = lambda p: f_ref[0, p].reshape(cells, 128)
        lines_of = lambda: t_ref[0].astype(f32)
    row = pl.multiple_of(out_row, 16)
    shard = known.shard
    cell0 = known.first
    cells = inv_ref.shape[0]
    third = cells // 3
    half = third // 2
    unroll = step_planes

    grids = jnp.full((1, 128), known.total(lanes).astype(f32), f32)
    root = lax.rsqrt(grids)
    root = root * (1.5 - 0.5 * grids * root * root)

    @pl.when((g == 0) & (blk == 0))
    def _():
        total_ref[...] = jnp.zeros_like(total_ref)
        for n in range(2):
            rhs_ref[n, 0:128, :] = w_ref[...]
            rhs_ref[n, 128:256, :] = jnp.zeros((128, 128), bf16)
        if not own:
            rows = (kept + 1) * 16
            for d in range(MX):
                outs[d][0:rows, :] = given[d][0:rows, :]

    @pl.when(some & (blk == 0))
    def _():
        q_ref[...] = jnp.zeros_like(q_ref)
        lines = lines_of() * root[:, 0:1]
        for a in range(planes):
            far_t_ref[a] = jnp.broadcast_to(lines[a : a + 1, :], (8, cells))
        high = lines.astype(bf16).astype(f32)
        low = lines - high
        early = lax.broadcasted_iota(jnp.int32, (planes, 128), 1) < 64
        for at in range(0, cells, 128):
            part_h, part_l = high[:, at : at + 128], low[:, at : at + 128]
            turned_h, turned_l = pltpu.roll(part_h, 64, 1), pltpu.roll(part_l, 64, 1)
            both = (jnp.where(early, part_h, turned_l), jnp.where(early, turned_h, part_l))
            for n in range(2):
                for a in range(planes):
                    line = jnp.broadcast_to(both[n][a : a + 1, :], (16, 128))
                    t16_ref[a, :, 2 * at + 128 * n : 2 * at + 128 * (n + 1)] = line.astype(bf16)
        for d in range(MX):
            spec_ref[d] = specs[d][pl.ds(pl.multiple_of(spec_row, 16), 16), :].astype(f32)

    @pl.when(live)
    def _():
        gate = proj_ref[...] * root * 0.5
        edge = proj_ref[...] * root * inv_root_two_pi

        def first_rows(a, rhs):
            re = jnp.zeros((8, 128), f32)
            im = jnp.zeros((8, 128), f32)
            for d in range(MX):
                i = lax.rem(shard - d + MX, MX)
                at = ((cell0 + a) * MX + i) * 2
                c = xtab_ref[at]
                s = xtab_ref[at + 1]
                s_re = spec_ref[d, 0:8, :]
                s_im = spec_ref[d, 8:16, :]
                re = re + (s_re * c - s_im * s)
                im = im + (s_re * s + s_im * c)
            first = jnp.concatenate([re, im], axis=0) * scale
            high = first.astype(bf16)
            low = (first - high.astype(f32)).astype(bf16)
            rhs[128:144, :] = high
            rhs[144:160, :] = high
            rhs[160:176, :] = low
            rhs[176:192, :] = low

        def planes_together(n, carry):
            units = [(u, k) for u in range(unroll) for k in range(3)]
            for u in range(unroll):
                field_ref[u] = plane_of(n * unroll + u)
                line_ref[u] = t16_ref[blk * step_planes + n * unroll + u]
                far_line_ref[u] = far_t_ref[blk * step_planes + n * unroll + u]

            def before(s, r0):
                u, k = units[s]
                rhs = rhs_ref.at[u % 2]
                if k == 0 and r0 == 0:
                    first_rows(blk * step_planes + n * unroll + u, rhs)
                part = slice(k * third + r0, k * third + r0 + half)
                lhs = jnp.concatenate([field_ref[u, part, :], inv_ref[part, :]], axis=1)
                pre_ref[s % 2, r0 : r0 + half, :] = jnp.dot(lhs, rhs[...], preferred_element_type=f32)

            def elementwise(s, r0):
                u, k = units[s]
                rows = slice(r0, r0 + rows_step)
                pre = pre_ref[s % 2, rows, :]
                bell = jnp.exp2(pre * pre * (-half_log2e))
                gated = (1.0 + lax.erf(pre * root_half)) * gate
                slope_ref[s % 2, rows, :] = gated + pre * bell * edge
                active = pre * gated
                if r0 >= half:
                    at = k * third + r0
                    line = far_line_ref[u, :, at : at + 128]
                    wanted = jnp.concatenate([line] * (rows_step // 8), axis=0)
                    resid = jnp.sum(active - wanted * wide_eye_ref[...], axis=1, keepdims=True)
                    resid_ref[s % 2, r0 - half : r0 - half + rows_step, :] = jnp.broadcast_to(
                        resid, (rows_step, 128)
                    )
                    return
                both_ref[s % 2, rows, 0:128] = active.astype(bf16)
                for r1 in range(r0, r0 + rows_step, 16):
                    at = 2 * (k * third + r1 - r1 % 64)
                    line = line_ref[u, :, at : at + 128]
                    both_ref[s % 2, r1 : r1 + 16, 128:256] = line * eye_ref[r1 % 64 : r1 % 64 + 16, :]

            def after(s, r0):
                rows = slice(r0, r0 + half)
                if r0 >= half:
                    resid = resid_ref[s % 2]
                else:
                    resid = jnp.dot(both_ref[s % 2], ones_ref[...], preferred_element_type=f32)
                d_ref[s % 2, rows, :] = (resid * slope_ref[s % 2, rows, :]).astype(bf16)

            def last(s):
                u, k = units[s]
                part = slice(k * third, (k + 1) * third)
                lhs = jnp.concatenate([field_ref[u, part, :].T, basis_ref[:, part]], axis=0)
                sums = jnp.dot(lhs, d_ref[s % 2], preferred_element_type=f32)
                total_ref[...] += sums[0:128]
                back = sums[128:144] + sums[144:160]
                near_ref[u] = back if k == 0 else near_ref[u] + back

            pieces = third // rows_step
            for s in range(len(units) + 3):
                for piece in range(pieces):
                    r0 = piece * rows_step
                    if s < len(units) and r0 % half == 0:
                        before(s, r0)
                    if 0 <= s - 2 < len(units) and r0 % half == 0:
                        after(s - 2, r0)
                    if 0 <= s - 3 and piece == pieces // 2 - 1:
                        last(s - 3)
                    if 0 <= s - 1 < len(units):
                        elementwise(s - 1, r0)
            for u in range(unroll):
                q_ref[blk * step_planes + n * unroll + u] = near_ref[u]
            return carry

        lax.fori_loop(0, step_planes // unroll, planes_together, 0)

    @pl.when(some & (blk == blocks - 1))
    def _():
        def store(d, re, im):
            outs[d][pl.ds(row, 8), :] = re
            outs[d][pl.ds(row + 8, 8), :] = im

        combine_planes(q_ref, xtab_ref, cell0, shard, planes, scale, store)

    @pl.when(jnp.logical_not(some) & (blk == 0))
    def _():
        for out in outs:
            out[pl.ds(row, 16), :] = jnp.zeros((16, 128), f32)

    @pl.when((g == positions - 1) & (blk == blocks - 1))
    def _():
        size = 128 // MX
        for d in range(MX):
            i = lax.rem(shard + d, MX)
            at = pl.multiple_of(i * size, size)
            part = total_ref[pl.ds(at, size), :]
            if not own:
                part = part + given[d][(kept + 1) * 16 : (kept + 1) * 16 + size, :]
            rows = outs[d].shape[0]
            outs[d][rows - size : rows, :] = part


def mix_kernel(slots, per, shards, *refs):
    parts = refs[:shards]
    w_ref, coeff_out, spec_out, c_ref, s_ref = refs[shards:]
    total = parts[0][...]
    for part in parts[1:]:
        total = total + part[...]
    coeff = total.astype(bf16)
    coeff_out[...] = coeff
    c_ref[...] = coeff.astype(f32)
    for m in range(per):
        re_rows = pl.ds(m, slots, stride=2 * per)
        im_rows = pl.ds(per + m, slots, stride=2 * per)
        re = c_ref[re_rows, :].astype(bf16)
        im = c_ref[im_rows, :].astype(bf16)
        weight = w_ref[m].reshape(256, 128)
        s_ref[re_rows, :] = jnp.dot(
            jnp.concatenate([re, -im], axis=1), weight, preferred_element_type=f32
        )
        s_ref[im_rows, :] = jnp.dot(
            jnp.concatenate([im, re], axis=1), weight, preferred_element_type=f32
        )
    spec_out[...] = s_ref[...].astype(bf16)


def sum_kernel(count, *refs):
    total = refs[0][...]
    for part in refs[1:count]:
        total = total + part[...]
    refs[count][...] = total


def local_sum_kernel(count, rows, *refs):
    size = refs[count].shape[0]
    total = refs[0][rows : rows + size, :]
    for part in refs[1:count]:
        total = total + part[rows : rows + size, :]
    refs[count][...] = total


def weight_kernel(lanes, slots, per, *refs):
    coeffs, backs = refs[:lanes], refs[lanes : 2 * lanes]
    out_ref, all_ref, c_ref, b_ref = refs[2 * lanes :]
    each = 2 * per
    kept = slots - 3
    rows = (slots + 1) * each
    for n in range(lanes):
        coeff = coeffs[n][...].astype(f32)
        c_ref[n * rows : n * rows + (kept + 1) * each, :] = coeff[0 : (kept + 1) * each]
        all_ref[n] = coeff[kept * each :]
        b_ref[n * rows : (n + 1) * rows, :] = backs[n][0:rows, :]
    lane = lax.axis_index("dp")
    for n in range(lanes):
        source = lax.rem(lane - n + lanes, lanes)
        other = lax.rem(n - 1 + 2 * lax.rem(source, 2) + lanes, lanes)
        c_ref[n * rows + (kept + 1) * each : (n + 1) * rows, :] = all_ref[other]
    slots = slots + 1
    for m in range(per):
        re_rows = pl.ds(m, lanes * slots, stride=2 * per)
        im_rows = pl.ds(per + m, lanes * slots, stride=2 * per)
        c_re = c_ref[re_rows, :].astype(bf16)
        c_im = c_ref[im_rows, :].astype(bf16)
        b_re = b_ref[re_rows, :]
        b_im = b_ref[im_rows, :]
        left = jnp.concatenate([c_re, c_im], axis=0)
        right = jnp.concatenate(
            [jnp.concatenate([b_re, b_im], axis=1), jnp.concatenate([b_im, -b_re], axis=1)], axis=0
        )
        high = right.astype(bf16)
        low = (right - high.astype(f32)).astype(bf16)
        left = jnp.concatenate([left, left], axis=0)
        right = jnp.concatenate([high, low], axis=0)
        grad = lax.dot_general(
            left, right, (((0,), (0,)), ((), ())), preferred_element_type=f32
        )
        out_ref[m, 0] = grad[:, 0:128]
        out_ref[m, 1] = grad[:, 128:256]


def place_kernel(shards, *refs):
    out_ref = refs[shards]
    size = refs[0].shape[0]
    for d in range(shards):
        i = lax.rem(lax.axis_index("fsdp") - d + shards, shards)
        out_ref[pl.ds(pl.multiple_of(i * size, size), size), :] = refs[d][...]


def whole_vmem(count):
    return [pl.BlockSpec(memory_space=pltpu.VMEM)] * count


def params(limit=VMEM_BYTES):
    return pltpu.CompilerParams(vmem_limit_bytes=limit)


def rotations(value_of, axis, size):
    got = [value_of(0)]
    for d in range(1, size):
        perm = [(s, (s + d) % size) for s in range(size)]
        got.append(lax.ppermute(value_of(d), axis, perm))
    return got


def body(lanes, shards, fields, targets, lists, counts, spectral_w, local_w, proj):
    _, slots, planes, grid_len, _, width = fields.shape
    per = MODES // shards
    split = shards // MX
    cells = grid_len * grid_len
    step_planes = max(n for n in (1, 2, 3, 4) if planes % n == 0)
    blocks = planes // step_planes
    basis, inverse, xtab = phase_constants(grid_len)
    shard = lax.axis_index("fsdp").astype(jnp.int32)
    scalars = functools.partial(Scalars, planes, shards)
    kept = slots - 3

    def field_block(base):
        def block(g, blk, lists_ref, counts_ref, xtab_ref):
            known = scalars(lists_ref, counts_ref)
            blk = jnp.where(base + g < known.count, blk, blocks - 1)
            return (0, known.slot(base + g), blk, 0, 0, 0)

        return pl.BlockSpec((1, 1, step_planes, grid_len, grid_len, width), block)

    def target_block(base):
        def block(g, blk, lists_ref, counts_ref, xtab_ref):
            return (0, scalars(lists_ref, counts_ref).slot(base + g), 0, 0)

        return pl.BlockSpec((1, 1, planes, cells), block)

    def shared_item(g, blk):
        return jnp.maximum(g * blocks + blk - (blocks - 1), 0)

    def fixed(*shape):
        return pl.BlockSpec(shape, lambda g, blk, lists_ref, counts_ref, xtab_ref: (0,) * len(shape))

    items = 2 * blocks + 1
    shared_fields = pl.BlockSpec(
        (1, step_planes, grid_len, grid_len, width),
        lambda g, blk, lists_ref, counts_ref, xtab_ref: (shared_item(g, blk), 0, 0, 0, 0),
    )
    shared_targets = pl.BlockSpec((1, planes, cells), lambda g, blk, lists_ref, counts_ref, xtab_ref: (g, 0, 0))
    part_rows = slots * 16
    forward_scale = float(grid_len) ** (-1.5)
    *late_parts, sent_fields, sent_targets = pl.pallas_call(
        functools.partial(forward_kernel, kept, True, scalars, planes, step_planes, forward_scale),
        grid_spec=pltpu.PrefetchScalarGridSpec(
            num_scalar_prefetch=3,
            grid=(3, blocks),
            in_specs=[field_block(kept), fixed(*basis.shape), target_block(kept)],
            out_specs=[fixed(3 * 16, width)] * MX + [shared_fields, shared_targets],
            scratch_shapes=[pltpu.VMEM((planes, 16, width), f32)],
        ),
        out_shape=[jax.ShapeDtypeStruct((3 * 16, width), f32)] * MX
        + [
            jax.ShapeDtypeStruct((items, step_planes, grid_len, grid_len, width), bf16),
            jax.ShapeDtypeStruct((3, planes, cells), bf16),
        ],
        compiler_params=params(),
        name="forward_shared",
    )(lists, counts, xtab, fields, basis, targets)
    swap = lambda x: lax.ppermute(x, "dp", [(s, s ^ 1) for s in range(lanes)])
    came_fields = swap(sent_fields)
    came_targets = swap(sent_targets)
    parts = pl.pallas_call(
        functools.partial(forward_kernel, 0, False, scalars, planes, step_planes, forward_scale),
        grid_spec=pltpu.PrefetchScalarGridSpec(
            num_scalar_prefetch=3,
            grid=(3, blocks),
            in_specs=[field_block(0), fixed(*basis.shape)] + [fixed(3 * 16, width)] * MX,
            out_specs=[fixed(part_rows, width)] * MX,
            scratch_shapes=[pltpu.VMEM((planes, 16, width), f32)],
        ),
        out_shape=[jax.ShapeDtypeStruct((part_rows, width), f32)] * MX,
        compiler_params=params(),
        cost_estimate=pl.CostEstimate(
            flops=3 * planes * cells * 256 * 256,
            bytes_accessed=3 * planes * cells * width * 2,
            transcendentals=0,
        ),
        name="forward_modes",
    )(lists, counts, xtab, fields, basis, *late_parts)

    def shard_parts(pieces, count):
        if split == 1:
            return lambda d: pieces[d]
        stacked = jnp.stack(pieces).reshape(MX, count, 2, split, per, width)
        stacked = jnp.moveaxis(stacked, 3, 1).reshape(shards, count * 2 * per, width)
        return lambda d: lax.dynamic_index_in_dim(stacked, (shard + d) % shards, 0, keepdims=False)

    def mode_parts(pieces, count):
        if split == 1:
            return pieces
        stacked = jnp.stack(pieces)[(shard - jnp.arange(shards)) % shards]
        stacked = stacked.reshape(MX, split, count, 2, per, width)
        stacked = jnp.moveaxis(stacked, 1, 3).reshape(MX, count * 16, width)
        return [stacked[(-d) % MX] for d in range(MX)]

    came = rotations(shard_parts(parts, slots), "fsdp", shards)
    own_rows = slots * 2 * per
    coeff, own_spectrum = pl.pallas_call(
        functools.partial(mix_kernel, slots, per, shards),
        in_specs=whole_vmem(shards + 1),
        out_specs=whole_vmem(2),
        out_shape=[jax.ShapeDtypeStruct((own_rows, width), bf16)] * 2,
        scratch_shapes=[pltpu.VMEM((own_rows, width), f32)] * 2,
        compiler_params=params(),
        name="mix_modes",
    )(*came, spectral_w)
    spectrum = mode_parts(rotations(lambda d: own_spectrum, "fsdp", shards), slots)
    coeffs = rotations(lambda d: coeff, "dp", lanes)

    local_rows = width // MX
    eye = np.tile(np.eye(64, dtype=ml_dtypes.bfloat16), (1, 2))
    wide_eye = np.eye(128, dtype=np.float32)
    ones = np.ones((128, 128), ml_dtypes.bfloat16)
    ones = np.concatenate([ones, -ones], axis=0)

    def own_block(g, blk, lists_ref, counts_ref, xtab_ref):
        known = scalars(lists_ref, counts_ref)
        count, partner, slot = known.count, known.partner, known.slot(g)
        away = (g >= kept) & shared_live(slots, kept, blocks, count, partner, g - kept, blk)
        blk = jnp.where(away, max(blocks - 2, 0), blk)
        return (0, slot, jnp.where(g < count, blk, blocks - 1), 0, 0, 0)

    def came_item(g, blk, lists_ref, counts_ref):
        some = kept < scalars(lists_ref, counts_ref).partner
        return jnp.where(some, shared_item(g, blk), 0), jnp.where(some, g, 0)

    came_block = pl.BlockSpec(
        (1, step_planes, grid_len, grid_len, width),
        lambda g, blk, lists_ref, counts_ref, xtab_ref: (came_item(g, blk, lists_ref, counts_ref)[0], 0, 0, 0, 0),
    )
    came_lines = pl.BlockSpec(
        (1, planes, cells), lambda g, blk, lists_ref, counts_ref, xtab_ref: (came_item(g, blk, lists_ref, counts_ref)[1], 0, 0)
    )

    def backward(own, fields_, targets_, spectrum_, given):
        positions = kept + 1 if own else 3
        rows = (kept + 1 if own else slots + 1) * 16 + local_rows
        own_fields = pl.BlockSpec((1, 1, step_planes, grid_len, grid_len, width), own_block)
        return pl.pallas_call(
            functools.partial(
                backward_kernel, slots, own, scalars, lanes, planes, step_planes, 128, float(MODES) ** (-0.5)
            ),
            grid_spec=pltpu.PrefetchScalarGridSpec(
                num_scalar_prefetch=3,
                grid=(positions, blocks),
                in_specs=([own_fields, target_block(0)] if own else [came_block, came_lines])
                + [fixed(part_rows, width)] * MX
                + [
                    fixed(width, width),
                    fixed(1, width),
                    fixed(*inverse.shape),
                    fixed(*basis.shape),
                    fixed(*eye.shape),
                    fixed(*wide_eye.shape),
                    fixed(*ones.shape),
                ]
                + [fixed(*g.shape) for g in given],
                out_specs=[fixed(rows, width)] * MX,
                scratch_shapes=[
                    pltpu.VMEM((2, 256, width), bf16),
                    pltpu.VMEM((2, cells // 3, width), f32),
                    pltpu.VMEM((2, cells // 3, width), f32),
                    pltpu.VMEM((2, cells // 6, 2 * width), bf16),
                    pltpu.VMEM((2, cells // 6, width), f32),
                    pltpu.VMEM((2, cells // 3, width), bf16),
                    pltpu.VMEM((width, width), f32),
                    pltpu.VMEM((planes, 16, width), f32),
                    pltpu.VMEM((planes, 16, 2 * cells), bf16),
                    pltpu.VMEM((MX, 16, width), f32),
                    pltpu.VMEM((step_planes, cells, width), bf16),
                    pltpu.VMEM((step_planes, 16, 2 * cells), bf16),
                    pltpu.VMEM((step_planes, 16, width), f32),
                    pltpu.VMEM((planes, 8, cells), f32),
                    pltpu.VMEM((step_planes, 8, cells), f32),
                ],
            ),
            out_shape=[jax.ShapeDtypeStruct((rows, width), f32)] * MX,
            compiler_params=params(LARGE_VMEM_BYTES),
            cost_estimate=pl.CostEstimate(
                flops=4 * positions * planes * cells * 256 * 256,
                bytes_accessed=positions * planes * cells * width * 2,
                transcendentals=0,
            ),
            name="backward_own" if own else "backward_shared",
        )(
            lists, counts, xtab, fields_, targets_, *spectrum_, local_w, proj.reshape(1, width),
            inverse, basis, eye, wide_eye, ones, *given,
        )

    came_spectrum = [swap(piece) for piece in spectrum]
    own_results = backward(True, fields, targets, spectrum, [])
    results = backward(False, came_fields, came_targets, came_spectrum, own_results)
    places = slots + 1
    part_rows = places * 16
    place_rows = places * 2 * per

    if split == 1:
        chunk = lambda d: results[d]
    else:
        backs = shard_parts([r[:part_rows] for r in results], places)
        local = jnp.concatenate([r[part_rows:] for r in results], axis=0)
        rows = width // shards
        chunk = lambda d: jnp.concatenate(
            [backs(d), lax.dynamic_slice_in_dim(local, (shard + d) % shards * rows, rows, 0)], axis=0
        )
    came = rotations(chunk, "fsdp", shards)
    own_sum = pl.pallas_call(
        functools.partial(sum_kernel, shards),
        in_specs=whole_vmem(shards),
        out_specs=pl.BlockSpec(memory_space=pltpu.VMEM),
        out_shape=jax.ShapeDtypeStruct(came[0].shape, f32),
        compiler_params=params(),
        name="sum_shards",
    )(*came)
    sums = rotations(lambda d: own_sum, "dp", lanes)
    own_local = pl.pallas_call(
        functools.partial(local_sum_kernel, lanes, place_rows),
        in_specs=whole_vmem(lanes),
        out_specs=pl.BlockSpec(memory_space=pltpu.VMEM),
        out_shape=jax.ShapeDtypeStruct((width // shards, width), f32),
        compiler_params=params(),
        name="sum_local",
    )(*sums)
    locals_ = rotations(lambda d: own_local, "fsdp", shards)
    grad_spectral = pl.pallas_call(
        functools.partial(weight_kernel, lanes, slots, per),
        in_specs=whole_vmem(2 * lanes),
        out_specs=pl.BlockSpec(memory_space=pltpu.VMEM),
        out_shape=jax.ShapeDtypeStruct((per, 2, width, width), f32),
        scratch_shapes=[pltpu.VMEM((lanes, 3 * 2 * per, width), f32)]
        + [pltpu.VMEM((lanes * place_rows, width), f32)] * 2,
        compiler_params=params(),
        cost_estimate=pl.CostEstimate(
            flops=2 * per * 256 * 128 * 256, bytes_accessed=2 * per * 2 * width * width * 4, transcendentals=0
        ),
        name="weight_grad",
    )(*coeffs, *sums)
    grad_local = pl.pallas_call(
        functools.partial(place_kernel, shards),
        in_specs=whole_vmem(shards),
        out_specs=pl.BlockSpec(memory_space=pltpu.VMEM),
        out_shape=jax.ShapeDtypeStruct((width, width), f32),
        compiler_params=params(),
        name="place_local",
    )(*locals_)
    return (grad_spectral, grad_local)


def solution(mesh):
    return jax.shard_map(
        functools.partial(body, mesh.shape["dp"], mesh.shape["fsdp"]),
        mesh=mesh,
        in_specs=(
            P("dp", None, "fsdp", None, None, None),
            P("dp", None, "fsdp", None),
            P("dp", None),
            P(),
            P("fsdp", None, None, None),
            P(),
            P(),
        ),
        out_specs=(P("fsdp", None, None, None), P()),
        check_vma=False,
    )
```

```python
import functools
import math

import jax
import jax.numpy as jnp
import ml_dtypes
import numpy as np
from jax import lax
from jax.experimental import pallas as pl
from jax.experimental.pallas import tpu as pltpu
from jax.sharding import PartitionSpec as P

MX = 4
MY = 4
MZ = 2
MODES = MX * MY * MZ
VMEM_BYTES = 40 * 1024 * 1024
LARGE_VMEM_BYTES = 56 * 1024 * 1024
f32 = jnp.float32
bf16 = jnp.bfloat16
inv_root_two_pi = 0.3989422804014327
half_log2e = 0.7213475204444817
root_half = 0.7071067811865476


def split_bf16(values):
    high = values.astype(ml_dtypes.bfloat16)
    low = (values - high.astype(np.float64)).astype(ml_dtypes.bfloat16)
    return high, low


def angles(mode_ids, length):
    product = np.outer(mode_ids, np.arange(length)) % length
    return product * (2.0 * math.pi / length)


def phase_constants(length):
    y_angle = angles(np.arange(MY) - MY // 2, length)
    z_angle = angles(np.arange(MZ), length)
    rounded = lambda v: v.astype(np.float32).astype(ml_dtypes.bfloat16).astype(np.float64)
    cz, sz = rounded(np.cos(z_angle)), rounded(-np.sin(z_angle))
    cy, sy = np.cos(y_angle), -np.sin(y_angle)
    both = lambda a, b: (a[:, None, :, None] * b[None, :, None, :]).reshape(MY * MZ, length * length)
    fwd = np.concatenate([both(cy, cz) - both(sy, sz), both(sy, cz) + both(cy, sz)], axis=0)
    fwd = np.concatenate(split_bf16(fwd), axis=0)
    cz, sz = np.cos(z_angle), np.sin(z_angle)
    cy, sy = np.cos(y_angle), np.sin(y_angle)
    inv = np.concatenate([both(cy, cz) - both(sy, sz), -(both(sy, cz) + both(cy, sz))], axis=0).T
    high, low = split_bf16(inv)
    pad = np.zeros((length * length, 128 - 4 * high.shape[1]), ml_dtypes.bfloat16)
    inv = np.concatenate([high, low, high, low, pad], axis=1)
    x_angle = angles(np.arange(MX) - MX // 2, length).T
    xtab = np.stack([np.cos(x_angle), np.sin(x_angle)], axis=2).astype(np.float32)
    return fwd, inv, xtab.reshape(-1)


class Scalars:
    def __init__(self, planes, shards, lists_ref, counts_ref):
        self.lists, self.counts = lists_ref, counts_ref
        self.lane = lax.axis_index("dp")
        shard = lax.axis_index("fsdp")
        self.shard = shard if shards == MX else 0 * shard
        self.first = shard * planes

    @property
    def count(self):
        return self.counts[self.lane]

    @property
    def partner(self):
        return self.counts[self.lane ^ 1]

    def total(self, lanes):
        total = self.counts[0]
        for lane in range(1, lanes):
            total = total + self.counts[lane]
        return total

    def slot(self, position):
        return self.lists[0, jnp.minimum(position, self.count - 1)]


def combine_planes(q_ref, xtab_ref, cell0, shard, planes, scale, store):
    for d in range(MX):
        i = lax.rem(shard + d, MX)
        re = jnp.zeros((8, 128), f32)
        im = jnp.zeros((8, 128), f32)
        for a in range(planes):
            at = ((cell0 + a) * MX + i) * 2
            c = xtab_ref[at]
            s = xtab_ref[at + 1]
            q_re = q_ref[a, 0:8, :]
            q_im = q_ref[a, 8:16, :]
            re = re + (q_re * c + q_im * s)
            im = im + (q_im * c - q_re * s)
        store(d, re * scale, im * scale)


def forward_kernel(
    base, sends, scalars, planes, step_planes, scale, lists_ref, counts_ref, xtab_ref, f_ref, basis_ref, *rest
):
    if sends:
        t_ref, outs, send_ref, t_out_ref, q_ref = rest[0], rest[1 : MX + 1], *rest[MX + 1 :]
    else:
        given, outs, q_ref = rest[:MX], rest[MX : 2 * MX], rest[2 * MX]
    known = scalars(lists_ref, counts_ref)
    g, blk = pl.program_id(0), pl.program_id(1)
    live = base + g < known.count
    row = pl.multiple_of(g * 16, 16)

    if not sends:

        @pl.when((g == 0) & (blk == 0))
        def _():
            rows = given[0].shape[0]
            for d in range(MX):
                outs[d][rows : 2 * rows, :] = given[d][...]

    @pl.when(live)
    def _():
        cells = f_ref.shape[3] * f_ref.shape[4]
        for p in range(step_planes):
            field = f_ref[0, 0, p].reshape(cells, 128)
            part = jnp.dot(basis_ref[...], field, preferred_element_type=f32)
            q_ref[blk * step_planes + p] = part[0:16] + part[16:32]
            if sends:
                send_ref[0, p] = f_ref[0, 0, p]
        if sends:

            @pl.when(blk == 0)
            def _():
                t_out_ref[0] = t_ref[0, 0]

        @pl.when(blk == planes // step_planes - 1)
        def _():
            def store(d, re, im):
                outs[d][pl.ds(row, 8), :] = re
                outs[d][pl.ds(row + 8, 8), :] = im

            combine_planes(
                q_ref, xtab_ref, known.first, known.shard, planes, scale, store
            )

    @pl.when(jnp.logical_not(live) & (blk == 0))
    def _():
        for out in outs:
            out[pl.ds(row, 16), :] = jnp.zeros((16, 128), f32)


def shared_live(slots, kept, blocks, count, partner, g, blk):
    return (kept + g < count) & ((g > 0) | ((blk == blocks - 1) & (partner <= 1)))


def backward_kernel(
    slots, own, scalars, lanes, planes, step_planes, rows_step, scale,
    lists_ref, counts_ref, xtab_ref, f_ref, t_ref, *rest
):
    specs = rest[:MX]
    w_ref, proj_ref, inv_ref, basis_ref, eye_ref, wide_eye_ref, ones_ref = rest[MX : MX + 7]
    rest = rest[MX + 7 :]
    if not own:
        given, rest = rest[:MX], rest[MX:]
    outs = rest[:MX]
    rhs_ref, pre_ref, slope_ref, both_ref, resid_ref, d_ref, total_ref, q_ref, t16_ref, spec_ref, field_ref, line_ref, near_ref, far_t_ref, far_line_ref = rest[MX:]
    known = scalars(lists_ref, counts_ref)
    kept = slots - 3
    g, blk = pl.program_id(0), pl.program_id(1)
    blocks = planes // step_planes
    count, partner = known.count, known.partner
    if own:
        some = g < count
        away = (g >= kept) & shared_live(slots, kept, blocks, count, partner, g - kept, blk)
        live = some & jnp.logical_not(away)
        positions, spec_row, out_row = kept + 1, g * 16, g * 16
        plane_of = lambda p: f_ref[0, 0, p].reshape(cells, 128)
        lines_of = lambda: t_ref[0, 0].astype(f32)
    else:
        some = kept + g < partner
        live = shared_live(slots, kept, blocks, partner, count, g, blk)
        positions, spec_row, out_row = 3, (kept + g) * 16, (kept + 1 + g) * 16
        plane_of = lambda p: f_ref[0, p].reshape(cells, 128)
        lines_of = lambda: t_ref[0].astype(f32)
    row = pl.multiple_of(out_row, 16)
    shard = known.shard
    cell0 = known.first
    cells = inv_ref.shape[0]
    third = cells // 3
    half = third // 2
    unroll = step_planes

    grids = jnp.full((1, 128), known.total(lanes).astype(f32), f32)
    root = lax.rsqrt(grids)
    root = root * (1.5 - 0.5 * grids * root * root)

    @pl.when((g == 0) & (blk == 0))
    def _():
        total_ref[...] = jnp.zeros_like(total_ref)
        for n in range(2):
            rhs_ref[n, 0:128, :] = w_ref[...]
            rhs_ref[n, 128:256, :] = jnp.zeros((128, 128), bf16)
        if not own:
            rows = (kept + 1) * 16
            for d in range(MX):
                outs[d][0:rows, :] = given[d][0:rows, :].astype(bf16)

    @pl.when(some & (blk == 0))
    def _():
        q_ref[...] = jnp.zeros_like(q_ref)
        lines = lines_of() * root[:, 0:1]
        for a in range(planes):
            far_t_ref[a] = jnp.broadcast_to(lines[a : a + 1, :], (8, cells))
        high = lines.astype(bf16).astype(f32)
        low = lines - high
        early = lax.broadcasted_iota(jnp.int32, (planes, 128), 1) < 64
        for at in range(0, cells, 128):
            part_h, part_l = high[:, at : at + 128], low[:, at : at + 128]
            turned_h, turned_l = pltpu.roll(part_h, 64, 1), pltpu.roll(part_l, 64, 1)
            both = (jnp.where(early, part_h, turned_l), jnp.where(early, turned_h, part_l))
            for n in range(2):
                for a in range(planes):
                    line = jnp.broadcast_to(both[n][a : a + 1, :], (16, 128))
                    t16_ref[a, :, 2 * at + 128 * n : 2 * at + 128 * (n + 1)] = line.astype(bf16)
        for d in range(MX):
            spec_ref[d] = specs[d][pl.ds(pl.multiple_of(spec_row, 16), 16), :].astype(f32)

    @pl.when(live)
    def _():
        gate = proj_ref[...] * root * 0.5
        edge = proj_ref[...] * root * inv_root_two_pi

        def first_rows(a, rhs):
            re = jnp.zeros((8, 128), f32)
            im = jnp.zeros((8, 128), f32)
            for d in range(MX):
                i = lax.rem(shard - d + MX, MX)
                at = ((cell0 + a) * MX + i) * 2
                c = xtab_ref[at]
                s = xtab_ref[at + 1]
                s_re = spec_ref[d, 0:8, :]
                s_im = spec_ref[d, 8:16, :]
                re = re + (s_re * c - s_im * s)
                im = im + (s_re * s + s_im * c)
            first = jnp.concatenate([re, im], axis=0) * scale
            high = first.astype(bf16)
            low = (first - high.astype(f32)).astype(bf16)
            rhs[128:144, :] = high
            rhs[144:160, :] = high
            rhs[160:176, :] = low
            rhs[176:192, :] = low

        def planes_together(n, carry):
            units = [(u, k) for u in range(unroll) for k in range(3)]
            for u in range(unroll):
                field_ref[u] = plane_of(n * unroll + u)
                line_ref[u] = t16_ref[blk * step_planes + n * unroll + u]
                far_line_ref[u] = far_t_ref[blk * step_planes + n * unroll + u]

            def before(s, r0):
                u, k = units[s]
                rhs = rhs_ref.at[u % 2]
                if k == 0 and r0 == 0:
                    first_rows(blk * step_planes + n * unroll + u, rhs)
                part = slice(k * third + r0, k * third + r0 + half)
                lhs = jnp.concatenate([field_ref[u, part, :], inv_ref[part, :]], axis=1)
                pre_ref[s % 2, r0 : r0 + half, :] = jnp.dot(lhs, rhs[...], preferred_element_type=f32)

            def elementwise(s, r0):
                u, k = units[s]
                rows = slice(r0, r0 + rows_step)
                pre = pre_ref[s % 2, rows, :]
                bell = jnp.exp2(pre * pre * (-half_log2e))
                gated = (1.0 + lax.erf(pre * root_half)) * gate
                slope_ref[s % 2, rows, :] = gated + pre * bell * edge
                active = pre * gated
                if r0 >= half:
                    at = k * third + r0
                    line = far_line_ref[u, :, at : at + 128]
                    wanted = jnp.concatenate([line] * (rows_step // 8), axis=0)
                    resid = jnp.sum(active - wanted * wide_eye_ref[...], axis=1, keepdims=True)
                    resid_ref[s % 2, r0 - half : r0 - half + rows_step, :] = jnp.broadcast_to(
                        resid, (rows_step, 128)
                    )
                    return
                both_ref[s % 2, rows, 0:128] = active.astype(bf16)
                for r1 in range(r0, r0 + rows_step, 16):
                    at = 2 * (k * third + r1 - r1 % 64)
                    line = line_ref[u, :, at : at + 128]
                    both_ref[s % 2, r1 : r1 + 16, 128:256] = line * eye_ref[r1 % 64 : r1 % 64 + 16, :]

            def after(s, r0):
                rows = slice(r0, r0 + half)
                if r0 >= half:
                    resid = resid_ref[s % 2]
                else:
                    resid = jnp.dot(both_ref[s % 2], ones_ref[...], preferred_element_type=f32)
                d_ref[s % 2, rows, :] = (resid * slope_ref[s % 2, rows, :]).astype(bf16)

            def last(s):
                u, k = units[s]
                part = slice(k * third, (k + 1) * third)
                lhs = jnp.concatenate([field_ref[u, part, :].T, basis_ref[:, part]], axis=0)
                sums = jnp.dot(lhs, d_ref[s % 2], preferred_element_type=f32)
                total_ref[...] += sums[0:128]
                back = sums[128:144] + sums[144:160]
                near_ref[u] = back if k == 0 else near_ref[u] + back

            pieces = third // rows_step
            for s in range(len(units) + 3):
                for piece in range(pieces):
                    r0 = piece * rows_step
                    if s < len(units) and r0 % half == 0:
                        before(s, r0)
                    if 0 <= s - 2 < len(units) and r0 % half == 0:
                        after(s - 2, r0)
                    if 0 <= s - 3 and piece == pieces // 2 - 1:
                        last(s - 3)
                    if 0 <= s - 1 < len(units):
                        elementwise(s - 1, r0)
            for u in range(unroll):
                q_ref[blk * step_planes + n * unroll + u] = near_ref[u]
            return carry

        lax.fori_loop(0, step_planes // unroll, planes_together, 0)

    @pl.when(some & (blk == blocks - 1))
    def _():
        def store(d, re, im):
            both = jnp.concatenate([re, im], axis=0)
            outs[d][pl.ds(row, 16), :] = both.astype(outs[d].dtype)

        combine_planes(q_ref, xtab_ref, cell0, shard, planes, scale, store)

    @pl.when(jnp.logical_not(some) & (blk == 0))
    def _():
        for out in outs:
            out[pl.ds(row, 16), :] = jnp.zeros((16, 128), out.dtype)

    @pl.when((g == positions - 1) & (blk == blocks - 1))
    def _():
        size = 128 // MX
        for d in range(MX):
            i = lax.rem(shard + d, MX)
            at = pl.multiple_of(i * size, size)
            part = total_ref[pl.ds(at, size), :]
            if not own:
                part = part + given[d][(kept + 1) * 16 : (kept + 1) * 16 + size, :]
            rows = outs[d].shape[0]
            outs[d][rows - size : rows, :] = part.astype(outs[d].dtype)


def mix_kernel(slots, per, shards, *refs):
    parts = refs[:shards]
    w_ref, coeff_out, spec_out, c_ref, s_ref = refs[shards:]
    total = parts[0][...]
    for part in parts[1:]:
        total = total + part[...]
    coeff = total.astype(bf16)
    coeff_out[...] = coeff
    c_ref[...] = coeff.astype(f32)
    for m in range(per):
        re_rows = pl.ds(m, slots, stride=2 * per)
        im_rows = pl.ds(per + m, slots, stride=2 * per)
        re = c_ref[re_rows, :].astype(bf16)
        im = c_ref[im_rows, :].astype(bf16)
        weight = w_ref[m].reshape(256, 128)
        s_ref[re_rows, :] = jnp.dot(
            jnp.concatenate([re, -im], axis=1), weight, preferred_element_type=f32
        )
        s_ref[im_rows, :] = jnp.dot(
            jnp.concatenate([im, re], axis=1), weight, preferred_element_type=f32
        )
    spec_out[...] = s_ref[...].astype(bf16)


def sum_kernel(count, *refs):
    total = refs[0][...].astype(f32)
    for part in refs[1:count]:
        total = total + part[...].astype(f32)
    refs[count][...] = total.astype(refs[count].dtype)


def local_sum_kernel(count, rows, *refs):
    size = refs[count].shape[0]
    total = refs[0][...].astype(f32)[rows : rows + size]
    for part in refs[1:count]:
        total = total + part[...].astype(f32)[rows : rows + size]
    refs[count][...] = total


def weight_kernel(lanes, slots, per, *refs):
    coeffs, backs = refs[:lanes], refs[lanes : 2 * lanes]
    out_ref, all_ref, c_ref, b_ref = refs[2 * lanes :]
    each = 2 * per
    kept = slots - 3
    rows = (slots + 1) * each
    for n in range(lanes):
        coeff = coeffs[n][...].astype(f32)
        c_ref[n * rows : n * rows + (kept + 1) * each, :] = coeff[0 : (kept + 1) * each]
        all_ref[n] = coeff[kept * each :]
        b_ref[n * rows : (n + 1) * rows, :] = backs[n][...].astype(f32)[0:rows]
    lane = lax.axis_index("dp")
    for n in range(lanes):
        source = lax.rem(lane - n + lanes, lanes)
        other = lax.rem(n - 1 + 2 * lax.rem(source, 2) + lanes, lanes)
        c_ref[n * rows + (kept + 1) * each : (n + 1) * rows, :] = all_ref[other]
    slots = slots + 1
    for m in range(per):
        re_rows = pl.ds(m, lanes * slots, stride=2 * per)
        im_rows = pl.ds(per + m, lanes * slots, stride=2 * per)
        c_re = c_ref[re_rows, :].astype(bf16)
        c_im = c_ref[im_rows, :].astype(bf16)
        b_re = b_ref[re_rows, :]
        b_im = b_ref[im_rows, :]
        left = jnp.concatenate([c_re, c_im], axis=0)
        right = jnp.concatenate(
            [jnp.concatenate([b_re, b_im], axis=1), jnp.concatenate([b_im, -b_re], axis=1)], axis=0
        )
        right = right.astype(bf16)
        grad = lax.dot_general(
            left, right, (((0,), (0,)), ((), ())), preferred_element_type=f32
        )
        out_ref[m, 0] = grad[:, 0:128]
        out_ref[m, 1] = grad[:, 128:256]


def place_kernel(shards, *refs):
    out_ref = refs[shards]
    size = refs[0].shape[0]
    for d in range(shards):
        i = lax.rem(lax.axis_index("fsdp") - d + shards, shards)
        out_ref[pl.ds(pl.multiple_of(i * size, size), size), :] = refs[d][...]


def whole_vmem(count):
    return [pl.BlockSpec(memory_space=pltpu.VMEM)] * count


def params(limit=VMEM_BYTES):
    return pltpu.CompilerParams(vmem_limit_bytes=limit)


def rotations(value_of, axis, size):
    got = [value_of(0)]
    for d in range(1, size):
        perm = [(s, (s + d) % size) for s in range(size)]
        got.append(lax.ppermute(value_of(d), axis, perm))
    return got


def body(lanes, shards, fields, targets, lists, counts, spectral_w, local_w, proj):
    _, slots, planes, grid_len, _, width = fields.shape
    per = MODES // shards
    split = shards // MX
    cells = grid_len * grid_len
    step_planes = max(n for n in (1, 2, 3, 4) if planes % n == 0)
    blocks = planes // step_planes
    basis, inverse, xtab = phase_constants(grid_len)
    shard = lax.axis_index("fsdp").astype(jnp.int32)
    scalars = functools.partial(Scalars, planes, shards)
    kept = slots - 3

    def field_block(base):
        def block(g, blk, lists_ref, counts_ref, xtab_ref):
            known = scalars(lists_ref, counts_ref)
            blk = jnp.where(base + g < known.count, blk, blocks - 1)
            return (0, known.slot(base + g), blk, 0, 0, 0)

        return pl.BlockSpec((1, 1, step_planes, grid_len, grid_len, width), block)

    def target_block(base):
        def block(g, blk, lists_ref, counts_ref, xtab_ref):
            return (0, scalars(lists_ref, counts_ref).slot(base + g), 0, 0)

        return pl.BlockSpec((1, 1, planes, cells), block)

    def shared_item(g, blk):
        return jnp.maximum(g * blocks + blk - (blocks - 1), 0)

    def fixed(*shape):
        return pl.BlockSpec(shape, lambda g, blk, lists_ref, counts_ref, xtab_ref: (0,) * len(shape))

    items = 2 * blocks + 1
    shared_fields = pl.BlockSpec(
        (1, step_planes, grid_len, grid_len, width),
        lambda g, blk, lists_ref, counts_ref, xtab_ref: (shared_item(g, blk), 0, 0, 0, 0),
    )
    shared_targets = pl.BlockSpec((1, planes, cells), lambda g, blk, lists_ref, counts_ref, xtab_ref: (g, 0, 0))
    part_rows = slots * 16
    forward_scale = float(grid_len) ** (-1.5)
    *late_parts, sent_fields, sent_targets = pl.pallas_call(
        functools.partial(forward_kernel, kept, True, scalars, planes, step_planes, forward_scale),
        grid_spec=pltpu.PrefetchScalarGridSpec(
            num_scalar_prefetch=3,
            grid=(3, blocks),
            in_specs=[field_block(kept), fixed(*basis.shape), target_block(kept)],
            out_specs=[fixed(3 * 16, width)] * MX + [shared_fields, shared_targets],
            scratch_shapes=[pltpu.VMEM((planes, 16, width), f32)],
        ),
        out_shape=[jax.ShapeDtypeStruct((3 * 16, width), f32)] * MX
        + [
            jax.ShapeDtypeStruct((items, step_planes, grid_len, grid_len, width), bf16),
            jax.ShapeDtypeStruct((3, planes, cells), bf16),
        ],
        compiler_params=params(),
        name="forward_shared",
    )(lists, counts, xtab, fields, basis, targets)
    swap = lambda x: lax.ppermute(x, "dp", [(s, s ^ 1) for s in range(lanes)])
    came_fields = swap(sent_fields)
    came_targets = swap(sent_targets)
    parts = pl.pallas_call(
        functools.partial(forward_kernel, 0, False, scalars, planes, step_planes, forward_scale),
        grid_spec=pltpu.PrefetchScalarGridSpec(
            num_scalar_prefetch=3,
            grid=(3, blocks),
            in_specs=[field_block(0), fixed(*basis.shape)] + [fixed(3 * 16, width)] * MX,
            out_specs=[fixed(part_rows, width)] * MX,
            scratch_shapes=[pltpu.VMEM((planes, 16, width), f32)],
        ),
        out_shape=[jax.ShapeDtypeStruct((part_rows, width), f32)] * MX,
        compiler_params=params(),
        cost_estimate=pl.CostEstimate(
            flops=3 * planes * cells * 256 * 256,
            bytes_accessed=3 * planes * cells * width * 2,
            transcendentals=0,
        ),
        name="forward_modes",
    )(lists, counts, xtab, fields, basis, *late_parts)

    def shard_parts(pieces, count):
        if split == 1:
            return lambda d: pieces[d]
        stacked = jnp.stack(pieces).reshape(MX, count, 2, split, per, width)
        stacked = jnp.moveaxis(stacked, 3, 1).reshape(shards, count * 2 * per, width)
        return lambda d: lax.dynamic_index_in_dim(stacked, (shard + d) % shards, 0, keepdims=False)

    def mode_parts(pieces, count):
        if split == 1:
            return pieces
        stacked = jnp.stack(pieces)[(shard - jnp.arange(shards)) % shards]
        stacked = stacked.reshape(MX, split, count, 2, per, width)
        stacked = jnp.moveaxis(stacked, 1, 3).reshape(MX, count * 16, width)
        return [stacked[(-d) % MX] for d in range(MX)]

    came = rotations(shard_parts(parts, slots), "fsdp", shards)
    own_rows = slots * 2 * per
    coeff, own_spectrum = pl.pallas_call(
        functools.partial(mix_kernel, slots, per, shards),
        in_specs=whole_vmem(shards + 1),
        out_specs=whole_vmem(2),
        out_shape=[jax.ShapeDtypeStruct((own_rows, width), bf16)] * 2,
        scratch_shapes=[pltpu.VMEM((own_rows, width), f32)] * 2,
        compiler_params=params(),
        name="mix_modes",
    )(*came, spectral_w)
    came = rotations(lambda d: own_spectrum, "fsdp", shards)
    coeffs = rotations(lambda d: coeff, "dp", lanes)
    came, coeffs = lax.optimization_barrier((came, coeffs))
    spectrum = mode_parts(came, slots)

    local_rows = width // MX
    eye = np.tile(np.eye(64, dtype=ml_dtypes.bfloat16), (1, 2))
    wide_eye = np.eye(128, dtype=np.float32)
    ones = np.ones((128, 128), ml_dtypes.bfloat16)
    ones = np.concatenate([ones, -ones], axis=0)

    def own_block(g, blk, lists_ref, counts_ref, xtab_ref):
        known = scalars(lists_ref, counts_ref)
        count, partner, slot = known.count, known.partner, known.slot(g)
        away = (g >= kept) & shared_live(slots, kept, blocks, count, partner, g - kept, blk)
        blk = jnp.where(away, max(blocks - 2, 0), blk)
        return (0, slot, jnp.where(g < count, blk, blocks - 1), 0, 0, 0)

    def came_item(g, blk, lists_ref, counts_ref):
        some = kept < scalars(lists_ref, counts_ref).partner
        return jnp.where(some, shared_item(g, blk), 0), jnp.where(some, g, 0)

    came_block = pl.BlockSpec(
        (1, step_planes, grid_len, grid_len, width),
        lambda g, blk, lists_ref, counts_ref, xtab_ref: (came_item(g, blk, lists_ref, counts_ref)[0], 0, 0, 0, 0),
    )
    came_lines = pl.BlockSpec(
        (1, planes, cells), lambda g, blk, lists_ref, counts_ref, xtab_ref: (came_item(g, blk, lists_ref, counts_ref)[1], 0, 0)
    )

    def backward(own, fields_, targets_, spectrum_, given):
        positions = kept + 1 if own else 3
        rows = (kept + 1 if own else slots + 1) * 16 + local_rows
        own_fields = pl.BlockSpec((1, 1, step_planes, grid_len, grid_len, width), own_block)
        return pl.pallas_call(
            functools.partial(
                backward_kernel, slots, own, scalars, lanes, planes, step_planes, 128, float(MODES) ** (-0.5)
            ),
            grid_spec=pltpu.PrefetchScalarGridSpec(
                num_scalar_prefetch=3,
                grid=(positions, blocks),
                in_specs=([own_fields, target_block(0)] if own else [came_block, came_lines])
                + [fixed(part_rows, width)] * MX
                + [
                    fixed(width, width),
                    fixed(1, width),
                    fixed(*inverse.shape),
                    fixed(*basis.shape),
                    fixed(*eye.shape),
                    fixed(*wide_eye.shape),
                    fixed(*ones.shape),
                ]
                + [fixed(*g.shape) for g in given],
                out_specs=[fixed(rows, width)] * MX,
                scratch_shapes=[
                    pltpu.VMEM((2, 256, width), bf16),
                    pltpu.VMEM((2, cells // 3, width), f32),
                    pltpu.VMEM((2, cells // 3, width), f32),
                    pltpu.VMEM((2, cells // 6, 2 * width), bf16),
                    pltpu.VMEM((2, cells // 6, width), f32),
                    pltpu.VMEM((2, cells // 3, width), bf16),
                    pltpu.VMEM((width, width), f32),
                    pltpu.VMEM((planes, 16, width), f32),
                    pltpu.VMEM((planes, 16, 2 * cells), bf16),
                    pltpu.VMEM((MX, 16, width), f32),
                    pltpu.VMEM((step_planes, cells, width), bf16),
                    pltpu.VMEM((step_planes, 16, 2 * cells), bf16),
                    pltpu.VMEM((step_planes, 16, width), f32),
                    pltpu.VMEM((planes, 8, cells), f32),
                    pltpu.VMEM((step_planes, 8, cells), f32),
                ],
            ),
            out_shape=[jax.ShapeDtypeStruct((rows, width), f32 if own else bf16)] * MX,
            compiler_params=params(LARGE_VMEM_BYTES),
            cost_estimate=pl.CostEstimate(
                flops=4 * positions * planes * cells * 256 * 256,
                bytes_accessed=positions * planes * cells * width * 2,
                transcendentals=0,
            ),
            name="backward_own" if own else "backward_shared",
        )(
            lists, counts, xtab, fields_, targets_, *spectrum_, local_w, proj.reshape(1, width),
            inverse, basis, eye, wide_eye, ones, *given,
        )

    came_spectrum = [swap(piece) for piece in spectrum]
    own_results = backward(True, fields, targets, spectrum, [])
    results = backward(False, came_fields, came_targets, came_spectrum, own_results)
    places = slots + 1
    part_rows = places * 16
    place_rows = places * 2 * per

    if split == 1:
        chunk = lambda d: results[d]
    else:
        backs = shard_parts([r[:part_rows] for r in results], places)
        local = jnp.concatenate([r[part_rows:] for r in results], axis=0)
        rows = width // shards
        chunk = lambda d: jnp.concatenate(
            [backs(d), lax.dynamic_slice_in_dim(local, (shard + d) % shards * rows, rows, 0)], axis=0
        )
    came = rotations(chunk, "fsdp", shards)
    own_sum = pl.pallas_call(
        functools.partial(sum_kernel, shards),
        in_specs=whole_vmem(shards),
        out_specs=pl.BlockSpec(memory_space=pltpu.VMEM),
        out_shape=jax.ShapeDtypeStruct(came[0].shape, bf16),
        compiler_params=params(),
        name="sum_shards",
    )(*came)
    sums = rotations(lambda d: own_sum, "dp", lanes)
    own_local = pl.pallas_call(
        functools.partial(local_sum_kernel, lanes, place_rows),
        in_specs=whole_vmem(lanes),
        out_specs=pl.BlockSpec(memory_space=pltpu.VMEM),
        out_shape=jax.ShapeDtypeStruct((width // shards, width), f32),
        compiler_params=params(),
        name="sum_local",
    )(*sums)
    locals_ = rotations(lambda d: own_local, "fsdp", shards)
    grad_spectral = pl.pallas_call(
        functools.partial(weight_kernel, lanes, slots, per),
        in_specs=whole_vmem(2 * lanes),
        out_specs=pl.BlockSpec(memory_space=pltpu.VMEM),
        out_shape=jax.ShapeDtypeStruct((per, 2, width, width), f32),
        scratch_shapes=[pltpu.VMEM((lanes, 3 * 2 * per, width), f32)]
        + [pltpu.VMEM((lanes * place_rows, width), f32)] * 2,
        compiler_params=params(),
        cost_estimate=pl.CostEstimate(
            flops=2 * per * 256 * 128 * 256, bytes_accessed=2 * per * 2 * width * width * 4, transcendentals=0
        ),
        name="weight_grad",
    )(*coeffs, *sums)
    grad_local = pl.pallas_call(
        functools.partial(place_kernel, shards),
        in_specs=whole_vmem(shards),
        out_specs=pl.BlockSpec(memory_space=pltpu.VMEM),
        out_shape=jax.ShapeDtypeStruct((width, width), f32),
        compiler_params=params(),
        name="place_local",
    )(*locals_)
    return (grad_spectral, grad_local)


def solution(mesh):
    return jax.shard_map(
        functools.partial(body, mesh.shape["dp"], mesh.shape["fsdp"]),
        mesh=mesh,
        in_specs=(
            P("dp", None, "fsdp", None, None, None),
            P("dp", None, "fsdp", None),
            P("dp", None),
            P(),
            P("fsdp", None, None, None),
            P(),
            P(),
        ),
        out_specs=(P("fsdp", None, None, None), P()),
        check_vma=False,
    )
```

```python
import functools
import math

import jax
import jax.numpy as jnp
import ml_dtypes
import numpy as np
from jax import lax
from jax.experimental import pallas as pl
from jax.experimental.pallas import tpu as pltpu
from jax.sharding import PartitionSpec as P

MX = 4
MY = 4
MZ = 2
MODES = MX * MY * MZ
VMEM_BYTES = 40 * 1024 * 1024
LARGE_VMEM_BYTES = 56 * 1024 * 1024
f32 = jnp.float32
bf16 = jnp.bfloat16
inv_root_two_pi = 0.3989422804014327
half_log2e = 0.7213475204444817
root_half = 0.7071067811865476


def split_bf16(values):
    high = values.astype(ml_dtypes.bfloat16)
    low = (values - high.astype(np.float64)).astype(ml_dtypes.bfloat16)
    return high, low


def angles(mode_ids, length):
    product = np.outer(mode_ids, np.arange(length)) % length
    return product * (2.0 * math.pi / length)


def phase_constants(length):
    y_angle = angles(np.arange(MY) - MY // 2, length)
    z_angle = angles(np.arange(MZ), length)
    rounded = lambda v: v.astype(np.float32).astype(ml_dtypes.bfloat16).astype(np.float64)
    cz, sz = rounded(np.cos(z_angle)), rounded(-np.sin(z_angle))
    cy, sy = np.cos(y_angle), -np.sin(y_angle)
    both = lambda a, b: (a[:, None, :, None] * b[None, :, None, :]).reshape(MY * MZ, length * length)
    fwd = np.concatenate([both(cy, cz) - both(sy, sz), both(sy, cz) + both(cy, sz)], axis=0)
    fwd = np.concatenate(split_bf16(fwd), axis=0)
    cz, sz = np.cos(z_angle), np.sin(z_angle)
    cy, sy = np.cos(y_angle), np.sin(y_angle)
    inv = np.concatenate([both(cy, cz) - both(sy, sz), -(both(sy, cz) + both(cy, sz))], axis=0).T
    high, low = split_bf16(inv)
    pad = np.zeros((length * length, 128 - 4 * high.shape[1]), ml_dtypes.bfloat16)
    inv = np.concatenate([high, low, high, low, pad], axis=1)
    x_angle = angles(np.arange(MX) - MX // 2, length).T
    xtab = np.stack([np.cos(x_angle), np.sin(x_angle)], axis=2).astype(np.float32)
    return fwd, inv, xtab.reshape(-1)


class Scalars:
    def __init__(self, planes, shards, lists_ref, counts_ref):
        self.lists, self.counts = lists_ref, counts_ref
        self.lane = lax.axis_index("dp")
        shard = lax.axis_index("fsdp")
        self.shard = shard if shards == MX else 0 * shard
        self.first = shard * planes

    @property
    def count(self):
        return self.counts[self.lane]

    @property
    def partner(self):
        return self.counts[self.lane ^ 1]

    def total(self, lanes):
        total = self.counts[0]
        for lane in range(1, lanes):
            total = total + self.counts[lane]
        return total

    def slot(self, position):
        return self.lists[0, jnp.minimum(position, self.count - 1)]


def combine_planes(q_ref, xtab_ref, cell0, shard, planes, scale, store):
    for d in range(MX):
        i = lax.rem(shard + d, MX)
        re = jnp.zeros((8, 128), f32)
        im = jnp.zeros((8, 128), f32)
        for a in range(planes):
            at = ((cell0 + a) * MX + i) * 2
            c = xtab_ref[at]
            s = xtab_ref[at + 1]
            q_re = q_ref[a, 0:8, :]
            q_im = q_ref[a, 8:16, :]
            re = re + (q_re * c + q_im * s)
            im = im + (q_im * c - q_re * s)
        store(d, re * scale, im * scale)


def forward_kernel(
    base, sends, scalars, planes, step_planes, scale, lists_ref, counts_ref, xtab_ref, f_ref, basis_ref, *rest
):
    if sends:
        t_ref, outs, send_ref, t_out_ref, q_ref = rest[0], rest[1 : MX + 1], *rest[MX + 1 :]
    else:
        given, outs, q_ref = rest[:MX], rest[MX : 2 * MX], rest[2 * MX]
    known = scalars(lists_ref, counts_ref)
    g, blk = pl.program_id(0), pl.program_id(1)
    live = base + g < known.count
    row = pl.multiple_of(g * 16, 16)

    if not sends:

        @pl.when((g == 0) & (blk == 0))
        def _():
            rows = given[0].shape[0]
            for d in range(MX):
                outs[d][rows : 2 * rows, :] = given[d][...]

    @pl.when(live)
    def _():
        cells = f_ref.shape[3] * f_ref.shape[4]
        for p in range(step_planes):
            field = f_ref[0, 0, p].reshape(cells, 128)
            part = jnp.dot(basis_ref[...], field, preferred_element_type=f32)
            q_ref[blk * step_planes + p] = part[0:16] + part[16:32]
            if sends:
                send_ref[0, p] = f_ref[0, 0, p]
        if sends:

            @pl.when(blk == 0)
            def _():
                t_out_ref[0] = t_ref[0, 0]

        @pl.when(blk == planes // step_planes - 1)
        def _():
            def store(d, re, im):
                outs[d][pl.ds(row, 8), :] = re
                outs[d][pl.ds(row + 8, 8), :] = im

            combine_planes(
                q_ref, xtab_ref, known.first, known.shard, planes, scale, store
            )

    @pl.when(jnp.logical_not(live) & (blk == 0))
    def _():
        for out in outs:
            out[pl.ds(row, 16), :] = jnp.zeros((16, 128), f32)


def shared_live(slots, kept, blocks, count, partner, g, blk):
    return (kept + g < count) & ((g > 0) | ((blk == blocks - 1) & (partner <= 1)))


def backward_kernel(
    slots, own, scalars, lanes, planes, step_planes, rows_step, scale,
    lists_ref, counts_ref, xtab_ref, f_ref, t_ref, *rest
):
    specs = rest[:MX]
    w_ref, proj_ref, inv_ref, basis_ref, eye_ref, wide_eye_ref, ones_ref = rest[MX : MX + 7]
    rest = rest[MX + 7 :]
    if not own:
        given, rest = rest[:MX], rest[MX:]
    outs = rest[:MX]
    rhs_ref, pre_ref, slope_ref, both_ref, resid_ref, d_ref, total_ref, q_ref, t16_ref, spec_ref, field_ref, line_ref, near_ref, far_t_ref, far_line_ref = rest[MX:]
    known = scalars(lists_ref, counts_ref)
    kept = slots - 3
    g, blk = pl.program_id(0), pl.program_id(1)
    blocks = planes // step_planes
    count, partner = known.count, known.partner
    if own:
        some = g < count
        away = (g >= kept) & shared_live(slots, kept, blocks, count, partner, g - kept, blk)
        live = some & jnp.logical_not(away)
        positions, spec_row, out_row = kept + 1, g * 16, g * 16
        plane_of = lambda p: f_ref[0, 0, p].reshape(cells, 128)
        lines_of = lambda: t_ref[0, 0].astype(f32)
    else:
        some = kept + g < partner
        live = shared_live(slots, kept, blocks, partner, count, g, blk)
        positions, spec_row, out_row = 3, (kept + g) * 16, (kept + 1 + g) * 16
        plane_of = lambda p: f_ref[0, p].reshape(cells, 128)
        lines_of = lambda: t_ref[0].astype(f32)
    row = pl.multiple_of(out_row, 16)
    shard = known.shard
    cell0 = known.first
    cells = inv_ref.shape[0]
    third = cells // 3
    half = third // 2
    dotted = third // 3
    unroll = step_planes

    grids = jnp.full((1, 128), known.total(lanes).astype(f32), f32)
    root = lax.rsqrt(grids)
    root = root * (1.5 - 0.5 * grids * root * root)

    @pl.when((g == 0) & (blk == 0))
    def _():
        total_ref[...] = jnp.zeros_like(total_ref)
        for n in range(2):
            rhs_ref[n, 0:128, :] = w_ref[...]
            rhs_ref[n, 128:256, :] = jnp.zeros((128, 128), bf16)
        if not own:
            rows = (kept + 1) * 16
            for d in range(MX):
                outs[d][0:rows, :] = given[d][0:rows, :].astype(bf16)

    @pl.when(some & (blk == 0))
    def _():
        q_ref[...] = jnp.zeros_like(q_ref)
        lines = lines_of() * root[:, 0:1]
        for a in range(planes):
            far_t_ref[a] = jnp.broadcast_to(lines[a : a + 1, :], (8, cells))
        high = lines.astype(bf16).astype(f32)
        low = lines - high
        early = lax.broadcasted_iota(jnp.int32, (planes, 128), 1) < 64
        for at in range(0, cells, 128):
            part_h, part_l = high[:, at : at + 128], low[:, at : at + 128]
            turned_h, turned_l = pltpu.roll(part_h, 64, 1), pltpu.roll(part_l, 64, 1)
            both = (jnp.where(early, part_h, turned_l), jnp.where(early, turned_h, part_l))
            for n in range(2):
                for a in range(planes):
                    line = jnp.broadcast_to(both[n][a : a + 1, :], (16, 128))
                    t16_ref[a, :, 2 * at + 128 * n : 2 * at + 128 * (n + 1)] = line.astype(bf16)
        for d in range(MX):
            spec_ref[d] = specs[d][pl.ds(pl.multiple_of(spec_row, 16), 16), :].astype(f32)

    @pl.when(live)
    def _():
        gate = proj_ref[...] * root * 0.5
        edge = proj_ref[...] * root * inv_root_two_pi

        def first_rows(a, rhs):
            re = jnp.zeros((8, 128), f32)
            im = jnp.zeros((8, 128), f32)
            for d in range(MX):
                i = lax.rem(shard - d + MX, MX)
                at = ((cell0 + a) * MX + i) * 2
                c = xtab_ref[at]
                s = xtab_ref[at + 1]
                s_re = spec_ref[d, 0:8, :]
                s_im = spec_ref[d, 8:16, :]
                re = re + (s_re * c - s_im * s)
                im = im + (s_re * s + s_im * c)
            first = jnp.concatenate([re, im], axis=0) * scale
            high = first.astype(bf16)
            low = (first - high.astype(f32)).astype(bf16)
            rhs[128:144, :] = high
            rhs[144:160, :] = high
            rhs[160:176, :] = low
            rhs[176:192, :] = low

        def planes_together(n, carry):
            units = [(u, k) for u in range(unroll) for k in range(3)]
            for u in range(unroll):
                field_ref[u] = plane_of(n * unroll + u)
                line_ref[u] = t16_ref[blk * step_planes + n * unroll + u]
                far_line_ref[u] = far_t_ref[blk * step_planes + n * unroll + u]

            def before(s, r0):
                u, k = units[s]
                rhs = rhs_ref.at[u % 2]
                if k == 0 and r0 == 0:
                    first_rows(blk * step_planes + n * unroll + u, rhs)
                part = slice(k * third + r0, k * third + r0 + half)
                lhs = jnp.concatenate([field_ref[u, part, :], inv_ref[part, :]], axis=1)
                pre_ref[s % 2, r0 : r0 + half, :] = jnp.dot(lhs, rhs[...], preferred_element_type=f32)

            def elementwise(s, r0):
                u, k = units[s]
                rows = slice(r0, r0 + rows_step)
                pre = pre_ref[s % 2, rows, :]
                bell = jnp.exp2(pre * pre * (-half_log2e))
                gated = (1.0 + lax.erf(pre * root_half)) * gate
                slope_ref[s % 2, rows, :] = gated + pre * bell * edge
                active = pre * gated
                if r0 >= dotted:
                    at = k * third + r0
                    line = far_line_ref[u, :, at : at + 128]
                    wanted = jnp.concatenate([line] * (rows_step // 8), axis=0)
                    resid = jnp.sum(active - wanted * wide_eye_ref[...], axis=1, keepdims=True)
                    resid_ref[s % 2, r0 - dotted : r0 - dotted + rows_step, :] = jnp.broadcast_to(
                        resid, (rows_step, 128)
                    )
                    return
                both_ref[s % 2, rows, 0:128] = active.astype(bf16)
                for r1 in range(r0, r0 + rows_step, 16):
                    at = 2 * (k * third + r1 - r1 % 64)
                    line = line_ref[u, :, at : at + 128]
                    both_ref[s % 2, r1 : r1 + 16, 128:256] = line * eye_ref[r1 % 64 : r1 % 64 + 16, :]

            def after(s, r0):
                rows = slice(dotted, third) if r0 else slice(0, dotted)
                if r0:
                    resid = resid_ref[s % 2]
                else:
                    resid = jnp.dot(both_ref[s % 2], ones_ref[...], preferred_element_type=f32)
                d_ref[s % 2, rows, :] = (resid * slope_ref[s % 2, rows, :]).astype(bf16)

            def last(s):
                u, k = units[s]
                part = slice(k * third, (k + 1) * third)
                lhs = jnp.concatenate([field_ref[u, part, :].T, basis_ref[:, part]], axis=0)
                sums = jnp.dot(lhs, d_ref[s % 2], preferred_element_type=f32)
                total_ref[...] += sums[0:128]
                back = sums[128:144] + sums[144:160]
                near_ref[u] = back if k == 0 else near_ref[u] + back

            pieces = third // rows_step
            for s in range(len(units) + 3):
                for piece in range(pieces):
                    r0 = piece * rows_step
                    if s < len(units) and r0 % half == 0:
                        before(s, r0)
                    if 0 <= s - 2 < len(units) and r0 % half == 0:
                        after(s - 2, r0)
                    if 0 <= s - 3 and piece == pieces // 2 - 1:
                        last(s - 3)
                    if 0 <= s - 1 < len(units):
                        elementwise(s - 1, r0)
            for u in range(unroll):
                q_ref[blk * step_planes + n * unroll + u] = near_ref[u]
            return carry

        lax.fori_loop(0, step_planes // unroll, planes_together, 0)

    @pl.when(some & (blk == blocks - 1))
    def _():
        def store(d, re, im):
            both = jnp.concatenate([re, im], axis=0)
            outs[d][pl.ds(row, 16), :] = both.astype(outs[d].dtype)

        combine_planes(q_ref, xtab_ref, cell0, shard, planes, scale, store)

    @pl.when(jnp.logical_not(some) & (blk == 0))
    def _():
        for out in outs:
            out[pl.ds(row, 16), :] = jnp.zeros((16, 128), out.dtype)

    @pl.when((g == positions - 1) & (blk == blocks - 1))
    def _():
        size = 128 // MX
        for d in range(MX):
            i = lax.rem(shard + d, MX)
            at = pl.multiple_of(i * size, size)
            part = total_ref[pl.ds(at, size), :]
            if not own:
                part = part + given[d][(kept + 1) * 16 : (kept + 1) * 16 + size, :]
            rows = outs[d].shape[0]
            outs[d][rows - size : rows, :] = part.astype(outs[d].dtype)


def mix_kernel(slots, per, shards, *refs):
    parts = refs[:shards]
    w_ref, coeff_out, spec_out, c_ref, s_ref = refs[shards:]
    total = parts[0][...]
    for part in parts[1:]:
        total = total + part[...]
    coeff = total.astype(bf16)
    coeff_out[...] = coeff
    c_ref[...] = coeff.astype(f32)
    for m in range(per):
        re_rows = pl.ds(m, slots, stride=2 * per)
        im_rows = pl.ds(per + m, slots, stride=2 * per)
        re = c_ref[re_rows, :].astype(bf16)
        im = c_ref[im_rows, :].astype(bf16)
        weight = w_ref[m].reshape(256, 128)
        s_ref[re_rows, :] = jnp.dot(
            jnp.concatenate([re, -im], axis=1), weight, preferred_element_type=f32
        )
        s_ref[im_rows, :] = jnp.dot(
            jnp.concatenate([im, re], axis=1), weight, preferred_element_type=f32
        )
    spec_out[...] = s_ref[...].astype(bf16)


def sum_kernel(count, *refs):
    total = refs[0][...].astype(f32)
    for part in refs[1:count]:
        total = total + part[...].astype(f32)
    refs[count][...] = total.astype(refs[count].dtype)


def local_sum_kernel(count, rows, *refs):
    size = refs[count].shape[0]
    total = refs[0][...].astype(f32)[rows : rows + size]
    for part in refs[1:count]:
        total = total + part[...].astype(f32)[rows : rows + size]
    refs[count][...] = total


def weight_kernel(lanes, slots, per, *refs):
    coeffs, backs = refs[:lanes], refs[lanes : 2 * lanes]
    out_ref, all_ref, c_ref, b_ref = refs[2 * lanes :]
    each = 2 * per
    kept = slots - 3
    rows = (slots + 1) * each
    for n in range(lanes):
        coeff = coeffs[n][...].astype(f32)
        c_ref[n * rows : n * rows + (kept + 1) * each, :] = coeff[0 : (kept + 1) * each]
        all_ref[n] = coeff[kept * each :]
        b_ref[n * rows : (n + 1) * rows, :] = backs[n][...].astype(f32)[0:rows]
    lane = lax.axis_index("dp")
    for n in range(lanes):
        source = lax.rem(lane - n + lanes, lanes)
        other = lax.rem(n - 1 + 2 * lax.rem(source, 2) + lanes, lanes)
        c_ref[n * rows + (kept + 1) * each : (n + 1) * rows, :] = all_ref[other]
    slots = slots + 1
    for m in range(per):
        re_rows = pl.ds(m, lanes * slots, stride=2 * per)
        im_rows = pl.ds(per + m, lanes * slots, stride=2 * per)
        c_re = c_ref[re_rows, :].astype(bf16)
        c_im = c_ref[im_rows, :].astype(bf16)
        b_re = b_ref[re_rows, :]
        b_im = b_ref[im_rows, :]
        left = jnp.concatenate([c_re, c_im], axis=0)
        right = jnp.concatenate(
            [jnp.concatenate([b_re, b_im], axis=1), jnp.concatenate([b_im, -b_re], axis=1)], axis=0
        )
        right = right.astype(bf16)
        grad = lax.dot_general(
            left, right, (((0,), (0,)), ((), ())), preferred_element_type=f32
        )
        out_ref[m, 0] = grad[:, 0:128]
        out_ref[m, 1] = grad[:, 128:256]


def place_kernel(shards, *refs):
    out_ref = refs[shards]
    size = refs[0].shape[0]
    for d in range(shards):
        i = lax.rem(lax.axis_index("fsdp") - d + shards, shards)
        out_ref[pl.ds(pl.multiple_of(i * size, size), size), :] = refs[d][...]


def whole_vmem(count):
    return [pl.BlockSpec(memory_space=pltpu.VMEM)] * count


def params(limit=VMEM_BYTES):
    return pltpu.CompilerParams(vmem_limit_bytes=limit)


def rotations(value_of, axis, size):
    got = [value_of(0)]
    for d in range(1, size):
        perm = [(s, (s + d) % size) for s in range(size)]
        got.append(lax.ppermute(value_of(d), axis, perm))
    return got


def body(lanes, shards, fields, targets, lists, counts, spectral_w, local_w, proj):
    _, slots, planes, grid_len, _, width = fields.shape
    per = MODES // shards
    split = shards // MX
    cells = grid_len * grid_len
    step_planes = max(n for n in (1, 2, 3, 4) if planes % n == 0)
    blocks = planes // step_planes
    basis, inverse, xtab = phase_constants(grid_len)
    shard = lax.axis_index("fsdp").astype(jnp.int32)
    scalars = functools.partial(Scalars, planes, shards)
    kept = slots - 3

    def field_block(base):
        def block(g, blk, lists_ref, counts_ref, xtab_ref):
            known = scalars(lists_ref, counts_ref)
            blk = jnp.where(base + g < known.count, blk, blocks - 1)
            return (0, known.slot(base + g), blk, 0, 0, 0)

        return pl.BlockSpec((1, 1, step_planes, grid_len, grid_len, width), block)

    def target_block(base):
        def block(g, blk, lists_ref, counts_ref, xtab_ref):
            return (0, scalars(lists_ref, counts_ref).slot(base + g), 0, 0)

        return pl.BlockSpec((1, 1, planes, cells), block)

    def shared_item(g, blk):
        return jnp.maximum(g * blocks + blk - (blocks - 1), 0)

    def fixed(*shape):
        return pl.BlockSpec(shape, lambda g, blk, lists_ref, counts_ref, xtab_ref: (0,) * len(shape))

    items = 2 * blocks + 1
    shared_fields = pl.BlockSpec(
        (1, step_planes, grid_len, grid_len, width),
        lambda g, blk, lists_ref, counts_ref, xtab_ref: (shared_item(g, blk), 0, 0, 0, 0),
    )
    shared_targets = pl.BlockSpec((1, planes, cells), lambda g, blk, lists_ref, counts_ref, xtab_ref: (g, 0, 0))
    part_rows = slots * 16
    forward_scale = float(grid_len) ** (-1.5)
    *late_parts, sent_fields, sent_targets = pl.pallas_call(
        functools.partial(forward_kernel, kept, True, scalars, planes, step_planes, forward_scale),
        grid_spec=pltpu.PrefetchScalarGridSpec(
            num_scalar_prefetch=3,
            grid=(3, blocks),
            in_specs=[field_block(kept), fixed(*basis.shape), target_block(kept)],
            out_specs=[fixed(3 * 16, width)] * MX + [shared_fields, shared_targets],
            scratch_shapes=[pltpu.VMEM((planes, 16, width), f32)],
        ),
        out_shape=[jax.ShapeDtypeStruct((3 * 16, width), f32)] * MX
        + [
            jax.ShapeDtypeStruct((items, step_planes, grid_len, grid_len, width), bf16),
            jax.ShapeDtypeStruct((3, planes, cells), bf16),
        ],
        compiler_params=params(),
        name="forward_shared",
    )(lists, counts, xtab, fields, basis, targets)
    swap = lambda x: lax.ppermute(x, "dp", [(s, s ^ 1) for s in range(lanes)])
    came_fields = swap(sent_fields)
    came_targets = swap(sent_targets)
    parts = pl.pallas_call(
        functools.partial(forward_kernel, 0, False, scalars, planes, step_planes, forward_scale),
        grid_spec=pltpu.PrefetchScalarGridSpec(
            num_scalar_prefetch=3,
            grid=(3, blocks),
            in_specs=[field_block(0), fixed(*basis.shape)] + [fixed(3 * 16, width)] * MX,
            out_specs=[fixed(part_rows, width)] * MX,
            scratch_shapes=[pltpu.VMEM((planes, 16, width), f32)],
        ),
        out_shape=[jax.ShapeDtypeStruct((part_rows, width), f32)] * MX,
        compiler_params=params(),
        cost_estimate=pl.CostEstimate(
            flops=3 * planes * cells * 256 * 256,
            bytes_accessed=3 * planes * cells * width * 2,
            transcendentals=0,
        ),
        name="forward_modes",
    )(lists, counts, xtab, fields, basis, *late_parts)

    def shard_parts(pieces, count):
        if split == 1:
            return lambda d: pieces[d]
        stacked = jnp.stack(pieces).reshape(MX, count, 2, split, per, width)
        stacked = jnp.moveaxis(stacked, 3, 1).reshape(shards, count * 2 * per, width)
        return lambda d: lax.dynamic_index_in_dim(stacked, (shard + d) % shards, 0, keepdims=False)

    def mode_parts(pieces, count):
        if split == 1:
            return pieces
        stacked = jnp.stack(pieces)[(shard - jnp.arange(shards)) % shards]
        stacked = stacked.reshape(MX, split, count, 2, per, width)
        stacked = jnp.moveaxis(stacked, 1, 3).reshape(MX, count * 16, width)
        return [stacked[(-d) % MX] for d in range(MX)]

    came = rotations(shard_parts(parts, slots), "fsdp", shards)
    own_rows = slots * 2 * per
    coeff, own_spectrum = pl.pallas_call(
        functools.partial(mix_kernel, slots, per, shards),
        in_specs=whole_vmem(shards + 1),
        out_specs=whole_vmem(2),
        out_shape=[jax.ShapeDtypeStruct((own_rows, width), bf16)] * 2,
        scratch_shapes=[pltpu.VMEM((own_rows, width), f32)] * 2,
        compiler_params=params(),
        name="mix_modes",
    )(*came, spectral_w)
    came = rotations(lambda d: own_spectrum, "fsdp", shards)
    coeffs = rotations(lambda d: coeff, "dp", lanes)
    came, coeffs = lax.optimization_barrier((came, coeffs))
    spectrum = mode_parts(came, slots)

    local_rows = width // MX
    eye = np.tile(np.eye(64, dtype=ml_dtypes.bfloat16), (1, 2))
    wide_eye = np.eye(128, dtype=np.float32)
    ones = np.ones((128, 128), ml_dtypes.bfloat16)
    ones = np.concatenate([ones, -ones], axis=0)

    def own_block(g, blk, lists_ref, counts_ref, xtab_ref):
        known = scalars(lists_ref, counts_ref)
        count, partner, slot = known.count, known.partner, known.slot(g)
        away = (g >= kept) & shared_live(slots, kept, blocks, count, partner, g - kept, blk)
        blk = jnp.where(away, max(blocks - 2, 0), blk)
        return (0, slot, jnp.where(g < count, blk, blocks - 1), 0, 0, 0)

    def came_item(g, blk, lists_ref, counts_ref):
        some = kept < scalars(lists_ref, counts_ref).partner
        return jnp.where(some, shared_item(g, blk), 0), jnp.where(some, g, 0)

    came_block = pl.BlockSpec(
        (1, step_planes, grid_len, grid_len, width),
        lambda g, blk, lists_ref, counts_ref, xtab_ref: (came_item(g, blk, lists_ref, counts_ref)[0], 0, 0, 0, 0),
    )
    came_lines = pl.BlockSpec(
        (1, planes, cells), lambda g, blk, lists_ref, counts_ref, xtab_ref: (came_item(g, blk, lists_ref, counts_ref)[1], 0, 0)
    )

    def backward(own, fields_, targets_, spectrum_, given):
        positions = kept + 1 if own else 3
        rows = (kept + 1 if own else slots + 1) * 16 + local_rows
        own_fields = pl.BlockSpec((1, 1, step_planes, grid_len, grid_len, width), own_block)
        return pl.pallas_call(
            functools.partial(
                backward_kernel, slots, own, scalars, lanes, planes, step_planes, 128, float(MODES) ** (-0.5)
            ),
            grid_spec=pltpu.PrefetchScalarGridSpec(
                num_scalar_prefetch=3,
                grid=(positions, blocks),
                in_specs=([own_fields, target_block(0)] if own else [came_block, came_lines])
                + [fixed(part_rows, width)] * MX
                + [
                    fixed(width, width),
                    fixed(1, width),
                    fixed(*inverse.shape),
                    fixed(*basis.shape),
                    fixed(*eye.shape),
                    fixed(*wide_eye.shape),
                    fixed(*ones.shape),
                ]
                + [fixed(*g.shape) for g in given],
                out_specs=[fixed(rows, width)] * MX,
                scratch_shapes=[
                    pltpu.VMEM((2, 256, width), bf16),
                    pltpu.VMEM((2, cells // 3, width), f32),
                    pltpu.VMEM((2, cells // 3, width), f32),
                    pltpu.VMEM((2, cells // 9, 2 * width), bf16),
                    pltpu.VMEM((2, cells // 9 * 2, width), f32),
                    pltpu.VMEM((2, cells // 3, width), bf16),
                    pltpu.VMEM((width, width), f32),
                    pltpu.VMEM((planes, 16, width), f32),
                    pltpu.VMEM((planes, 16, 2 * cells), bf16),
                    pltpu.VMEM((MX, 16, width), f32),
                    pltpu.VMEM((step_planes, cells, width), bf16),
                    pltpu.VMEM((step_planes, 16, 2 * cells), bf16),
                    pltpu.VMEM((step_planes, 16, width), f32),
                    pltpu.VMEM((planes, 8, cells), f32),
                    pltpu.VMEM((step_planes, 8, cells), f32),
                ],
            ),
            out_shape=[jax.ShapeDtypeStruct((rows, width), f32 if own else bf16)] * MX,
            compiler_params=params(LARGE_VMEM_BYTES),
            cost_estimate=pl.CostEstimate(
                flops=4 * positions * planes * cells * 256 * 256,
                bytes_accessed=positions * planes * cells * width * 2,
                transcendentals=0,
            ),
            name="backward_own" if own else "backward_shared",
        )(
            lists, counts, xtab, fields_, targets_, *spectrum_, local_w, proj.reshape(1, width),
            inverse, basis, eye, wide_eye, ones, *given,
        )

    came_spectrum = [swap(piece) for piece in spectrum]
    own_results = backward(True, fields, targets, spectrum, [])
    results = backward(False, came_fields, came_targets, came_spectrum, own_results)
    places = slots + 1
    part_rows = places * 16
    place_rows = places * 2 * per

    if split == 1:
        chunk = lambda d: results[d]
    else:
        backs = shard_parts([r[:part_rows] for r in results], places)
        local = jnp.concatenate([r[part_rows:] for r in results], axis=0)
        rows = width // shards
        chunk = lambda d: jnp.concatenate(
            [backs(d), lax.dynamic_slice_in_dim(local, (shard + d) % shards * rows, rows, 0)], axis=0
        )
    came = rotations(chunk, "fsdp", shards)
    own_sum = pl.pallas_call(
        functools.partial(sum_kernel, shards),
        in_specs=whole_vmem(shards),
        out_specs=pl.BlockSpec(memory_space=pltpu.VMEM),
        out_shape=jax.ShapeDtypeStruct(came[0].shape, bf16),
        compiler_params=params(),
        name="sum_shards",
    )(*came)
    sums = rotations(lambda d: own_sum, "dp", lanes)
    own_local = pl.pallas_call(
        functools.partial(local_sum_kernel, lanes, place_rows),
        in_specs=whole_vmem(lanes),
        out_specs=pl.BlockSpec(memory_space=pltpu.VMEM),
        out_shape=jax.ShapeDtypeStruct((width // shards, width), f32),
        compiler_params=params(),
        name="sum_local",
    )(*sums)
    locals_ = rotations(lambda d: own_local, "fsdp", shards)
    grad_spectral = pl.pallas_call(
        functools.partial(weight_kernel, lanes, slots, per),
        in_specs=whole_vmem(2 * lanes),
        out_specs=pl.BlockSpec(memory_space=pltpu.VMEM),
        out_shape=jax.ShapeDtypeStruct((per, 2, width, width), f32),
        scratch_shapes=[pltpu.VMEM((lanes, 3 * 2 * per, width), f32)]
        + [pltpu.VMEM((lanes * place_rows, width), f32)] * 2,
        compiler_params=params(),
        cost_estimate=pl.CostEstimate(
            flops=2 * per * 256 * 128 * 256, bytes_accessed=2 * per * 2 * width * width * 4, transcendentals=0
        ),
        name="weight_grad",
    )(*coeffs, *sums)
    grad_local = pl.pallas_call(
        functools.partial(place_kernel, shards),
        in_specs=whole_vmem(shards),
        out_specs=pl.BlockSpec(memory_space=pltpu.VMEM),
        out_shape=jax.ShapeDtypeStruct((width, width), f32),
        compiler_params=params(),
        name="place_local",
    )(*locals_)
    return (grad_spectral, grad_local)


def solution(mesh):
    return jax.shard_map(
        functools.partial(body, mesh.shape["dp"], mesh.shape["fsdp"]),
        mesh=mesh,
        in_specs=(
            P("dp", None, "fsdp", None, None, None),
            P("dp", None, "fsdp", None),
            P("dp", None),
            P(),
            P("fsdp", None, None, None),
            P(),
            P(),
        ),
        out_specs=(P("fsdp", None, None, None), P()),
        check_vma=False,
    )
```
